512 devices in a mesh: sec: 8 (over z_lo, core), ctx: 64 (over z_hi, x, y).
Axes of the slice: x: 4, y: 8, z: 8 (z_hi: 2, z_lo: 4; z = z_hi * 4 + z_lo), core: 2. Of those that a mesh axis runs over, the one named last changes fastest.
Arguments:
- offsets: int32 [64], replicated, may hold values from 0 to 112, as said below
- queries: bfloat16 [8, 1024, 2560], P('sec', 'ctx'), may hold values from -150 to 150
- output_grad: bfloat16 [8, 1024, 2560], P('sec', 'ctx'), may hold values from -6 to 6
- attention_out: bfloat16 [8, 1024, 2560], P('sec', 'ctx'), may hold values from -6 to 6
- cache_keys: bfloat16 [8192, 128], P('ctx'), may hold values from -7 to 7
- cache_values: bfloat16 [8192, 128], P('ctx'), may hold values from -6 to 6
- key_projection: bfloat16 [5120, 128], P('sec'), may hold values from -0.5 to 0.5
- value_projection: bfloat16 [5120, 128], P('sec'), may hold values from -0.5 to 0.5
- retention_query: bfloat16 [8192, 5120], P('ctx', 'sec'), may hold values from -0.046875 to 0.046875
- retention_key: bfloat16 [8192, 5120], P('ctx', 'sec'), may hold values from -0.046875 to 0.046875
- retention_value: bfloat16 [8192, 5120], P('ctx', 'sec'), may hold values from -6 to 6
- retention_decay: float32 [40, 8192], P('sec', 'ctx'), may hold values from -1 to 0, as said below
Outputs:
- cross_query_grad: bfloat16 [8, 1024, 2560], P('sec', 'ctx')
- cache_key_grad: bfloat16 [8192, 128], P('ctx')
- cache_value_grad: bfloat16 [8192, 128], P('ctx')
- retention_query_grad: float32 [8192, 5120], P('ctx', 'sec')
- retention_key_grad: float32 [8192, 5120], P('ctx', 'sec')
- retention_value_grad: float32 [8192, 5120], P('ctx', 'sec')
The draws below stay inside these ranges and needn't reach their ends.
Inputs may be any that keep to these rules, and one draw needn't show every extreme that they name: Query row r of context shard c stands at sequence position c * 128 + offsets[c] + r; some shard has offset 128 - 16 and some shard has offset 0. `retention_decay`: every entry is negative.
All inputs are finite; a program needn't handle non-finite values.
Results may differ from the reference program's by a relative error of at most 0.015.
Values may be sent and summed in bfloat16 or wider, within the bound.
No kernel may reach another device: no remote copies, remote signals or barrier semaphores. Data moves between devices by JAX's collectives and lax.ppermute only.
A program may use at most 128 MiB of HBM per device.

```python
import math
from functools import partial
import jax
import jax.numpy as jnp
from jax import lax

R = 128
QROWS = 16
QH = 20
HEAD = 128
HR = 40
LAYERS = 8
SEQUENCE_ROWS = 8192
NQ = 1024
QW = 2560
RW = 5120
N_CTX = 64


def key_base(key):
    return jax.random.truncated_normal(jax.random.fold_in(key, 101), -6.0, 6.0, (SEQUENCE_ROWS, HEAD), jnp.float32)


def draw_offsets(key, part):
    key = jax.random.fold_in(key, 3)
    first_key, second_key = jax.random.split(key)
    chosen = jax.random.randint(first_key, (N_CTX,), 0, R - QROWS + 1)
    shuffled = jax.random.permutation(second_key, N_CTX)
    location_list = jnp.arange(N_CTX)
    chosen = jnp.where(location_list == shuffled[0], R - QROWS, chosen)
    chosen = jnp.where(location_list == shuffled[1], 0, chosen)
    return chosen.astype(jnp.int32)


def draw_cache_keys(key, part):
    base_rows = key_base(key)
    return base_rows.astype(jnp.bfloat16)


def draw_queries(key, part):
    key = jax.random.fold_in(key, 7)
    normal_key = jax.random.fold_in(key, 0)
    drawn = jax.random.truncated_normal(normal_key, -6.0, 6.0, (LAYERS, NQ, QH, HEAD), jnp.float32)
    return drawn.reshape(LAYERS, NQ, QH * HEAD).astype(jnp.bfloat16)


def draw_retention_decay(key, part):
    key = jax.random.fold_in(key, 11)
    key_collection = jax.random.split(key, 7)
    slow_limit = 5
    gentle_heads = jax.random.randint(key_collection[0], (HR, 1), 0, 10) < slow_limit
    slow_rate = jax.random.uniform(key_collection[1], (HR, 1), jnp.float32, 0.1, 0.5) / SEQUENCE_ROWS
    fast_rate = jax.random.uniform(key_collection[2], (HR, 1), jnp.float32, 1.0 / 50.0, 1.0 / 30.0)
    decay_speed = jnp.where(gentle_heads, slow_rate, fast_rate)
    shard_multiplier = jnp.exp(jax.random.uniform(key_collection[3], (N_CTX, 1), jnp.float32, math.log(0.5), math.log(1.6)))
    shard_multiplier = jnp.broadcast_to(shard_multiplier, (N_CTX, R)).reshape(1, SEQUENCE_ROWS)
    token_multiplier = jax.random.uniform(key_collection[4], (HR, SEQUENCE_ROWS), jnp.float32, 0.5, 1.5)
    spike_locations = jax.random.randint(key_collection[5], (3,), 0, SEQUENCE_ROWS)
    spike_depth = jax.random.uniform(key_collection[6], (3,), jnp.float32, math.log(0.6), math.log(0.8))
    location_list = jnp.arange(SEQUENCE_ROWS, dtype=jnp.int32)
    spike_amount = jnp.sum(jnp.where(location_list[None, :] == spike_locations[:, None], spike_depth[:, None], 0.0), axis=0)
    return -decay_speed * shard_multiplier * token_multiplier + jnp.where(gentle_heads, spike_amount[None, :], 0.0)


def shard_levels(key, shape, pieces, low, high):
    def one(axis_at, shards_of):
        draws = jax.random.uniform(jax.random.fold_in(jax.random.fold_in(key, 6), axis_at), (shards_of,), jnp.float32, low / len(pieces), high / len(pieces))
        return jnp.repeat(jnp.exp(draws), shape[axis_at] // shards_of).reshape((-1,) + (1,) * (len(shape) - axis_at - 1))

    gain = one(*pieces[0])
    for cut in pieces[1:]:
        gain = gain * one(*cut)
    return gain


def normal_values(key, shape, spread, bound, cuts=(), kind=jnp.bfloat16):
    values = jax.random.normal(key, shape, jnp.float32) * spread
    if len(cuts) > 0:
        values = shard_levels(key, shape, cuts, -0.22, 0.18) * values
    return jnp.clip(values, min=-bound, max=bound).astype(kind)


def setup_inputs(seed: int = 0) -> dict:
    keys = jax.random.split(jax.random.key(seed), 13)
    offsets = draw_offsets(jax.random.fold_in(keys[12], 71), 0)
    queries = draw_queries(jax.random.fold_in(keys[12], 71), 0)
    output_grad = normal_values(keys[2], (LAYERS, NQ, QW), 1.0, 6.0, ((0, 8), (1, 64)))
    attention_out = normal_values(keys[3], (LAYERS, NQ, QW), 1.0, 6.0, ((0, 8), (1, 64)))
    cache_keys = draw_cache_keys(jax.random.fold_in(keys[12], 71), 0)
    cache_values = normal_values(keys[5], (SEQUENCE_ROWS, HEAD), 1.0, 6.0, ((0, 64),))
    key_projection = normal_values(keys[6], (RW, HEAD), HEAD ** -0.5, 0.5, ((0, 8),))
    value_projection = normal_values(keys[7], (RW, HEAD), HEAD ** -0.5, 0.5, ((0, 8),))
    retention_query = normal_values(keys[8], (SEQUENCE_ROWS, RW), (HEAD * R) ** -0.5, 0.046875, ((0, 64), (1, 8)))
    retention_key = normal_values(keys[9], (SEQUENCE_ROWS, RW), (HEAD * R) ** -0.5, 0.046875, ((0, 64), (1, 8)))
    retention_value = normal_values(keys[10], (SEQUENCE_ROWS, RW), 1.0, 6.0, ((0, 64), (1, 8)))
    retention_decay = draw_retention_decay(jax.random.fold_in(keys[12], 71), 0)
    return {"offsets": offsets, "queries": queries, "output_grad": output_grad, "attention_out": attention_out, "cache_keys": cache_keys, "cache_values": cache_values, "key_projection": key_projection, "value_projection": value_projection, "retention_query": retention_query, "retention_key": retention_key, "retention_value": retention_value, "retention_decay": retention_decay}


HIGHEST_PRECISION = lax.Precision.HIGHEST

def query_positions(offsets):
    rows = jnp.arange(N_CTX * QROWS, dtype=jnp.int32)
    shards = rows // QROWS
    return (shards * R + offsets[shards] + rows % QROWS).astype(jnp.int32)

def cross_group(cache_keys, cache_values, running, group):
    key_sum, value_sum = running
    query_rows, grad_rows, output_rows, row_position = group
    query_flat = query_rows.reshape(QROWS * QH, HEAD)
    grad_flat = grad_rows.reshape(QROWS * QH, HEAD)
    output_flat = output_rows.reshape(QROWS * QH, HEAD)
    flat_position = jnp.repeat(row_position, QH)
    factor = 1.0 / math.sqrt(HEAD)
    scores = jnp.dot(query_flat, cache_keys.T, preferred_element_type=jnp.float32) * factor
    visible = jnp.arange(SEQUENCE_ROWS, dtype=jnp.int32)[None, :] <= flat_position[:, None]
    row_max = lax.optimization_barrier(jnp.max(jnp.where(visible, scores, -jnp.inf), axis=1, keepdims=True))
    row_sum = lax.optimization_barrier(jnp.sum(jnp.where(visible, jnp.exp(scores - row_max), 0.0), axis=1, keepdims=True))
    log_total = row_max + jnp.log(row_sum)
    soft_probs = jnp.where(visible, jnp.exp(scores - log_total), 0.0)
    row_delta = lax.optimization_barrier(jnp.sum(grad_flat.astype(jnp.float32) * output_flat.astype(jnp.float32), axis=1, keepdims=True))
    grad_probs = jnp.dot(grad_flat, cache_values.T, preferred_element_type=jnp.float32)
    grad_scores = (soft_probs * (grad_probs - row_delta)).astype(jnp.bfloat16)
    query_grad = (jnp.dot(grad_scores, cache_keys, preferred_element_type=jnp.float32) * factor).astype(jnp.bfloat16)
    key_sum = key_sum + jnp.dot(grad_scores.T, query_flat, preferred_element_type=jnp.float32)
    value_sum = value_sum + jnp.dot(soft_probs.astype(jnp.bfloat16).T, grad_flat, preferred_element_type=jnp.float32)
    return ((key_sum, value_sum), query_grad.reshape(QROWS, QH * HEAD))

def exact_einsum(form, left_side, right_side):
    return jnp.einsum(form, left_side.astype(jnp.float32), right_side.astype(jnp.float32), precision=HIGHEST_PRECISION)

def rounded(array):
    return lax.optimization_barrier(array.astype(jnp.bfloat16)).astype(jnp.float32)

def block_sums(block):
    query_block, key_block, value_block, grad_block, running_decay = block
    decay_to_end = jnp.exp(running_decay[:, -1:] - running_decay)
    decay_from_start = jnp.exp(running_decay)
    key_weighted = rounded(key_block.astype(jnp.float32) * decay_to_end.T[:, :, None])
    query_weighted = rounded(query_block.astype(jnp.float32) * decay_from_start.T[:, :, None])
    block_state = exact_einsum('thd,the->hde', key_weighted, value_block)
    block_grad = exact_einsum('thd,the->hde', query_weighted, grad_block)
    return (block_state, block_grad)

def block_grads(block):
    query_block, key_block, value_block, grad_block, running_decay, state_enter, grad_enter = block
    positions = jnp.arange(R, dtype=jnp.int32)
    causal = (positions[:, None] >= positions[None, :])[None]
    decay_gap = running_decay[:, :, None] - running_decay[:, None, :]
    decay_matrix = jnp.where(causal, jnp.exp(jnp.where(causal, decay_gap, 0.0)), 0.0)
    decay_back = jnp.transpose(decay_matrix, (0, 2, 1))
    decay_to_end = jnp.exp(running_decay[:, -1:] - running_decay).T[:, :, None]
    decay_from_start = jnp.exp(running_decay).T[:, :, None]
    state_rounded = rounded(state_enter)
    grad_rounded = rounded(grad_enter)
    weight_one = rounded(decay_matrix * exact_einsum('thd,uhd->htu', grad_block, value_block))
    query_result = exact_einsum('htu,uhd->thd', weight_one, key_block) + decay_from_start * exact_einsum('thd,hed->the', grad_block, state_rounded)
    weight_two = rounded(decay_back * exact_einsum('thd,shd->hts', value_block, grad_block))
    key_result = exact_einsum('hts,shd->thd', weight_two, query_block) + decay_to_end * exact_einsum('thd,hed->the', value_block, grad_rounded)
    weight_three = rounded(decay_back * exact_einsum('thd,shd->hts', key_block, query_block))
    value_result = exact_einsum('hts,shd->thd', weight_three, grad_block) + decay_to_end * exact_einsum('the,hed->thd', key_block, grad_rounded)
    return (query_result, key_result, value_result)

def retention_backward(retention_query, retention_key, retention_value, retention_grad, retention_decay):

    def to_blocks(array):
        return array.reshape(N_CTX, R, HR, HEAD)
    running_decay = jnp.cumsum(jnp.transpose(retention_decay.reshape(HR, N_CTX, R), (1, 0, 2)), axis=2)
    blocks = (to_blocks(retention_query), to_blocks(retention_key), to_blocks(retention_value), to_blocks(retention_grad), running_decay)
    block_state, block_grad = lax.map(block_sums, blocks)
    block_decay = jnp.exp(running_decay[:, :, -1])
    zero_state = jnp.zeros((HR, HEAD, HEAD), jnp.float32)

    def forward_step(state_acc, scan_item):
        decay_now, state_now = scan_item
        return (decay_now[:, None, None] * state_acc + state_now, state_acc)

    def backward_step(grad_acc, scan_item):
        decay_now, grad_now = scan_item
        return (decay_now[:, None, None] * grad_acc + grad_now, grad_acc)
    final_state, state_enter = lax.scan(forward_step, zero_state, (block_decay, block_state))
    final_grad, grad_enter = lax.scan(backward_step, zero_state, (block_decay, block_grad), reverse=True)
    query_result, key_result, value_result = lax.map(block_grads, blocks + (state_enter, grad_enter))
    return (query_result.reshape(SEQUENCE_ROWS, RW), key_result.reshape(SEQUENCE_ROWS, RW), value_result.reshape(SEQUENCE_ROWS, RW))

def reference(offsets, queries, output_grad, attention_out, cache_keys, cache_values, key_projection, value_projection, retention_query, retention_key, retention_value, retention_decay):
    positions = query_positions(offsets).reshape(N_CTX, QROWS)
    group_position = jnp.broadcast_to(positions[None], (LAYERS, N_CTX, QROWS)).reshape(LAYERS * N_CTX, QROWS)

    def group_shape(array):
        return array.reshape(LAYERS * N_CTX, QROWS, QH * HEAD)
    start_sums = (jnp.zeros((SEQUENCE_ROWS, HEAD), jnp.float32), jnp.zeros((SEQUENCE_ROWS, HEAD), jnp.float32))
    grouped = (group_shape(queries), group_shape(output_grad), group_shape(attention_out), group_position)
    (key_sum, value_sum), query_grad = lax.scan(partial(cross_group, cache_keys, cache_values), start_sums, grouped)
    factor = 1.0 / math.sqrt(HEAD)
    cache_key_grad = (key_sum * factor).astype(jnp.bfloat16)
    cache_value_grad = value_sum.astype(jnp.bfloat16)
    retention_out_grad = (jnp.dot(cache_key_grad, key_projection.T, preferred_element_type=jnp.float32) + jnp.dot(cache_value_grad, value_projection.T, preferred_element_type=jnp.float32)).astype(jnp.bfloat16)
    query_result, key_result, value_result = retention_backward(retention_query, retention_key, retention_value, retention_out_grad, retention_decay)
    return (query_grad.reshape(LAYERS, NQ, QH * HEAD), cache_key_grad, cache_value_grad, query_result, key_result, value_result)
```

```python
import functools
import math

import jax
import jax.numpy as jnp
from jax import lax
from jax.experimental import pallas as pl
from jax.experimental.pallas import tpu as pltpu
from jax.sharding import PartitionSpec as P

BF = jnp.bfloat16
F32 = jnp.float32
LOW = -1e30
LOG2E = math.log2(math.e)
CHIPS = 4
CORES = 2
WIRE = 24
SCOPED = 32 * 1024 * 1024


def dot_nt(a, b):
    return lax.dot_general(a, b, (((1,), (1,)), ((), ())), preferred_element_type=F32)


def dot_nn(a, b):
    return lax.dot_general(a, b, (((1,), (0,)), ((), ())), preferred_element_type=F32)


def dot_tn(a, b):
    return lax.dot_general(a, b, (((0,), (0,)), ((), ())), preferred_element_type=F32)


def call(kernel, outs, in_smem, ins, scratch=(), flops=0):
    vmem = pl.BlockSpec(memory_space=pltpu.VMEM)
    smem = pl.BlockSpec(memory_space=pltpu.SMEM)
    return pl.pallas_call(
        kernel,
        out_shape=outs,
        in_specs=[smem] * len(in_smem) + [vmem] * len(ins),
        out_specs=jax.tree.map(lambda _: vmem, outs),
        scratch_shapes=list(scratch),
        compiler_params=pltpu.CompilerParams(vmem_limit_bytes=SCOPED),
        cost_estimate=pl.CostEstimate(flops=flops, bytes_accessed=4 << 20, transcendentals=0),
    )(*in_smem, *ins)


def key_positions(place, chunk, blocks, rows, width, block_rows):
    at = lax.broadcasted_iota(jnp.int32, (blocks * rows, width), 0)
    return (chunk * blocks + at // rows) * block_rows + place * rows + at % rows


def stats_kernel(blocks, block_rows, factor, where_ref, q_ref, kv_ref, pos_ref, lse_ref):
    shard, chip, place = where_ref[0], where_ref[1], where_ref[2]
    rows = kv_ref.shape[1] // 2
    width = q_ref.shape[1]
    full = shard // blocks
    pos = pos_ref[...]
    scale = factor * LOG2E
    for k in range(CHIPS):
        q = q_ref[k]

        def chunk(j, carry, masked=False):
            top, total = carry
            keys = kv_ref[pl.ds(j * blocks, blocks), 0:rows, :].reshape(blocks * rows, -1)
            s = dot_nt(keys, q)
            if masked:
                seen = key_positions(place, j, blocks, rows, width, block_rows) <= pos
                s = jnp.where(seen, s, LOW)
            new = jnp.maximum(top, jnp.max(s, axis=0, keepdims=True))
            p = jnp.exp2((s - new) * scale)
            if masked:
                p = jnp.where(seen, p, 0.0)
            total = total * jnp.exp2((top - new) * scale) + jnp.sum(p, axis=0, keepdims=True)
            return new, total

        start = (jnp.full((1, width), LOW, F32), jnp.zeros((1, width), F32))
        top, total = chunk(full, lax.fori_loop(0, full, chunk, start), masked=True)
        lse = jnp.where(total > 0.0, top * factor + jnp.log(total), LOW)
        lse_ref[lax.rem(chip + k, CHIPS)] = lse


def grads_kernel(
    blocks, block_rows, factor, where_ref, q_ref, g_ref, kv_ref, pos_ref, log_ref, delta_ref,
    dkv_ref, dq_ref, dk_total, dv_total,
):
    shard, chip, place = where_ref[0], where_ref[1], where_ref[2]
    rows = kv_ref.shape[1] // 2
    width = q_ref.shape[1]
    size = blocks * rows
    full = shard // blocks
    pos = pos_ref[...]
    scale = factor * LOG2E
    dk_total[...] = jnp.zeros_like(dk_total)
    dv_total[...] = jnp.zeros_like(dv_total)
    for k in range(CHIPS):
        layer = lax.rem(chip + k, CHIPS)
        q = q_ref[k]
        g = g_ref[k]
        log_total = log_ref[layer] * LOG2E
        delta = delta_ref[layer]

        def chunk(j, dq, masked=False):
            keys = kv_ref[pl.ds(j * blocks, blocks), 0:rows, :].reshape(size, -1)
            values = kv_ref[pl.ds(j * blocks, blocks), rows : 2 * rows, :].reshape(size, -1)
            p = jnp.exp2(dot_nt(keys, q) * scale - log_total)
            if masked:
                seen = key_positions(place, j, blocks, rows, width, block_rows) <= pos
                p = jnp.where(seen, p, 0.0)
            ds = (p * (dot_nt(values, g) - delta)).astype(BF)
            at = pl.ds(pl.multiple_of(j * size, size), size)
            dk_total[at, :] += dot_nn(ds, q)
            dv_total[at, :] += dot_nn(p.astype(BF), g)
            return dq + dot_tn(keys, ds)

        dq = lax.fori_loop(0, full, chunk, jnp.zeros((keys_width(kv_ref), width), F32))
        dq_ref[layer] = chunk(full, dq, masked=True).T
    for j in range(kv_ref.shape[0] // blocks):
        at = slice(j * size, (j + 1) * size)
        to = slice(j * blocks, (j + 1) * blocks)
        dkv_ref[to, 0:rows, :] = dk_total[at, :].astype(BF).reshape(blocks, rows, -1)
        dkv_ref[to, rows : 2 * rows, :] = dv_total[at, :].astype(BF).reshape(blocks, rows, -1)


def keys_width(ref):
    return ref.shape[-1]


def states_kernel(
    heads, ck_ref, cv_ref, kp_ref, vp_ref, rq_ref, rk_ref, rv_ref, from_ref, to_ref, extra_ref,
    gr_ref, send_ref, wire,
):
    half = send_ref.shape[0]
    wire[:, 4 * heads :, :] = jnp.broadcast_to(
        extra_ref[...][None], (half,) + extra_ref.shape
    )
    for i in range(heads):
        at = slice(i * 128, (i + 1) * 128)
        gr = (dot_nt(ck_ref[...], kp_ref[at, :]) + dot_nt(cv_ref[...], vp_ref[at, :])).astype(BF)
        gr_ref[:, at] = gr
        query_w = (rq_ref[:, at].astype(F32) * from_ref[:, i : i + 1]).astype(BF)
        key_w = (rk_ref[:, at].astype(F32) * to_ref[:, i : i + 1]).astype(BF)
        grad = dot_tn(query_w, gr)
        state = dot_tn(key_w, rv_ref[:, at])
        for k in range(2):
            wire[:, 2 * i + k, :] = grad[k * half : (k + 1) * half]
            wire[:, 2 * heads + 2 * i + k, :] = state[k * half : (k + 1) * half]
    send_ref[...] = wire[...].astype(BF)


def scan_kernel(heads, part_ref, decay_ref, out_ref, ahead, behind):
    count = part_ref.shape[0]
    zero = jnp.zeros(part_ref.shape[1:], F32)

    def step(b, carry):
        fore, back = carry
        ahead[b] = fore
        fore = decay_ref[b] * fore + part_ref[b].astype(F32)
        r = count - 1 - b
        behind[r] = back
        back = decay_ref[r] * back + part_ref[r].astype(F32)
        return fore, back

    lax.fori_loop(0, count, step, (zero, zero), unroll=4)
    row = lax.broadcasted_iota(jnp.int32, part_ref.shape, 1)
    out_ref[...] = jnp.where(row < 2 * heads, behind[...], ahead[...]).astype(BF)


def final_kernel(
    heads, rq_ref, rk_ref, rv_ref, gr_ref, cum_ref, cum_t_ref, from_ref, to_ref, wire_ref,
    q_ref, k_ref, v_ref, wire,
):
    wire[...] = wire_ref[...].astype(F32)

    def matrix(r):
        return jnp.concatenate([wire[:, r, :], wire[:, r + 1, :]], axis=0).astype(BF)

    size = rq_ref.shape[0]
    t = lax.broadcasted_iota(jnp.int32, (size, size), 0)
    u = lax.broadcasted_iota(jnp.int32, (size, size), 1)
    causal = t >= u
    for i in range(heads):
        at = slice(i * 128, (i + 1) * 128)
        qr, kr, vr, gr = rq_ref[:, at], rk_ref[:, at], rv_ref[:, at], gr_ref[:, at]
        grad_b, state_b = matrix(2 * i), matrix(2 * heads + 2 * i)
        gap = cum_t_ref[:, i : i + 1] - cum_ref[i : i + 1, :]
        decay = jnp.where(causal, jnp.exp(jnp.where(causal, gap, 0.0)), 0.0)
        from_start, to_end = from_ref[:, i : i + 1], to_ref[:, i : i + 1]
        one = (decay * dot_nt(gr, vr)).astype(BF)
        three = (decay * dot_nt(qr, kr)).astype(BF)
        q_ref[:, at] = dot_nn(one, kr) + from_start * dot_nt(gr, state_b)
        k_ref[:, at] = dot_tn(one, qr) + to_end * dot_nt(vr, grad_b)
        v_ref[:, at] = dot_tn(three, gr) + to_end * dot_nn(kr, grad_b)


def body(
    offsets,
    queries,
    output_grad,
    attention_out,
    cache_keys,
    cache_values,
    key_projection,
    value_projection,
    retention_query,
    retention_key,
    retention_value,
    retention_decay,
):
    shards = lax.axis_size("ctx")
    shard = lax.axis_index("ctx")
    secs = lax.axis_size("sec")
    place = lax.axis_index("sec")
    chip, core = place // CORES, lax.rem(place, CORES)
    block_rows, head = cache_keys.shape
    layers, query_rows, query_width = queries.shape
    heads = query_width // head
    flat = layers * query_rows * heads
    rows = block_rows // secs
    factor = 1.0 / math.sqrt(head)
    blocks = math.gcd(shards, 16)
    chips = secs // CORES

    q_own = queries.reshape(flat, head)
    g_own = output_grad.reshape(flat, head)
    own = jnp.concatenate([q_own, g_own], axis=0)
    parts = [own] + [
        lax.ppermute(own, "sec", [(i, (i - CORES * k) % secs) for i in range(secs)])
        for k in range(1, chips)
    ]
    kv_own = jnp.concatenate(
        [lax.dynamic_slice_in_dim(a, place * rows, rows, 0) for a in (cache_keys, cache_values)]
    )
    kv = lax.all_to_all(
        jnp.broadcast_to(kv_own[None], (shards,) + kv_own.shape), "ctx", 0, 0, tiled=True
    )
    mine = jnp.stack(parts)
    other = lax.ppermute(mine, "sec", [(i, i ^ 1) for i in range(secs)])
    first = jnp.where(core == 0, mine, other)
    second = jnp.where(core == 0, other, mine)
    q_all = jnp.concatenate([first[:, :flat], second[:, :flat]], axis=1)
    g_all = jnp.concatenate([first[:, flat:], second[:, flat:]], axis=1)

    own_offset = jnp.sum(
        jnp.where(jnp.arange(shards, dtype=jnp.int32) == shard, offsets, 0)
    )
    row_of = (jnp.arange(CORES * flat, dtype=jnp.int32) % (query_rows * heads)) // heads
    pos = (shard * block_rows + own_offset + row_of)[None]
    where = jnp.stack([shard, chip, place]).astype(jnp.int32)
    delta = jnp.sum(
        g_own.astype(F32) * attention_out.reshape(flat, head).astype(F32), axis=1
    )

    lse = call(
        functools.partial(stats_kernel, blocks, block_rows, factor),
        jax.ShapeDtypeStruct((chips, 1, CORES * flat), F32),
        (where,),
        (q_all, kv, pos),
        flops=1 << 30,
    )
    both = jnp.concatenate([lse.reshape(-1), delta])
    lines = -(-both.shape[0] // 1024) * 8
    both = jnp.pad(both, (0, lines * 128 - both.shape[0])).reshape(lines, 128)
    both = lax.all_to_all(
        jnp.broadcast_to(both[None], (secs,) + both.shape), "sec", 0, 0, tiled=True
    ).reshape(secs, -1)
    logs = both[:, : secs * flat]
    top = jnp.max(logs, axis=0)
    log_total = top + jnp.log(jnp.sum(jnp.exp(logs - top), axis=0))
    log_total = log_total.reshape(chips, 1, CORES * flat)
    deltas = both[:, secs * flat : (secs + 1) * flat].reshape(chips, 1, CORES * flat)

    dkv, dq = call(
        functools.partial(grads_kernel, blocks, block_rows, factor),
        (
            jax.ShapeDtypeStruct(kv.shape, BF),
            jax.ShapeDtypeStruct((chips, CORES * flat, head), F32),
        ),
        (where,),
        (q_all, g_all, kv, pos, log_total, deltas),
        scratch=[pltpu.VMEM((shards * rows, head), F32)] * 2,
        flops=4 << 30,
    )
    dq = lax.psum_scatter(
        dq.reshape(secs * flat, head), "sec", scatter_dimension=0, tiled=True
    )
    cross_query_grad = (dq * factor).astype(BF).reshape(layers, query_rows, query_width)

    terms = lax.all_to_all(dkv, "ctx", 0, 0, tiled=True)
    total = jnp.sum(terms.astype(F32), axis=0)
    scale = jnp.where(jnp.arange(2 * rows) < rows, factor, 1.0)[:, None]
    total = (total * scale).astype(BF)
    whole = lax.all_to_all(
        jnp.broadcast_to(total[None], (secs,) + total.shape), "sec", 0, 0, tiled=True
    )
    cache_key_grad = whole[:, :rows].reshape(block_rows, head)
    cache_value_grad = whole[:, rows:].reshape(block_rows, head)

    local = retention_decay.shape[0]
    cum = jnp.cumsum(retention_decay, axis=1)
    cum_t = cum.T
    last = cum[:, -1]
    from_start = jnp.exp(cum_t)
    to_end = jnp.exp(last[None] - cum_t)
    high = last.astype(BF)
    rest = last - high.astype(F32)
    middle = rest.astype(BF)
    low = (rest - middle.astype(F32)).astype(BF)
    extra = jnp.concatenate([high, middle, low]).astype(F32)
    extra = jnp.pad(
        extra[None], ((0, WIRE - 4 * local - 1), (0, head - extra.shape[0]))
    )
    out_grad, send = call(
        functools.partial(states_kernel, local),
        (
            jax.ShapeDtypeStruct(retention_query.shape, BF),
            jax.ShapeDtypeStruct((shards, WIRE, head), BF),
        ),
        (),
        (
            cache_key_grad, cache_value_grad, key_projection, value_projection,
            retention_query, retention_key, retention_value, from_start, to_end, extra,
        ),
        scratch=[pltpu.VMEM((shards, WIRE, head), F32)],
        flops=1 << 27,
    )
    part = lax.all_to_all(send, "ctx", 0, 0, tiled=True)
    lasts = part[:, 4 * local, : 3 * local].astype(F32).reshape(shards, 3, local)
    decays = jnp.exp(lasts[:, 0] + lasts[:, 1] + lasts[:, 2])
    decays = jnp.concatenate([decays, decays], axis=1)
    decays = jnp.broadcast_to(decays[:, :, None], (shards, 2 * local, 2))
    decays = decays.reshape(shards, 4 * local, 1)
    decays = jnp.pad(decays, ((0, 0), (0, WIRE - 4 * local), (0, 0)))
    decays = jnp.broadcast_to(decays, (shards, WIRE, head))
    enter = call(
        functools.partial(scan_kernel, local),
        jax.ShapeDtypeStruct(part.shape, BF),
        (),
        (part, decays),
        scratch=[pltpu.VMEM(part.shape, F32)] * 2,
    )
    enter = lax.all_to_all(enter, "ctx", 0, 0, tiled=True)
    grads = call(
        functools.partial(final_kernel, local),
        (jax.ShapeDtypeStruct(retention_query.shape, F32),) * 3,
        (),
        (
            retention_query, retention_key, retention_value, out_grad, cum, cum_t,
            from_start, to_end, enter,
        ),
        scratch=[pltpu.VMEM(enter.shape, F32)],
        flops=1 << 28,
    )
    return (cross_query_grad, cache_key_grad, cache_value_grad) + tuple(grads)


def solution(mesh):
    in_specs = (
        P(),
        P("sec", "ctx", None),
        P("sec", "ctx", None),
        P("sec", "ctx", None),
        P("ctx", None),
        P("ctx", None),
        P("sec", None),
        P("sec", None),
        P("ctx", "sec"),
        P("ctx", "sec"),
        P("ctx", "sec"),
        P("sec", "ctx"),
    )
    out_specs = (
        P("sec", "ctx", None),
        P("ctx", None),
        P("ctx", None),
        P("ctx", "sec"),
        P("ctx", "sec"),
        P("ctx", "sec"),
    )
    return jax.shard_map(body, mesh=mesh, in_specs=in_specs, out_specs=out_specs, check_vma=False)
```

```python
import functools
import math

import jax
import jax.numpy as jnp
from jax import lax
from jax.experimental import pallas as pl
from jax.experimental.pallas import tpu as pltpu
from jax.sharding import Mesh
from jax.sharding import PartitionSpec as P

BF = jnp.bfloat16
F32 = jnp.float32
LOW = -1e30
LOG2E = math.log2(math.e)
CHIPS, CORES = 4, 2
HALVES, PLANE = 2, 32
PLANE_AXES = ("x", "y")
SLICE = 4
WIRE = 48
SCOPED = 32 * 1024 * 1024


def dot_nt(a, b):
    return lax.dot_general(a, b, (((1,), (1,)), ((), ())), preferred_element_type=F32)


def dot_nn(a, b):
    return lax.dot_general(a, b, (((1,), (0,)), ((), ())), preferred_element_type=F32)


def dot_tn(a, b):
    return lax.dot_general(a, b, (((0,), (0,)), ((), ())), preferred_element_type=F32)


def call(kernel, outs, in_smem, ins, scratch=(), flops=0):
    vmem = pl.BlockSpec(memory_space=pltpu.VMEM)
    smem = pl.BlockSpec(memory_space=pltpu.SMEM)
    return pl.pallas_call(
        kernel,
        out_shape=outs,
        in_specs=[smem] * len(in_smem) + [vmem] * len(ins),
        out_specs=jax.tree.map(lambda _: vmem, outs),
        scratch_shapes=list(scratch),
        compiler_params=pltpu.CompilerParams(vmem_limit_bytes=SCOPED),
        cost_estimate=pl.CostEstimate(flops=flops, bytes_accessed=1 << 20, transcendentals=0),
    )(*in_smem, *ins)


def shape(dims, dtype):
    return jax.ShapeDtypeStruct(dims, dtype)


def pinned_exchange(array, axes, later):
    array, later = lax.optimization_barrier((array, later))
    array = lax.all_to_all(array, axes, 0, 0, tiled=True)
    return lax.optimization_barrier((array, later))


def pack_kernel(heads, q_ref, g_ref, out_ref):
    rows = q_ref.shape[1]
    for h in range(heads):
        at = slice(h * 128, (h + 1) * 128)
        out_ref[h * rows : (h + 1) * rows, :] = q_ref[0, :, at]
        out_ref[(heads + h) * rows : (heads + h + 1) * rows, :] = g_ref[0, :, at]


def delta_kernel(heads, where_ref, g_ref, o_ref, out_ref, product):
    rows = g_ref.shape[1]
    base = where_ref[3] * (heads * rows)
    product[...] = jnp.zeros_like(product)
    for h in range(heads):
        at = slice(h * 128, (h + 1) * 128)
        to = pl.ds(pl.multiple_of(base + h * rows, rows), rows)
        product[to, :] = g_ref[0, :, at].astype(F32) * o_ref[0, :, at].astype(F32)
    sums = jnp.sum(product[...].T, axis=0, keepdims=True)
    out_ref[...] = jnp.zeros_like(out_ref)
    for n in range(sums.shape[1] // 128):
        out_ref[n : n + 1, :] = sums[:, n * 128 : (n + 1) * 128]


def key_positions(place, chunk, blocks, rows, block_rows):
    at = lax.broadcasted_iota(jnp.int32, (blocks * rows, 1), 0)
    return (chunk * blocks + at // rows) * block_rows + place * rows + at % rows


def cache_slice(kv_ref, chunk, blocks, rows, values):
    per = kv_ref.shape[0] // blocks
    line = pl.multiple_of((chunk // per) * (2 * rows) + values * rows, rows)
    at = pl.ds(lax.rem(chunk, per) * blocks, blocks)
    return kv_ref[at, pl.ds(line, rows), :].reshape(blocks * rows, -1)


def stats_kernel(blocks, rows, block_rows, factor, where_ref, q_ref, kv_ref, pos_ref, delta_ref, out_ref):
    shard, chip, place = where_ref[0], where_ref[1], where_ref[2]
    width = q_ref.shape[1]
    lines = width // 128
    full = shard // blocks
    pos = pos_ref[...]
    scale = factor * LOG2E
    out_ref[:, CHIPS * lines :, :] = jnp.broadcast_to(
        delta_ref[0 : out_ref.shape[1] - CHIPS * lines, :][None],
        (out_ref.shape[0], out_ref.shape[1] - CHIPS * lines, 128),
    )
    for k in range(CHIPS):
        q = q_ref[k]

        def chunk(j, carry, masked=False):
            top, total = carry
            s = dot_nt(cache_slice(kv_ref, j, blocks, rows, 0), q)
            if masked:
                seen = key_positions(place, j, blocks, rows, block_rows) <= pos
                s = jnp.where(seen, s, LOW)
            new = jnp.maximum(top, jnp.max(s, axis=0, keepdims=True))
            p = jnp.exp2((s - new) * scale)
            if masked:
                p = jnp.where(seen, p, 0.0)
            total = total * jnp.exp2((top - new) * scale) + jnp.sum(p, axis=0, keepdims=True)
            return new, total

        start = (jnp.full((1, width), LOW, F32), jnp.zeros((1, width), F32))
        top, total = chunk(full, lax.fori_loop(0, full, chunk, start), masked=True)
        lse = jnp.where(total > 0.0, top * factor + jnp.log(total), LOW)
        line = lax.rem(chip + k, CHIPS) * lines
        for n in range(lines):
            out_ref[:, pl.ds(line + n, 1), :] = jnp.broadcast_to(
                lse[:, n * 128 : (n + 1) * 128][None], (out_ref.shape[0], 1, 128)
            )


def grads_kernel(
    blocks, rows, block_rows, factor, where_ref, q_ref, g_ref, kv_ref, pos_ref, log_ref, delta_ref,
    dkv_ref, dq_ref, dk_total, dv_total,
):
    shard, chip, place = where_ref[0], where_ref[1], where_ref[2]
    width = q_ref.shape[1]
    size = blocks * rows
    full = shard // blocks
    pos = pos_ref[...]
    scale = factor * LOG2E
    dk_total[...] = jnp.zeros_like(dk_total)
    dv_total[...] = jnp.zeros_like(dv_total)
    for k in range(CHIPS):
        layer = lax.rem(chip + k, CHIPS)
        q = q_ref[k]
        g = g_ref[k]
        log_total = log_ref[layer] * LOG2E
        delta = delta_ref[layer]

        def chunk(j, dq, masked=False):
            keys = cache_slice(kv_ref, j, blocks, rows, 0)
            values = cache_slice(kv_ref, j, blocks, rows, 1)
            p = jnp.exp2(dot_nt(keys, q) * scale - log_total)
            if masked:
                seen = key_positions(place, j, blocks, rows, block_rows) <= pos
                p = jnp.where(seen, p, 0.0)
            ds = (p * (dot_nt(values, g) - delta)).astype(BF)
            at = pl.ds(pl.multiple_of(j * size, size), size)
            dk_total[at, :] += dot_nn(ds, q)
            dv_total[at, :] += dot_nn(p.astype(BF), g)
            return dq + dot_tn(keys, ds)

        dq = lax.fori_loop(0, full, chunk, jnp.zeros((kv_ref.shape[-1], width), F32))
        dq = chunk(full, dq, masked=True).T
        half = width // CORES
        for n in range(CORES):
            dq_ref[n, layer] = dq[n * half : (n + 1) * half]
    per = dkv_ref.shape[0] // blocks
    for j in range(HALVES * per):
        at = slice(j * size, (j + 1) * size)
        to = slice((j % per) * blocks, (j % per + 1) * blocks)
        line = (j // per) * 2 * rows
        dkv_ref[to, line : line + rows, :] = dk_total[at, :].astype(BF).reshape(blocks, rows, -1)
        line += rows
        dkv_ref[to, line : line + rows, :] = dv_total[at, :].astype(BF).reshape(blocks, rows, -1)


def total_kernel(factor, terms_ref, out_ref):
    total = jnp.sum(terms_ref[...].astype(F32), axis=0)
    lines = out_ref.shape[1]
    row = lax.broadcasted_iota(jnp.int32, (lines, 1), 0)
    scale = jnp.where(row < lines // 2, factor, 1.0)
    count = out_ref.shape[0] // HALVES
    for n in range(HALVES):
        part = (total[n * lines : (n + 1) * lines] * scale).astype(BF)
        out_ref[n * count : (n + 1) * count] = jnp.broadcast_to(part[None], (count,) + part.shape)


def states_kernel(
    heads, whole_ref, kp_ref, vp_ref, rq_ref, rk_ref, rv_ref, from_ref, to_ref, extra_ref,
    ck_ref, cv_ref, gr_ref, send_ref, wire,
):
    count = whole_ref.shape[0] // HALVES
    rows = whole_ref.shape[1] // 2
    both = (whole_ref[0:count].astype(F32) + whole_ref[count:].astype(F32)).astype(BF)
    ck = both[:, 0:rows, :].reshape(count * rows, -1)
    cv = both[:, rows:, :].reshape(count * rows, -1)
    ck_ref[...] = ck
    cv_ref[...] = cv
    plane = send_ref.shape[0]
    used = 2 * SLICE * heads
    wire[:, used:, :] = jnp.broadcast_to(extra_ref[...][None], (plane,) + extra_ref.shape)
    for i in range(heads):
        at = slice(i * 128, (i + 1) * 128)
        gr = (dot_nt(ck, kp_ref[at, :]) + dot_nt(cv, vp_ref[at, :])).astype(BF)
        gr_ref[:, at] = gr
        query_w = (rq_ref[:, at].astype(F32) * from_ref[:, i : i + 1]).astype(BF)
        key_w = (rk_ref[:, at].astype(F32) * to_ref[:, i : i + 1]).astype(BF)
        grad = dot_tn(query_w, gr)
        state = dot_tn(key_w, rv_ref[:, at])
        for k in range(SLICE):
            part = slice(k * plane, (k + 1) * plane)
            wire[:, SLICE * i + k, :] = grad[part]
            wire[:, SLICE * (heads + i) + k, :] = state[part]
    send_ref[...] = wire[...].astype(BF)


def totals_kernel(heads, part_ref, decay_ref, out_ref):
    count = part_ref.shape[0]
    zero = jnp.zeros(part_ref.shape[1:], F32)

    def step(b, carry):
        fore, back = carry
        fore = decay_ref[b] * fore + part_ref[b].astype(F32)
        r = count - 1 - b
        back = decay_ref[r] * back + part_ref[r].astype(F32)
        return fore, back

    fore, back = lax.fori_loop(0, count, step, (zero, zero), unroll=4)
    row = lax.broadcasted_iota(jnp.int32, zero.shape, 0)
    out_ref[...] = jnp.where(row < SLICE * heads, back, fore)


def scan_kernel(heads, where_ref, part_ref, decay_ref, other_ref, out_ref, ahead, behind):
    count = part_ref.shape[0]
    upper = where_ref[0] >= count
    other = other_ref[...]
    zero = jnp.zeros_like(other)

    def step(b, carry):
        fore, back = carry
        ahead[b] = fore
        fore = decay_ref[b] * fore + part_ref[b].astype(F32)
        r = count - 1 - b
        behind[r] = back
        back = decay_ref[r] * back + part_ref[r].astype(F32)
        return fore, back

    start = (jnp.where(upper, other, zero), jnp.where(upper, zero, other))
    lax.fori_loop(0, count, step, start, unroll=4)
    row = lax.broadcasted_iota(jnp.int32, part_ref.shape, 1)
    out_ref[...] = jnp.where(row < SLICE * heads, behind[...], ahead[...]).astype(BF)


def final_kernel(
    heads, rq_ref, rk_ref, rv_ref, gr_ref, cum_ref, cum_t_ref, from_ref, to_ref, wire_ref,
    q_ref, k_ref, v_ref, wire,
):
    wire[...] = wire_ref[...].astype(F32)

    def matrix(r):
        return jnp.concatenate([wire[:, r + k, :] for k in range(SLICE)], axis=0).astype(BF)

    size = rq_ref.shape[0]
    t = lax.broadcasted_iota(jnp.int32, (size, size), 0)
    u = lax.broadcasted_iota(jnp.int32, (size, size), 1)
    causal = t >= u
    for i in range(heads):
        at = slice(i * 128, (i + 1) * 128)
        qr, kr, vr, gr = rq_ref[:, at], rk_ref[:, at], rv_ref[:, at], gr_ref[:, at]
        grad_b, state_b = matrix(SLICE * i), matrix(SLICE * (heads + i))
        gap = cum_t_ref[:, i : i + 1] - cum_ref[i : i + 1, :]
        decay = jnp.where(causal, jnp.exp(jnp.where(causal, gap, 0.0)), 0.0)
        from_start, to_end = from_ref[:, i : i + 1], to_ref[:, i : i + 1]
        one = (decay * dot_nt(gr, vr)).astype(BF)
        three = (decay * dot_nt(qr, kr)).astype(BF)
        q_ref[:, at] = dot_nn(one, kr) + from_start * dot_nt(gr, state_b)
        k_ref[:, at] = dot_tn(one, qr) + to_end * dot_nt(vr, grad_b)
        v_ref[:, at] = dot_tn(three, gr) + to_end * dot_nn(kr, grad_b)


def query_grad_kernel(heads, factor, own_ref, a_ref, b_ref, c_ref, out_ref):
    rows = out_ref.shape[1]
    total = own_ref[...] + a_ref[...].astype(F32) + b_ref[...].astype(F32) + c_ref[...].astype(F32)
    total = (total * factor).astype(BF)
    for h in range(heads):
        out_ref[0, :, h * 128 : (h + 1) * 128] = total[h * rows : (h + 1) * rows]


def body(
    offsets,
    queries,
    output_grad,
    attention_out,
    cache_keys,
    cache_values,
    key_projection,
    value_projection,
    retention_query,
    retention_key,
    retention_value,
    retention_decay,
):
    core, chip = lax.axis_index("core"), lax.axis_index("zl")
    place = chip * CORES + core
    secs = CHIPS * CORES
    half = lax.axis_index("zh")
    shard = half * PLANE + lax.axis_index(PLANE_AXES)
    shards = HALVES * PLANE
    block_rows, head = cache_keys.shape
    _, query_rows, query_width = queries.shape
    heads = query_width // head
    flat = query_rows * heads
    width = CORES * flat
    rows = block_rows // secs
    factor = 1.0 / math.sqrt(head)
    blocks = 16
    where = jnp.stack([shard, chip, place, core]).astype(jnp.int32)

    kv_own = jnp.concatenate(
        [lax.dynamic_slice_in_dim(a, place * rows, rows, 0) for a in (cache_keys, cache_values)]
    )
    kv_own, queries, output_grad = lax.optimization_barrier((kv_own, queries, output_grad))
    kv_other = lax.ppermute(kv_own, "zh", [(0, 1), (1, 0)])
    own = call(
        functools.partial(pack_kernel, heads),
        shape((2 * flat, head), BF), (), (queries, output_grad),
    )
    parts = [own] + [
        lax.ppermute(own, "zl", [(i, (i - k) % CHIPS) for i in range(CHIPS)])
        for k in range(1, CHIPS)
    ]
    delta = call(
        functools.partial(delta_kernel, heads),
        shape((12, head), F32), (where,), (output_grad, attention_out),
        scratch=[pltpu.VMEM((width, head), F32)],
    )
    own_offset = jnp.sum(
        jnp.where(jnp.arange(shards, dtype=jnp.int32) == shard, offsets, 0)
    )
    row_of = jnp.arange(width, dtype=jnp.int32) % query_rows
    pos = (shard * block_rows + own_offset + row_of)[None]

    local = retention_decay.shape[0]
    cum = jnp.cumsum(retention_decay, axis=1)
    cum_t = cum.T
    last = cum[:, -1]
    from_start = jnp.exp(cum_t)
    to_end = jnp.exp(last[None] - cum_t)
    high = last.astype(BF)
    rest = last - high.astype(F32)
    middle = rest.astype(BF)
    low = (rest - middle.astype(F32)).astype(BF)
    extra = jnp.concatenate([high, middle, low]).astype(F32)
    used = 2 * SLICE * local
    extra = jnp.pad(extra[None], ((0, WIRE - used - 1), (0, head - extra.shape[0])))

    early = (where, pos, delta, cum, cum_t, from_start, to_end, extra)
    kv = jnp.where(
        half == 0,
        jnp.concatenate([kv_own, kv_other]),
        jnp.concatenate([kv_other, kv_own]),
    )
    kv = jnp.broadcast_to(kv[None], (PLANE,) + kv.shape)
    kv, early = pinned_exchange(kv, PLANE_AXES, early)
    where, pos, delta, cum, cum_t, from_start, to_end, extra = early

    kv, *parts = lax.optimization_barrier((kv, *parts))
    mine = jnp.stack(parts)
    other = lax.ppermute(mine, "core", [(0, 1), (1, 0)])
    first = jnp.where(core == 0, mine, other)
    second = jnp.where(core == 0, other, mine)
    q_all = jnp.concatenate([first[:, :flat], second[:, :flat]], axis=1)
    g_all = jnp.concatenate([first[:, flat:], second[:, flat:]], axis=1)

    sizes = (blocks, rows, block_rows, factor)
    both = call(
        functools.partial(stats_kernel, *sizes),
        shape((secs, 32, head), F32), (where,), (q_all, kv, pos, delta),
        flops=1 << 30,
    )
    both, (q_all, g_all, kv) = pinned_exchange(both, ("zl", "core"), (q_all, g_all, kv))
    lines = width // 128
    logs = both[:, : CHIPS * lines]
    top = jnp.max(logs, axis=0)
    log_total = top + jnp.log(jnp.sum(jnp.exp(logs - top), axis=0))
    log_total = log_total.reshape(CHIPS, 1, width)
    deltas = both[:, CHIPS * lines : (CHIPS + 1) * lines]
    deltas = (deltas[0::CORES] + deltas[1::CORES]).reshape(CHIPS, 1, width)

    dkv, dq = call(
        functools.partial(grads_kernel, *sizes),
        (shape(kv.shape, BF), shape((CORES, CHIPS, flat, head), F32)),
        (where,),
        (q_all, g_all, kv, pos, log_total, deltas),
        scratch=[pltpu.VMEM((shards * rows, head), F32)] * 2,
        flops=4 << 30,
    )
    dq_other = lax.ppermute(
        lax.dynamic_index_in_dim(dq, 1 - core, 0, False), "core", [(0, 1), (1, 0)]
    )
    dq_own = lax.dynamic_index_in_dim(dq, core, 0, False)
    terms, dq_own = pinned_exchange(dkv, PLANE_AXES, dq_own)
    total = call(
        functools.partial(total_kernel, factor),
        shape((HALVES * secs, 2 * rows, head), BF), (), (terms,),
    )
    whole, (dq_own, dq_other) = pinned_exchange(total, ("zh", "zl", "core"), (dq_own, dq_other))

    cache_key_grad, cache_value_grad, out_grad, send = call(
        functools.partial(states_kernel, local),
        (
            shape((block_rows, head), BF), shape((block_rows, head), BF),
            shape(retention_query.shape, BF), shape((PLANE, WIRE, head), BF),
        ),
        (),
        (
            whole, key_projection, value_projection,
            retention_query, retention_key, retention_value, from_start, to_end, extra,
        ),
        scratch=[pltpu.VMEM((PLANE, WIRE, head), F32)],
        flops=1 << 27,
    )
    part, (dq_own, dq_other) = pinned_exchange(send, PLANE_AXES, (dq_own, dq_other))
    lasts = part[:, used, : 3 * local].astype(F32).reshape(PLANE, 3, local)
    decays = jnp.exp(lasts[:, 0] + lasts[:, 1] + lasts[:, 2])
    decays = jnp.concatenate([decays, decays], axis=1)
    decays = jnp.broadcast_to(decays[:, :, None], (PLANE, 2 * local, SLICE))
    decays = decays.reshape(PLANE, used, 1)
    decays = jnp.pad(decays, ((0, 0), (0, WIRE - used), (0, 0)))
    decays = jnp.broadcast_to(decays, (PLANE, WIRE, head))
    totals = call(
        functools.partial(totals_kernel, local),
        shape((WIRE, head), F32), (), (part, decays),
    )
    dq_sum = dq_own + dq_other
    totals, dq_sum = lax.optimization_barrier((totals, dq_sum))
    totals = lax.ppermute(totals, "zh", [(0, 1), (1, 0)])
    pieces = [
        lax.ppermute(
            lax.dynamic_index_in_dim(dq_sum, lax.rem(chip + k, CHIPS), 0, False).astype(BF),
            "zl", [(i, (i + k) % CHIPS) for i in range(CHIPS)],
        )
        for k in range(1, CHIPS)
    ]
    dq_mine = lax.dynamic_index_in_dim(dq_sum, chip, 0, False)
    enter = call(
        functools.partial(scan_kernel, local),
        shape(part.shape, BF), (where,), (part, decays, totals),
        scratch=[pltpu.VMEM(part.shape, F32)] * 2,
    )
    enter, (dq_mine, pieces, out_grad) = pinned_exchange(
        enter, PLANE_AXES, (dq_mine, pieces, out_grad)
    )
    cross_query_grad = call(
        functools.partial(query_grad_kernel, heads, factor),
        shape(queries.shape, BF), (), (dq_mine, *pieces),
    )
    grads = call(
        functools.partial(final_kernel, local),
        (shape(retention_query.shape, F32),) * 3,
        (),
        (
            retention_query, retention_key, retention_value, out_grad, cum, cum_t,
            from_start, to_end, enter,
        ),
        scratch=[pltpu.VMEM(enter.shape, F32)],
        flops=1 << 28,
    )
    return (cross_query_grad, cache_key_grad, cache_value_grad) + tuple(grads)


def solution(mesh):
    sec, ctx = ("zl", "core"), ("zh", "x", "y")
    split = Mesh(mesh.devices.reshape(CHIPS, CORES, HALVES, 4, 8), sec + ctx)
    in_specs = (
        P(),
        P(sec, ctx, None),
        P(sec, ctx, None),
        P(sec, ctx, None),
        P(ctx, None),
        P(ctx, None),
        P(sec, None),
        P(sec, None),
        P(ctx, sec),
        P(ctx, sec),
        P(ctx, sec),
        P(sec, ctx),
    )
    out_specs = (
        P(sec, ctx, None),
        P(ctx, None),
        P(ctx, None),
        P(ctx, sec),
        P(ctx, sec),
        P(ctx, sec),
    )
    return jax.shard_map(body, mesh=split, in_specs=in_specs, out_specs=out_specs, check_vma=False)
```

```python
import functools
import math

import jax
import jax.numpy as jnp
from jax import lax
from jax.experimental import pallas as pl
from jax.experimental.pallas import tpu as pltpu
from jax.sharding import Mesh
from jax.sharding import PartitionSpec as P

BF = jnp.bfloat16
F32 = jnp.float32
LOW = -1e30
LOG2E = math.log2(math.e)
CHIPS, CORES = 4, 2
HALVES, PLANE = 2, 32
PLANE_AXES = ("x", "y")
SLICE = 4
WIRE = 48
SCOPED = 32 * 1024 * 1024


def dot_nt(a, b):
    return lax.dot_general(a, b, (((1,), (1,)), ((), ())), preferred_element_type=F32)


def dot_nn(a, b):
    return lax.dot_general(a, b, (((1,), (0,)), ((), ())), preferred_element_type=F32)


def dot_tn(a, b):
    return lax.dot_general(a, b, (((0,), (0,)), ((), ())), preferred_element_type=F32)


def call(kernel, outs, in_smem, ins, scratch=(), flops=0):
    vmem = pl.BlockSpec(memory_space=pltpu.VMEM)
    smem = pl.BlockSpec(memory_space=pltpu.SMEM)
    return pl.pallas_call(
        kernel,
        out_shape=outs,
        in_specs=[smem] * len(in_smem) + [vmem] * len(ins),
        out_specs=jax.tree.map(lambda _: vmem, outs),
        scratch_shapes=list(scratch),
        compiler_params=pltpu.CompilerParams(vmem_limit_bytes=SCOPED),
        cost_estimate=pl.CostEstimate(flops=flops, bytes_accessed=1 << 20, transcendentals=0),
    )(*in_smem, *ins)


def shape(dims, dtype):
    return jax.ShapeDtypeStruct(dims, dtype)


def pinned_exchange(array, axes, later):
    array, later = lax.optimization_barrier((array, later))
    array = lax.all_to_all(array, axes, 0, 0, tiled=True)
    return lax.optimization_barrier((array, later))


def pack_kernel(heads, q_ref, g_ref, out_ref):
    rows = q_ref.shape[1]
    for h in range(heads):
        at = slice(h * 128, (h + 1) * 128)
        out_ref[h * rows : (h + 1) * rows, :] = q_ref[0, :, at]
        out_ref[(heads + h) * rows : (heads + h + 1) * rows, :] = g_ref[0, :, at]


def delta_kernel(heads, where_ref, g_ref, o_ref, out_ref, product):
    rows = g_ref.shape[1]
    base = lax.rem(where_ref[1], 2) * (heads * rows)
    product[...] = jnp.zeros_like(product)
    for h in range(heads):
        at = slice(h * 128, (h + 1) * 128)
        to = pl.ds(pl.multiple_of(base + h * rows, rows), rows)
        product[to, :] = g_ref[0, :, at].astype(F32) * o_ref[0, :, at].astype(F32)
    sums = jnp.sum(product[...].T, axis=0, keepdims=True)
    out_ref[...] = jnp.zeros_like(out_ref)
    for n in range(sums.shape[1] // 128):
        out_ref[n : n + 1, :] = sums[:, n * 128 : (n + 1) * 128]


def gather_kernel(where_ref, a_ref, b_ref, c_ref, d_ref, out_ref):
    flat = out_ref.shape[2]
    for k, ref in enumerate((a_ref, b_ref, c_ref, d_ref)):
        chip = lax.rem(where_ref[1] + k, CHIPS)
        out_ref[0, chip] = ref[0:flat]
        out_ref[1, chip] = ref[flat:]


def row_positions(where_ref, offset_ref, width, rows, block_rows):
    lane = lax.broadcasted_iota(jnp.int32, (1, width), 1)
    shard = where_ref[0]
    return lax.rem(lane, rows) + (shard * block_rows + offset_ref[shard])


def key_positions(place, chunk, blocks, rows, block_rows):
    at = lax.broadcasted_iota(jnp.int32, (blocks * rows, 1), 0)
    return (chunk * blocks + at // rows) * block_rows + place * rows + at % rows


def cache_slice(kv_ref, chunk, blocks, rows, values):
    per = kv_ref.shape[0] // blocks
    line = pl.multiple_of((chunk // per) * (2 * rows) + values * rows, rows)
    at = pl.ds(lax.rem(chunk, per) * blocks, blocks)
    return kv_ref[at, pl.ds(line, rows), :].reshape(blocks * rows, -1)


def tile(refs, which, n, t):
    return refs[n][which, 2 * t : 2 * t + 2].reshape(2 * refs[n].shape[2], -1)


def stats_kernel(
    blocks, rows, query_rows, block_rows, factor,
    where_ref, offset_ref, mine_ref, other_ref, kv_ref, delta_ref, out_ref,
):
    shard, place, core = where_ref[0], where_ref[2], where_ref[3]
    width = 2 * mine_ref.shape[2]
    lines = width // 128
    full = shard // blocks
    pos = row_positions(where_ref, offset_ref, width, query_rows, block_rows)
    scale = factor * LOG2E
    count, total_lines = out_ref.shape[0], out_ref.shape[1]
    out_ref[:, CHIPS * lines :, :] = jnp.broadcast_to(
        delta_ref[...][None], (count, total_lines - CHIPS * lines, 128)
    )
    for n in range(CORES):
        for t in range(CHIPS // 2):
            q = tile((mine_ref, other_ref), 0, n, t)

            def chunk(j, carry, masked=False):
                top, total = carry
                s = dot_nt(cache_slice(kv_ref, j, blocks, rows, 0), q)
                if masked:
                    seen = key_positions(place, j, blocks, rows, block_rows) <= pos
                    s = jnp.where(seen, s, LOW)
                new = jnp.maximum(top, jnp.max(s, axis=0, keepdims=True))
                p = jnp.exp2((s - new) * scale)
                if masked:
                    p = jnp.where(seen, p, 0.0)
                total = total * jnp.exp2((top - new) * scale) + jnp.sum(p, axis=0, keepdims=True)
                return new, total

            start = (jnp.full((1, width), LOW, F32), jnp.zeros((1, width), F32))
            top, total = chunk(full, lax.fori_loop(0, full, chunk, start), masked=True)
            lse = jnp.where(total > 0.0, top * factor + jnp.log(total), LOW)
            line = lax.rem(core + n, CORES) * (CHIPS // 2 * lines) + t * lines
            for m in range(lines):
                out_ref[:, pl.ds(line + m, 1), :] = jnp.broadcast_to(
                    lse[:, m * 128 : (m + 1) * 128][None], (count, 1, 128)
                )


def grads_kernel(
    blocks, rows, query_rows, block_rows, factor,
    where_ref, offset_ref, mine_ref, other_ref, kv_ref, log_ref, delta_ref,
    dkv_ref, dq_own_ref, dq_other_ref, dk_total, dv_total,
):
    shard, place, core = where_ref[0], where_ref[2], where_ref[3]
    flat = mine_ref.shape[2]
    width = 2 * flat
    size = blocks * rows
    full = shard // blocks
    pos = row_positions(where_ref, offset_ref, width, query_rows, block_rows)
    scale = factor * LOG2E
    dk_total[...] = jnp.zeros_like(dk_total)
    dv_total[...] = jnp.zeros_like(dv_total)
    for n in range(CORES):
        for t in range(CHIPS // 2):
            q = tile((mine_ref, other_ref), 0, n, t)
            g = tile((mine_ref, other_ref), 1, n, t)
            at_core = lax.rem(core + n, CORES)
            log_total = log_ref[at_core, t] * LOG2E
            delta = delta_ref[at_core, t]

            def chunk(j, dq, masked=False):
                keys = cache_slice(kv_ref, j, blocks, rows, 0)
                values = cache_slice(kv_ref, j, blocks, rows, 1)
                p = jnp.exp2(dot_nt(keys, q) * scale - log_total)
                if masked:
                    seen = key_positions(place, j, blocks, rows, block_rows) <= pos
                    p = jnp.where(seen, p, 0.0)
                ds = (p * (dot_nt(values, g) - delta)).astype(BF)
                at = pl.ds(pl.multiple_of(j * size, size), size)
                dk_total[at, :] += dot_nn(ds, q)
                dv_total[at, :] += dot_nn(p.astype(BF), g)
                return dq + dot_tn(keys, ds)

            dq = lax.fori_loop(0, full, chunk, jnp.zeros((kv_ref.shape[-1], width), F32))
            dq = chunk(full, dq, masked=True).T
            dq_ref = (dq_own_ref, dq_other_ref)[n]
            for m in range(2):
                dq_ref[2 * t + m] = dq[m * flat : (m + 1) * flat]
    per = kv_ref.shape[0] // blocks
    for j in range(HALVES * per):
        at = slice(j * size, (j + 1) * size)
        to = slice(j * blocks, (j + 1) * blocks)
        dkv_ref[to, 0:rows, :] = dk_total[at, :].astype(BF).reshape(blocks, rows, -1)
        dkv_ref[to, rows : 2 * rows, :] = dv_total[at, :].astype(BF).reshape(blocks, rows, -1)


def pieces_kernel(where_ref, own_ref, other_ref, mine_ref, a_ref, b_ref, c_ref):
    chip = where_ref[1]
    mine_ref[...] = own_ref[chip] + other_ref[chip]
    for k, ref in ((1, a_ref), (2, b_ref), (3, c_ref)):
        to = lax.rem(chip + k, CHIPS)
        ref[...] = (own_ref[to] + other_ref[to]).astype(BF)


def total_kernel(factor, terms_ref, out_ref):
    total = jnp.sum(terms_ref[...].astype(F32), axis=0)
    row = lax.broadcasted_iota(jnp.int32, (total.shape[0], 1), 0)
    total = (total * jnp.where(row < total.shape[0] // 2, factor, 1.0)).astype(BF)
    out_ref[...] = jnp.broadcast_to(total[None], out_ref.shape)


def states_kernel(
    heads, whole_ref, kp_ref, vp_ref, rq_ref, rk_ref, rv_ref, from_ref, to_ref, extra_ref,
    ck_ref, cv_ref, gr_ref, send_ref, wire,
):
    count = whole_ref.shape[0]
    rows = whole_ref.shape[1] // 2
    ck = whole_ref[:, 0:rows, :].reshape(count * rows, -1)
    cv = whole_ref[:, rows:, :].reshape(count * rows, -1)
    ck_ref[...] = ck
    cv_ref[...] = cv
    plane = send_ref.shape[0]
    used = 2 * SLICE * heads
    wire[:, used:, :] = jnp.broadcast_to(extra_ref[...][None], (plane,) + extra_ref.shape)
    for i in range(heads):
        at = slice(i * 128, (i + 1) * 128)
        gr = (dot_nt(ck, kp_ref[at, :]) + dot_nt(cv, vp_ref[at, :])).astype(BF)
        gr_ref[:, at] = gr
        query_w = (rq_ref[:, at].astype(F32) * from_ref[:, i : i + 1]).astype(BF)
        key_w = (rk_ref[:, at].astype(F32) * to_ref[:, i : i + 1]).astype(BF)
        grad = dot_tn(query_w, gr)
        state = dot_tn(key_w, rv_ref[:, at])
        for k in range(SLICE):
            part = slice(k * plane, (k + 1) * plane)
            wire[:, SLICE * i + k, :] = grad[part]
            wire[:, SLICE * (heads + i) + k, :] = state[part]
    send_ref[...] = wire[...].astype(BF)


def totals_kernel(heads, part_ref, decay_ref, out_ref):
    count = part_ref.shape[0]
    zero = jnp.zeros(part_ref.shape[1:], F32)

    def step(b, carry):
        fore, back = carry
        fore = decay_ref[b] * fore + part_ref[b].astype(F32)
        r = count - 1 - b
        back = decay_ref[r] * back + part_ref[r].astype(F32)
        return fore, back

    fore, back = lax.fori_loop(0, count, step, (zero, zero), unroll=4)
    row = lax.broadcasted_iota(jnp.int32, zero.shape, 0)
    out_ref[...] = jnp.where(row < SLICE * heads, back, fore)


def scan_kernel(heads, where_ref, part_ref, decay_ref, other_ref, out_ref, ahead, behind):
    count = part_ref.shape[0]
    upper = where_ref[0] >= count
    other = other_ref[...]
    zero = jnp.zeros_like(other)

    def step(b, carry):
        fore, back = carry
        ahead[b] = fore
        fore = decay_ref[b] * fore + part_ref[b].astype(F32)
        r = count - 1 - b
        behind[r] = back
        back = decay_ref[r] * back + part_ref[r].astype(F32)
        return fore, back

    start = (jnp.where(upper, other, zero), jnp.where(upper, zero, other))
    lax.fori_loop(0, count, step, start, unroll=4)
    row = lax.broadcasted_iota(jnp.int32, part_ref.shape, 1)
    out_ref[...] = jnp.where(row < SLICE * heads, behind[...], ahead[...]).astype(BF)


def final_kernel(
    heads, rq_ref, rk_ref, rv_ref, gr_ref, cum_ref, cum_t_ref, from_ref, to_ref, wire_ref,
    q_ref, k_ref, v_ref, wire,
):
    wire[...] = wire_ref[...].astype(F32)

    def matrix(r):
        return jnp.concatenate([wire[:, r + k, :] for k in range(SLICE)], axis=0).astype(BF)

    size = rq_ref.shape[0]
    t = lax.broadcasted_iota(jnp.int32, (size, size), 0)
    u = lax.broadcasted_iota(jnp.int32, (size, size), 1)
    causal = t >= u
    for i in range(heads):
        at = slice(i * 128, (i + 1) * 128)
        qr, kr, vr, gr = rq_ref[:, at], rk_ref[:, at], rv_ref[:, at], gr_ref[:, at]
        grad_b, state_b = matrix(SLICE * i), matrix(SLICE * (heads + i))
        gap = cum_t_ref[:, i : i + 1] - cum_ref[i : i + 1, :]
        decay = jnp.where(causal, jnp.exp(jnp.where(causal, gap, 0.0)), 0.0)
        from_start, to_end = from_ref[:, i : i + 1], to_ref[:, i : i + 1]
        one = (decay * dot_nt(gr, vr)).astype(BF)
        three = (decay * dot_nt(qr, kr)).astype(BF)
        q_ref[:, at] = dot_nn(one, kr) + from_start * dot_nt(gr, state_b)
        k_ref[:, at] = dot_tn(one, qr) + to_end * dot_nt(vr, grad_b)
        v_ref[:, at] = dot_tn(three, gr) + to_end * dot_nn(kr, grad_b)


def query_grad_kernel(heads, factor, own_ref, a_ref, b_ref, c_ref, out_ref):
    rows = out_ref.shape[1]
    total = own_ref[...] + a_ref[...].astype(F32) + b_ref[...].astype(F32) + c_ref[...].astype(F32)
    total = (total * factor).astype(BF)
    for h in range(heads):
        out_ref[0, :, h * 128 : (h + 1) * 128] = total[h * rows : (h + 1) * rows]


def body(
    offsets,
    queries,
    output_grad,
    attention_out,
    cache_keys,
    cache_values,
    key_projection,
    value_projection,
    retention_query,
    retention_key,
    retention_value,
    retention_decay,
):
    core, chip = lax.axis_index("core"), lax.axis_index("zl")
    place = chip * CORES + core
    secs = CHIPS * CORES
    half = lax.axis_index("zh")
    shard = half * PLANE + lax.axis_index(PLANE_AXES)
    shards = HALVES * PLANE
    block_rows, head = cache_keys.shape
    _, query_rows, query_width = queries.shape
    heads = query_width // head
    flat = query_rows * heads
    width = 2 * flat
    lines = width // 128
    rows = block_rows // secs
    factor = 1.0 / math.sqrt(head)
    blocks = 16
    sizes = (blocks, rows, query_rows, block_rows, factor)
    where = jnp.stack([shard, chip, place, core]).astype(jnp.int32)

    kv_own = jnp.concatenate(
        [lax.dynamic_slice_in_dim(a, place * rows, rows, 0) for a in (cache_keys, cache_values)]
    )
    kv_other = lax.ppermute(kv_own, "zh", [(0, 1), (1, 0)])
    kv = jnp.where(
        half == 0,
        jnp.concatenate([kv_own, kv_other]),
        jnp.concatenate([kv_other, kv_own]),
    )
    kv = jnp.broadcast_to(kv[None], (PLANE,) + kv.shape)
    own = call(
        functools.partial(pack_kernel, heads),
        shape((2 * flat, head), BF), (), (queries, output_grad),
    )
    parts = [own] + [
        lax.ppermute(own, "zl", [(i, (i - k) % CHIPS) for i in range(CHIPS)])
        for k in range(1, CHIPS)
    ]
    delta = call(
        functools.partial(delta_kernel, heads),
        shape((32 - CHIPS * lines, head), F32), (where,), (output_grad, attention_out),
        scratch=[pltpu.VMEM((width, head), F32)],
    )

    local = retention_decay.shape[0]
    used = 2 * SLICE * local
    cum = jnp.cumsum(retention_decay, axis=1)
    cum_t = cum.T
    last = cum[:, -1]
    from_start = jnp.exp(cum_t)
    to_end = jnp.exp(last[None] - cum_t)
    high = last.astype(BF)
    rest = last - high.astype(F32)
    middle = rest.astype(BF)
    low = (rest - middle.astype(F32)).astype(BF)
    extra = jnp.concatenate([high, middle, low]).astype(F32)
    extra = jnp.pad(extra[None], ((0, WIRE - used - 1), (0, head - extra.shape[0])))

    env = (where, offsets, delta, cum, cum_t, from_start, to_end, extra)
    mine = call(gather_kernel, shape((2, CHIPS, flat, head), BF), (where,), tuple(parts))
    mine, kv, env = lax.optimization_barrier((mine, kv, env))
    other = lax.ppermute(mine, "core", [(0, 1), (1, 0)])
    kv = lax.all_to_all(kv, PLANE_AXES, 0, 0, tiled=True)
    mine, other, kv, env = lax.optimization_barrier((mine, other, kv, env))
    where, offsets, delta = env[:3]

    both = call(
        functools.partial(stats_kernel, *sizes),
        shape((secs, 32, head), F32), (where, offsets), (mine, other, kv, delta),
        flops=1 << 30,
    )
    both, (mine, other, kv, env) = pinned_exchange(both, ("zl", "core"), (mine, other, kv, env))
    where, offsets = env[:2]
    tiles = (CORES, CHIPS // 2, 1, width)
    logs = both[:, : CHIPS * lines]
    top = jnp.max(logs, axis=0)
    log_total = (top + jnp.log(jnp.sum(jnp.exp(logs - top), axis=0))).reshape(tiles)
    deltas = both[:, CHIPS * lines : (CHIPS + 1) * lines]
    deltas = deltas.reshape(CHIPS // 2, 2, CORES, lines, head)
    deltas = (deltas[:, 0] + deltas[:, 1]).transpose(1, 0, 2, 3).reshape(tiles)

    dkv, dq_own, dq_other = call(
        functools.partial(grads_kernel, *sizes),
        (shape((shards, 2 * rows, head), BF),) + (shape((CHIPS, flat, head), F32),) * 2,
        (where, offsets),
        (mine, other, kv, log_total, deltas),
        scratch=[pltpu.VMEM((shards * rows, head), F32)] * 2,
        flops=4 << 30,
    )
    terms, (dq_own, dq_other, env) = pinned_exchange(
        dkv, ("zh",) + PLANE_AXES, (dq_own, dq_other, env)
    )
    total = call(
        functools.partial(total_kernel, factor),
        shape((secs, 2 * rows, head), BF), (), (terms,),
    )
    whole, (dq_own, dq_other, env) = pinned_exchange(
        total, ("zl", "core"), (dq_own, dq_other, env)
    )
    where, offsets, delta, cum, cum_t, from_start, to_end, extra = env

    cache_key_grad, cache_value_grad, out_grad, send = call(
        functools.partial(states_kernel, local),
        (
            shape((block_rows, head), BF), shape((block_rows, head), BF),
            shape(retention_query.shape, BF), shape((PLANE, WIRE, head), BF),
        ),
        (),
        (
            whole, key_projection, value_projection,
            retention_query, retention_key, retention_value, from_start, to_end, extra,
        ),
        scratch=[pltpu.VMEM((PLANE, WIRE, head), F32)],
        flops=1 << 27,
    )
    send, dq_own, dq_other = lax.optimization_barrier((send, dq_own, dq_other))
    dq_other = lax.ppermute(dq_other, "core", [(0, 1), (1, 0)])
    part = lax.all_to_all(send, PLANE_AXES, 0, 0, tiled=True)
    part, dq_own, dq_other, where = lax.optimization_barrier((part, dq_own, dq_other, where))
    lasts = part[:, used, : 3 * local].astype(F32).reshape(PLANE, 3, local)
    decays = jnp.exp(lasts[:, 0] + lasts[:, 1] + lasts[:, 2])
    decays = jnp.concatenate([decays, decays], axis=1)
    decays = jnp.broadcast_to(decays[:, :, None], (PLANE, 2 * local, SLICE))
    decays = decays.reshape(PLANE, used, 1)
    decays = jnp.pad(decays, ((0, 0), (0, WIRE - used), (0, 0)))
    decays = jnp.broadcast_to(decays, (PLANE, WIRE, head))
    totals = call(
        functools.partial(totals_kernel, local),
        shape((WIRE, head), F32), (), (part, decays),
    )
    totals, dq_own, dq_other = lax.optimization_barrier((totals, dq_own, dq_other))
    totals = lax.ppermute(totals, "zh", [(0, 1), (1, 0)])
    piece = shape((flat, head), BF)
    dq_mine, *pieces = call(
        pieces_kernel, (shape((flat, head), F32), piece, piece, piece),
        (where,), (dq_own, dq_other), flops=4 << 30,
    )
    enter = call(
        functools.partial(scan_kernel, local),
        shape(part.shape, BF), (where,), (part, decays, totals),
        scratch=[pltpu.VMEM(part.shape, F32)] * 2,
    )
    enter, dq_mine, pieces = lax.optimization_barrier((enter, dq_mine, pieces))
    pieces = [
        lax.ppermute(piece, "zl", [(i, (i + k) % CHIPS) for i in range(CHIPS)])
        for k, piece in enumerate(pieces, 1)
    ]
    enter = lax.all_to_all(enter, PLANE_AXES, 0, 0, tiled=True)
    cross_query_grad = call(
        functools.partial(query_grad_kernel, heads, factor),
        shape(queries.shape, BF), (), (dq_mine, *pieces),
    )
    grads = call(
        functools.partial(final_kernel, local),
        (shape(retention_query.shape, F32),) * 3,
        (),
        (
            retention_query, retention_key, retention_value, out_grad, cum, cum_t,
            from_start, to_end, enter,
        ),
        scratch=[pltpu.VMEM(enter.shape, F32)],
        flops=1 << 28,
    )
    return (cross_query_grad, cache_key_grad, cache_value_grad) + tuple(grads)


def solution(mesh):
    sec, ctx = ("zl", "core"), ("zh", "x", "y")
    split = Mesh(mesh.devices.reshape(CHIPS, CORES, HALVES, 4, 8), sec + ctx)
    in_specs = (
        P(),
        P(sec, ctx, None),
        P(sec, ctx, None),
        P(sec, ctx, None),
        P(ctx, None),
        P(ctx, None),
        P(sec, None),
        P(sec, None),
        P(ctx, sec),
        P(ctx, sec),
        P(ctx, sec),
        P(sec, ctx),
    )
    out_specs = (
        P(sec, ctx, None),
        P(ctx, None),
        P(ctx, None),
        P(ctx, sec),
        P(ctx, sec),
        P(ctx, sec),
    )
    return jax.shard_map(body, mesh=split, in_specs=in_specs, out_specs=out_specs, check_vma=False)
```

```python
import functools
import math

import jax
import jax.numpy as jnp
from jax import lax
from jax.experimental import pallas as pl
from jax.experimental.pallas import tpu as pltpu
from jax.sharding import Mesh
from jax.sharding import PartitionSpec as P

BF = jnp.bfloat16
F32 = jnp.float32
LOW = -1e30
LOG2E = math.log2(math.e)
CHIPS, CORES = 4, 2
HALVES, PLANE = 2, 32
PLANE_AXES = ("x", "y")
SLICE = 4
WIRE = 48
SCOPED = 32 * 1024 * 1024


def dot_nt(a, b):
    return lax.dot_general(a, b, (((1,), (1,)), ((), ())), preferred_element_type=F32)


def dot_nn(a, b):
    return lax.dot_general(a, b, (((1,), (0,)), ((), ())), preferred_element_type=F32)


def dot_tn(a, b):
    return lax.dot_general(a, b, (((0,), (0,)), ((), ())), preferred_element_type=F32)


def call(kernel, outs, in_smem, ins, scratch=(), flops=0):
    vmem = pl.BlockSpec(memory_space=pltpu.VMEM)
    smem = pl.BlockSpec(memory_space=pltpu.SMEM)
    return pl.pallas_call(
        kernel,
        out_shape=outs,
        in_specs=[smem] * len(in_smem) + [vmem] * len(ins),
        out_specs=jax.tree.map(lambda _: vmem, outs),
        scratch_shapes=list(scratch),
        compiler_params=pltpu.CompilerParams(vmem_limit_bytes=SCOPED),
        cost_estimate=pl.CostEstimate(flops=flops, bytes_accessed=1 << 20, transcendentals=0),
    )(*in_smem, *ins)


def shape(dims, dtype):
    return jax.ShapeDtypeStruct(dims, dtype)


def pinned_exchange(array, axes, later):
    array, later = lax.optimization_barrier((array, later))
    array = lax.all_to_all(array, axes, 0, 0, tiled=True)
    return lax.optimization_barrier((array, later))


def pack_kernel(heads, q_ref, g_ref, out_ref):
    rows = q_ref.shape[1]
    for h in range(heads):
        at = slice(h * 128, (h + 1) * 128)
        out_ref[h * rows : (h + 1) * rows, :] = q_ref[0, :, at]
        out_ref[(heads + h) * rows : (heads + h + 1) * rows, :] = g_ref[0, :, at]


def delta_kernel(heads, where_ref, g_ref, o_ref, out_ref, product):
    rows = g_ref.shape[1]
    base = lax.rem(where_ref[1], 2) * (heads * rows)
    product[...] = jnp.zeros_like(product)
    for h in range(heads):
        at = slice(h * 128, (h + 1) * 128)
        to = pl.ds(pl.multiple_of(base + h * rows, rows), rows)
        product[to, :] = g_ref[0, :, at].astype(F32) * o_ref[0, :, at].astype(F32)
    sums = jnp.sum(product[...].T, axis=0, keepdims=True)
    out_ref[...] = jnp.zeros_like(out_ref)
    for n in range(sums.shape[1] // 128):
        out_ref[n : n + 1, :] = sums[:, n * 128 : (n + 1) * 128]


def gather_kernel(where_ref, a_ref, b_ref, c_ref, d_ref, out_ref):
    flat = out_ref.shape[2]
    for k, ref in enumerate((a_ref, b_ref, c_ref, d_ref)):
        chip = lax.rem(where_ref[1] + k, CHIPS)
        out_ref[0, chip] = ref[0:flat]
        out_ref[1, chip] = ref[flat:]


def row_positions(where_ref, offset_ref, width, rows, block_rows):
    lane = lax.broadcasted_iota(jnp.int32, (1, width), 1)
    shard = where_ref[0]
    return lax.rem(lane, rows) + (shard * block_rows + offset_ref[shard])


def key_positions(place, chunk, blocks, rows, block_rows):
    at = lax.broadcasted_iota(jnp.int32, (blocks * rows, 1), 0)
    return (chunk * blocks + at // rows) * block_rows + place * rows + at % rows


def cache_slice(kv_ref, chunk, blocks, rows, values):
    per = kv_ref.shape[0] // blocks
    line = pl.multiple_of((chunk // per) * (2 * rows) + values * rows, rows)
    at = pl.ds(lax.rem(chunk, per) * blocks, blocks)
    return kv_ref[at, pl.ds(line, rows), :].reshape(blocks * rows, -1)


def tile(refs, which, n, t):
    return refs[n][which, 2 * t : 2 * t + 2].reshape(2 * refs[n].shape[2], -1)


def stats_kernel(
    blocks, rows, query_rows, block_rows, factor, where_ref, offset_ref, rows_ref, kv_ref, out_ref,
):
    shard, place = where_ref[0], where_ref[2]
    width = 2 * rows_ref.shape[2]
    lines = width // 128
    full = shard // blocks
    pos = row_positions(where_ref, offset_ref, width, query_rows, block_rows)
    scale = factor * LOG2E
    tiles = range(CHIPS // 2)

    def chunk(j, carry, masked=False):
        keys = cache_slice(kv_ref, j, blocks, rows, 0)
        if masked:
            seen = key_positions(place, j, blocks, rows, block_rows) <= pos
        out = []
        for t, (top, total) in zip(tiles, carry):
            s = dot_nt(keys, tile((rows_ref,), 0, 0, t))
            if masked:
                s = jnp.where(seen, s, LOW)
            new = jnp.maximum(top, jnp.max(s, axis=0, keepdims=True))
            p = jnp.exp2((s - new) * scale)
            if masked:
                p = jnp.where(seen, p, 0.0)
            total = total * jnp.exp2((top - new) * scale) + jnp.sum(p, axis=0, keepdims=True)
            out.append((new, total))
        return tuple(out)

    start = ((jnp.full((1, width), LOW, F32), jnp.zeros((1, width), F32)),) * len(tiles)
    done = chunk(full, lax.fori_loop(0, full, chunk, start), masked=True)
    for t, (top, total) in zip(tiles, done):
        lse = jnp.where(total > 0.0, top * factor + jnp.log(total), LOW)
        for m in range(lines):
            out_ref[t * lines + m : t * lines + m + 1, :] = lse[:, m * 128 : (m + 1) * 128]


def grads_kernel(
    blocks, rows, query_rows, block_rows, factor,
    where_ref, offset_ref, mine_ref, other_ref, kv_ref, log_ref, delta_ref,
    dkv_ref, dq_own_ref, dq_other_ref, dq_total,
):
    shard, place, core = where_ref[0], where_ref[2], where_ref[3]
    flat = mine_ref.shape[2]
    width = 2 * flat
    size = blocks * rows
    full = shard // blocks
    pos = row_positions(where_ref, offset_ref, width, query_rows, block_rows)
    scale = factor * LOG2E
    tiles = [(n, t) for n in range(CORES) for t in range(CHIPS // 2)]
    dq_total[...] = jnp.zeros_like(dq_total)

    def chunk(j, masked=False):
        keys = cache_slice(kv_ref, j, blocks, rows, 0)
        values = cache_slice(kv_ref, j, blocks, rows, 1)
        if masked:
            seen = key_positions(place, j, blocks, rows, block_rows) <= pos
        dk = dv = 0.0
        for i, (n, t) in enumerate(tiles):
            q = tile((mine_ref, other_ref), 0, n, t)
            g = tile((mine_ref, other_ref), 1, n, t)
            at_core = lax.rem(core + n, CORES)
            p = jnp.exp2(dot_nt(keys, q) * scale - log_ref[at_core, t] * LOG2E)
            if masked:
                p = jnp.where(seen, p, 0.0)
            ds = (p * (dot_nt(values, g) - delta_ref[at_core, t])).astype(BF)
            dk = dk + dot_nn(ds, q)
            dv = dv + dot_nn(p.astype(BF), g)
            dq_total[i] += dot_tn(keys, ds)
        at = pl.ds(pl.multiple_of(j * blocks, blocks), blocks)
        dkv_ref[at, 0:rows, :] = dk.astype(BF).reshape(blocks, rows, -1)
        dkv_ref[at, rows : 2 * rows, :] = dv.astype(BF).reshape(blocks, rows, -1)

    def step(j, _):
        chunk(j)
        return 0

    lax.fori_loop(0, full, step, 0)
    chunk(full, masked=True)

    def clear(j, _):
        at = pl.ds(pl.multiple_of(j * blocks, blocks), blocks)
        dkv_ref[at] = jnp.zeros((blocks, 2 * rows, kv_ref.shape[-1]), BF)
        return 0

    lax.fori_loop(full + 1, dkv_ref.shape[0] // blocks, clear, 0)
    for i, (n, t) in enumerate(tiles):
        dq = dq_total[i].T
        dq_ref = (dq_own_ref, dq_other_ref)[n]
        for m in range(2):
            dq_ref[2 * t + m] = dq[m * flat : (m + 1) * flat]


def pieces_kernel(where_ref, own_ref, other_ref, mine_ref, a_ref, b_ref, c_ref):
    chip = where_ref[1]
    mine_ref[...] = own_ref[chip] + other_ref[chip]
    for k, ref in ((1, a_ref), (2, b_ref), (3, c_ref)):
        to = lax.rem(chip + k, CHIPS)
        ref[...] = (own_ref[to] + other_ref[to]).astype(BF)


def total_kernel(factor, terms_ref, out_ref):
    total = jnp.sum(terms_ref[...].astype(F32), axis=0)
    row = lax.broadcasted_iota(jnp.int32, (total.shape[0], 1), 0)
    total = (total * jnp.where(row < total.shape[0] // 2, factor, 1.0)).astype(BF)
    out_ref[...] = jnp.broadcast_to(total[None], out_ref.shape)


def states_kernel(
    heads, whole_ref, kp_ref, vp_ref, rq_ref, rk_ref, rv_ref, from_ref, to_ref, extra_ref,
    ck_ref, cv_ref, gr_ref, send_ref, wire,
):
    count = whole_ref.shape[0]
    rows = whole_ref.shape[1] // 2
    ck = whole_ref[:, 0:rows, :].reshape(count * rows, -1)
    cv = whole_ref[:, rows:, :].reshape(count * rows, -1)
    ck_ref[...] = ck
    cv_ref[...] = cv
    plane = send_ref.shape[0]
    used = 2 * SLICE * heads
    wire[:, used:, :] = jnp.broadcast_to(extra_ref[...][None], (plane,) + extra_ref.shape)
    for i in range(heads):
        at = slice(i * 128, (i + 1) * 128)
        gr = (dot_nt(ck, kp_ref[at, :]) + dot_nt(cv, vp_ref[at, :])).astype(BF)
        gr_ref[:, at] = gr
        query_w = (rq_ref[:, at].astype(F32) * from_ref[:, i : i + 1]).astype(BF)
        key_w = (rk_ref[:, at].astype(F32) * to_ref[:, i : i + 1]).astype(BF)
        grad = dot_tn(query_w, gr)
        state = dot_tn(key_w, rv_ref[:, at])
        for k in range(SLICE):
            part = slice(k * plane, (k + 1) * plane)
            wire[:, SLICE * i + k, :] = grad[part]
            wire[:, SLICE * (heads + i) + k, :] = state[part]
    send_ref[...] = wire[...].astype(BF)


def totals_kernel(heads, part_ref, decay_ref, out_ref):
    count = part_ref.shape[0]
    zero = jnp.zeros(part_ref.shape[1:], F32)

    def step(b, carry):
        fore, back = carry
        fore = decay_ref[b] * fore + part_ref[b].astype(F32)
        r = count - 1 - b
        back = decay_ref[r] * back + part_ref[r].astype(F32)
        return fore, back

    fore, back = lax.fori_loop(0, count, step, (zero, zero), unroll=4)
    row = lax.broadcasted_iota(jnp.int32, zero.shape, 0)
    out_ref[...] = jnp.where(row < SLICE * heads, back, fore)


def scan_kernel(heads, where_ref, part_ref, decay_ref, other_ref, out_ref, ahead, behind):
    count = part_ref.shape[0]
    upper = where_ref[0] >= count
    other = other_ref[...]
    zero = jnp.zeros_like(other)

    def step(b, carry):
        fore, back = carry
        ahead[b] = fore
        fore = decay_ref[b] * fore + part_ref[b].astype(F32)
        r = count - 1 - b
        behind[r] = back
        back = decay_ref[r] * back + part_ref[r].astype(F32)
        return fore, back

    start = (jnp.where(upper, other, zero), jnp.where(upper, zero, other))
    lax.fori_loop(0, count, step, start, unroll=4)
    row = lax.broadcasted_iota(jnp.int32, part_ref.shape, 1)
    out_ref[...] = jnp.where(row < SLICE * heads, behind[...], ahead[...]).astype(BF)


def final_kernel(
    heads, rq_ref, rk_ref, rv_ref, gr_ref, cum_ref, cum_t_ref, from_ref, to_ref, wire_ref,
    q_ref, k_ref, v_ref, wire,
):
    wire[...] = wire_ref[...].astype(F32)

    def matrix(r):
        return jnp.concatenate([wire[:, r + k, :] for k in range(SLICE)], axis=0).astype(BF)

    size = rq_ref.shape[0]
    t = lax.broadcasted_iota(jnp.int32, (size, size), 0)
    u = lax.broadcasted_iota(jnp.int32, (size, size), 1)
    causal = t >= u
    for i in range(heads):
        at = slice(i * 128, (i + 1) * 128)
        qr, kr, vr, gr = rq_ref[:, at], rk_ref[:, at], rv_ref[:, at], gr_ref[:, at]
        grad_b, state_b = matrix(SLICE * i), matrix(SLICE * (heads + i))
        gap = cum_t_ref[:, i : i + 1] - cum_ref[i : i + 1, :]
        decay = jnp.where(causal, jnp.exp(jnp.where(causal, gap, 0.0)), 0.0)
        from_start, to_end = from_ref[:, i : i + 1], to_ref[:, i : i + 1]
        one = (decay * dot_nt(gr, vr)).astype(BF)
        three = (decay * dot_nt(qr, kr)).astype(BF)
        q_ref[:, at] = dot_nn(one, kr) + from_start * dot_nt(gr, state_b)
        k_ref[:, at] = dot_tn(one, qr) + to_end * dot_nt(vr, grad_b)
        v_ref[:, at] = dot_tn(three, gr) + to_end * dot_nn(kr, grad_b)


def query_grad_kernel(heads, factor, own_ref, a_ref, b_ref, c_ref, out_ref):
    rows = out_ref.shape[1]
    total = own_ref[...] + a_ref[...].astype(F32) + b_ref[...].astype(F32) + c_ref[...].astype(F32)
    total = (total * factor).astype(BF)
    for h in range(heads):
        out_ref[0, :, h * 128 : (h + 1) * 128] = total[h * rows : (h + 1) * rows]


def body(
    offsets,
    queries,
    output_grad,
    attention_out,
    cache_keys,
    cache_values,
    key_projection,
    value_projection,
    retention_query,
    retention_key,
    retention_value,
    retention_decay,
):
    core, chip = lax.axis_index("core"), lax.axis_index("zl")
    place = chip * CORES + core
    secs = CHIPS * CORES
    half = lax.axis_index("zh")
    shard = half * PLANE + lax.axis_index(PLANE_AXES)
    shards = HALVES * PLANE
    block_rows, head = cache_keys.shape
    _, query_rows, query_width = queries.shape
    heads = query_width // head
    flat = query_rows * heads
    width = 2 * flat
    lines = width // 128
    rows = block_rows // secs
    factor = 1.0 / math.sqrt(head)
    blocks = 32
    sizes = (blocks, rows, query_rows, block_rows, factor)
    where = jnp.stack([shard, chip, place, core]).astype(jnp.int32)

    kv_own = jnp.concatenate(
        [lax.dynamic_slice_in_dim(a, place * rows, rows, 0) for a in (cache_keys, cache_values)]
    )
    kv_other = lax.ppermute(kv_own, "zh", [(0, 1), (1, 0)])
    kv = jnp.where(
        half == 0,
        jnp.concatenate([kv_own, kv_other]),
        jnp.concatenate([kv_other, kv_own]),
    )
    kv = jnp.broadcast_to(kv[None], (PLANE,) + kv.shape)
    own = call(
        functools.partial(pack_kernel, heads),
        shape((2 * flat, head), BF), (), (queries, output_grad),
    )
    parts = [own] + [
        lax.ppermute(own, "zl", [(i, (i - k) % CHIPS) for i in range(CHIPS)])
        for k in range(1, CHIPS)
    ]
    delta = call(
        functools.partial(delta_kernel, heads),
        shape((32 - CHIPS * lines, head), F32), (where,), (output_grad, attention_out),
        scratch=[pltpu.VMEM((width, head), F32)],
    )

    local = retention_decay.shape[0]
    used = 2 * SLICE * local
    cum = jnp.cumsum(retention_decay, axis=1)
    cum_t = cum.T
    last = cum[:, -1]
    from_start = jnp.exp(cum_t)
    to_end = jnp.exp(last[None] - cum_t)
    high = last.astype(BF)
    rest = last - high.astype(F32)
    middle = rest.astype(BF)
    low = (rest - middle.astype(F32)).astype(BF)
    extra = jnp.concatenate([high, middle, low]).astype(F32)
    extra = jnp.pad(extra[None], ((0, WIRE - used - 1), (0, head - extra.shape[0])))

    env = (where, offsets, delta, cum, cum_t, from_start, to_end, extra)
    mine = call(gather_kernel, shape((2, CHIPS, flat, head), BF), (where,), tuple(parts))
    kv, env = lax.optimization_barrier((kv, env))
    kv = lax.all_to_all(kv, PLANE_AXES, 0, 0, tiled=True)
    kv, env = lax.optimization_barrier((kv, env))
    where, offsets, delta = env[:3]
    other = lax.ppermute(mine, "core", [(0, 1), (1, 0)])

    stats = [
        call(
            functools.partial(stats_kernel, *sizes),
            shape((CHIPS // 2 * lines, head), F32), (where, offsets), (part, kv),
            flops=4 << 30,
        )
        for part in (mine, other)
    ]
    own_stats, other_stats = stats
    both = jnp.concatenate([
        jnp.where(core == 0, own_stats, other_stats),
        jnp.where(core == 0, other_stats, own_stats),
        delta,
    ])
    both = jnp.broadcast_to(both[None], (secs,) + both.shape)
    both, (mine, other, kv, env) = pinned_exchange(both, ("zl", "core"), (mine, other, kv, env))
    where, offsets = env[:2]
    tiles = (CORES, CHIPS // 2, 1, width)
    logs = both[:, : CHIPS * lines]
    top = jnp.max(logs, axis=0)
    log_total = (top + jnp.log(jnp.sum(jnp.exp(logs - top), axis=0))).reshape(tiles)
    deltas = both[:, CHIPS * lines : (CHIPS + 1) * lines]
    deltas = deltas.reshape(CHIPS // 2, 2, CORES, lines, head)
    deltas = (deltas[:, 0] + deltas[:, 1]).transpose(1, 0, 2, 3).reshape(tiles)

    dkv, dq_own, dq_other = call(
        functools.partial(grads_kernel, *sizes),
        (shape((shards, 2 * rows, head), BF),) + (shape((CHIPS, flat, head), F32),) * 2,
        (where, offsets),
        (mine, other, kv, log_total, deltas),
        scratch=[pltpu.VMEM((CORES * CHIPS // 2, head, width), F32)],
        flops=4 << 30,
    )
    terms, env = pinned_exchange(dkv, ("zh",) + PLANE_AXES, env)
    total = call(
        functools.partial(total_kernel, factor),
        shape((secs, 2 * rows, head), BF), (), (terms,),
    )
    whole, env = pinned_exchange(total, ("zl", "core"), env)
    where, offsets, delta, cum, cum_t, from_start, to_end, extra = env

    cache_key_grad, cache_value_grad, out_grad, send = call(
        functools.partial(states_kernel, local),
        (
            shape((block_rows, head), BF), shape((block_rows, head), BF),
            shape(retention_query.shape, BF), shape((PLANE, WIRE, head), BF),
        ),
        (),
        (
            whole, key_projection, value_projection,
            retention_query, retention_key, retention_value, from_start, to_end, extra,
        ),
        scratch=[pltpu.VMEM((PLANE, WIRE, head), F32)],
        flops=1 << 27,
    )
    send, dq_own, dq_other = lax.optimization_barrier((send, dq_own, dq_other))
    dq_other = lax.ppermute(dq_other, "core", [(0, 1), (1, 0)])
    part = lax.all_to_all(send, PLANE_AXES, 0, 0, tiled=True)
    part, dq_own, dq_other, where = lax.optimization_barrier((part, dq_own, dq_other, where))
    lasts = part[:, used, : 3 * local].astype(F32).reshape(PLANE, 3, local)
    decays = jnp.exp(lasts[:, 0] + lasts[:, 1] + lasts[:, 2])
    decays = jnp.concatenate([decays, decays], axis=1)
    decays = jnp.broadcast_to(decays[:, :, None], (PLANE, 2 * local, SLICE))
    decays = decays.reshape(PLANE, used, 1)
    decays = jnp.pad(decays, ((0, 0), (0, WIRE - used), (0, 0)))
    decays = jnp.broadcast_to(decays, (PLANE, WIRE, head))
    totals = call(
        functools.partial(totals_kernel, local),
        shape((WIRE, head), F32), (), (part, decays),
    )
    totals, dq_own, dq_other = lax.optimization_barrier((totals, dq_own, dq_other))
    totals = lax.ppermute(totals, "zh", [(0, 1), (1, 0)])
    piece = shape((flat, head), BF)
    dq_mine, *pieces = call(
        pieces_kernel, (shape((flat, head), F32), piece, piece, piece),
        (where,), (dq_own, dq_other), flops=4 << 30,
    )
    enter = call(
        functools.partial(scan_kernel, local),
        shape(part.shape, BF), (where,), (part, decays, totals),
        scratch=[pltpu.VMEM(part.shape, F32)] * 2,
    )
    enter, dq_mine, pieces = lax.optimization_barrier((enter, dq_mine, pieces))
    pieces = [
        lax.ppermute(piece, "zl", [(i, (i + k) % CHIPS) for i in range(CHIPS)])
        for k, piece in enumerate(pieces, 1)
    ]
    enter = lax.all_to_all(enter, PLANE_AXES, 0, 0, tiled=True)
    cross_query_grad = call(
        functools.partial(query_grad_kernel, heads, factor),
        shape(queries.shape, BF), (), (dq_mine, *pieces),
    )
    grads = call(
        functools.partial(final_kernel, local),
        (shape(retention_query.shape, F32),) * 3,
        (),
        (
            retention_query, retention_key, retention_value, out_grad, cum, cum_t,
            from_start, to_end, enter,
        ),
        scratch=[pltpu.VMEM(enter.shape, F32)],
        flops=1 << 28,
    )
    return (cross_query_grad, cache_key_grad, cache_value_grad) + tuple(grads)


def solution(mesh):
    sec, ctx = ("zl", "core"), ("zh", "x", "y")
    split = Mesh(mesh.devices.reshape(CHIPS, CORES, HALVES, 4, 8), sec + ctx)
    in_specs = (
        P(),
        P(sec, ctx, None),
        P(sec, ctx, None),
        P(sec, ctx, None),
        P(ctx, None),
        P(ctx, None),
        P(sec, None),
        P(sec, None),
        P(ctx, sec),
        P(ctx, sec),
        P(ctx, sec),
        P(sec, ctx),
    )
    out_specs = (
        P(sec, ctx, None),
        P(ctx, None),
        P(ctx, None),
        P(ctx, sec),
        P(ctx, sec),
        P(ctx, sec),
    )
    return jax.shard_map(body, mesh=split, in_specs=in_specs, out_specs=out_specs, check_vma=False)
```

```python
import functools
import math

import jax
import jax.numpy as jnp
from jax import lax
from jax.experimental import pallas as pl
from jax.experimental.pallas import tpu as pltpu
from jax.sharding import Mesh
from jax.sharding import PartitionSpec as P

BF = jnp.bfloat16
F32 = jnp.float32
LOW = -1e30
LOG2E = math.log2(math.e)
CHIPS, CORES = 4, 2
HALVES, PLANE = 2, 32
PLANE_AXES = ("x", "y")
SLICE = 4
WIRE = 48
SCOPED = 32 * 1024 * 1024


def dot_nt(a, b):
    return lax.dot_general(a, b, (((1,), (1,)), ((), ())), preferred_element_type=F32)


def dot_nn(a, b):
    return lax.dot_general(a, b, (((1,), (0,)), ((), ())), preferred_element_type=F32)


def dot_tn(a, b):
    return lax.dot_general(a, b, (((0,), (0,)), ((), ())), preferred_element_type=F32)


def call(kernel, outs, in_smem, ins, scratch=(), flops=0):
    vmem = pl.BlockSpec(memory_space=pltpu.VMEM)
    smem = pl.BlockSpec(memory_space=pltpu.SMEM)
    return pl.pallas_call(
        kernel,
        out_shape=outs,
        in_specs=[smem] * len(in_smem) + [vmem] * len(ins),
        out_specs=jax.tree.map(lambda _: vmem, outs),
        scratch_shapes=list(scratch),
        compiler_params=pltpu.CompilerParams(vmem_limit_bytes=SCOPED),
        cost_estimate=pl.CostEstimate(flops=flops, bytes_accessed=1 << 20, transcendentals=0),
    )(*in_smem, *ins)


def shape(dims, dtype):
    return jax.ShapeDtypeStruct(dims, dtype)


def pinned_exchange(array, axes, later):
    array, later = lax.optimization_barrier((array, later))
    array = lax.all_to_all(array, axes, 0, 0, tiled=True)
    return lax.optimization_barrier((array, later))


def pack_kernel(heads, q_ref, g_ref, out_ref):
    rows = q_ref.shape[1]
    for h in range(heads):
        at = slice(h * 128, (h + 1) * 128)
        out_ref[h * rows : (h + 1) * rows, :] = q_ref[0, :, at]
        out_ref[(heads + h) * rows : (heads + h + 1) * rows, :] = g_ref[0, :, at]


def delta_kernel(heads, where_ref, g_ref, o_ref, out_ref, product):
    rows = g_ref.shape[1]
    base = lax.rem(where_ref[1], 2) * (heads * rows)
    product[...] = jnp.zeros_like(product)
    for h in range(heads):
        at = slice(h * 128, (h + 1) * 128)
        to = pl.ds(pl.multiple_of(base + h * rows, rows), rows)
        product[to, :] = g_ref[0, :, at].astype(F32) * o_ref[0, :, at].astype(F32)
    sums = jnp.sum(product[...].T, axis=0, keepdims=True)
    out_ref[...] = jnp.zeros_like(out_ref)
    for n in range(sums.shape[1] // 128):
        out_ref[n : n + 1, :] = sums[:, n * 128 : (n + 1) * 128]


def gather_kernel(where_ref, a_ref, b_ref, c_ref, d_ref, out_ref):
    flat = out_ref.shape[2]
    for k, ref in enumerate((a_ref, b_ref, c_ref, d_ref)):
        chip = lax.rem(where_ref[1] + k, CHIPS)
        out_ref[0, chip] = ref[0:flat]
        out_ref[1, chip] = ref[flat:]


def row_positions(where_ref, offset_ref, width, rows, block_rows):
    lane = lax.broadcasted_iota(jnp.int32, (1, width), 1)
    shard = where_ref[0]
    return lax.rem(lane, rows) + (shard * block_rows + offset_ref[shard])


def key_positions(place, chunk, blocks, rows, block_rows):
    at = lax.broadcasted_iota(jnp.int32, (blocks * rows, 1), 0)
    return (chunk * blocks + at // rows) * block_rows + place * rows + at % rows


def cache_place(kv_ref, chunk, blocks, rows):
    per = kv_ref.shape[0] // blocks
    line = pl.multiple_of((chunk // per) * (2 * rows), 2 * rows)
    return pl.ds(pl.multiple_of(lax.rem(chunk, per) * blocks, blocks), blocks), line


def cache_slice(kv_ref, chunk, blocks, rows, values):
    at, line = cache_place(kv_ref, chunk, blocks, rows)
    line = pl.multiple_of(line + values * rows, rows)
    return kv_ref[at, pl.ds(line, rows), :].reshape(blocks * rows, -1)


def tile(refs, which, n, t):
    return refs[n][which, 2 * t : 2 * t + 2].reshape(2 * refs[n].shape[2], -1)


def stats_kernel(
    blocks, rows, query_rows, block_rows, factor, where_ref, offset_ref, rows_ref, kv_ref, out_ref,
):
    shard, place = where_ref[0], where_ref[2]
    width = 2 * rows_ref.shape[2]
    lines = width // 128
    full = shard // blocks
    pos = row_positions(where_ref, offset_ref, width, query_rows, block_rows)
    scale = factor * LOG2E
    tiles = range(CHIPS // 2)

    def chunk(j, carry, masked=False):
        keys = cache_slice(kv_ref, j, blocks, rows, 0)
        if masked:
            seen = key_positions(place, j, blocks, rows, block_rows) <= pos
        out = []
        for t, (top, total) in zip(tiles, carry):
            s = dot_nt(keys, tile((rows_ref,), 0, 0, t))
            if masked:
                s = jnp.where(seen, s, LOW)
            new = jnp.maximum(top, jnp.max(s, axis=0, keepdims=True))
            p = jnp.exp2((s - new) * scale)
            if masked:
                p = jnp.where(seen, p, 0.0)
            total = total * jnp.exp2((top - new) * scale) + jnp.sum(p, axis=0, keepdims=True)
            out.append((new, total))
        return tuple(out)

    start = ((jnp.full((1, width), LOW, F32), jnp.zeros((1, width), F32)),) * len(tiles)
    done = chunk(full, lax.fori_loop(0, full, chunk, start), masked=True)
    for t, (top, total) in zip(tiles, done):
        lse = jnp.where(total > 0.0, top * factor + jnp.log(total), LOW)
        for m in range(lines):
            out_ref[t * lines + m : t * lines + m + 1, :] = lse[:, m * 128 : (m + 1) * 128]


def grads_kernel(
    blocks, rows, query_rows, block_rows, factor,
    where_ref, offset_ref, mine_ref, other_ref, kv_ref, log_ref, delta_ref,
    dkv_ref, dq_own_ref, dq_other_ref, dq_total,
):
    shard, place, core = where_ref[0], where_ref[2], where_ref[3]
    flat = mine_ref.shape[2]
    width = 2 * flat
    size = blocks * rows
    full = shard // blocks
    pos = row_positions(where_ref, offset_ref, width, query_rows, block_rows)
    scale = factor * LOG2E
    tiles = [(n, t) for n in range(CORES) for t in range(CHIPS // 2)]
    dq_total[...] = jnp.zeros_like(dq_total)

    def chunk(j, masked=False):
        keys = cache_slice(kv_ref, j, blocks, rows, 0)
        values = cache_slice(kv_ref, j, blocks, rows, 1)
        if masked:
            seen = key_positions(place, j, blocks, rows, block_rows) <= pos
        dk = dv = 0.0
        for i, (n, t) in enumerate(tiles):
            q = tile((mine_ref, other_ref), 0, n, t)
            g = tile((mine_ref, other_ref), 1, n, t)
            at_core = lax.rem(core + n, CORES)
            p = jnp.exp2(dot_nt(keys, q) * scale - log_ref[at_core, t] * LOG2E)
            if masked:
                p = jnp.where(seen, p, 0.0)
            ds = (p * (dot_nt(values, g) - delta_ref[at_core, t])).astype(BF)
            dk = dk + dot_nn(ds, q)
            dv = dv + dot_nn(p.astype(BF), g)
            dq_total[i] += dot_tn(keys, ds)
        at, line = cache_place(kv_ref, j, blocks, rows)
        dkv_ref[at, pl.ds(line, rows), :] = dk.astype(BF).reshape(blocks, rows, -1)
        dkv_ref[at, pl.ds(line + rows, rows), :] = dv.astype(BF).reshape(blocks, rows, -1)

    def step(j, _):
        chunk(j)
        return 0

    lax.fori_loop(0, full, step, 0)
    chunk(full, masked=True)

    def clear(j, _):
        at, line = cache_place(kv_ref, j, blocks, rows)
        dkv_ref[at, pl.ds(line, 2 * rows), :] = jnp.zeros((blocks, 2 * rows, kv_ref.shape[-1]), BF)
        return 0

    lax.fori_loop(full + 1, HALVES * kv_ref.shape[0] // blocks, clear, 0)
    for i, (n, t) in enumerate(tiles):
        dq = dq_total[i].T
        dq_ref = (dq_own_ref, dq_other_ref)[n]
        for m in range(2):
            dq_ref[2 * t + m] = dq[m * flat : (m + 1) * flat].astype(dq_ref.dtype)


def chip_pairs_kernel(where_ref, own_ref, other_ref, keep_ref, send_ref):
    pair = where_ref[1] // 2
    for m in range(2):
        to = 2 * pair + m
        keep_ref[m] = own_ref[to] + other_ref[to].astype(F32)
        to = 2 * (1 - pair) + m
        send_ref[m] = (own_ref[to] + other_ref[to].astype(F32)).astype(BF)


def chips_kernel(where_ref, keep_ref, got_ref, own_ref, send_ref):
    own = lax.rem(where_ref[1], 2)
    own_ref[...] = keep_ref[own] + got_ref[own].astype(F32)
    send_ref[...] = (keep_ref[1 - own] + got_ref[1 - own].astype(F32)).astype(BF)


def total_kernel(factor, terms_ref, out_ref):
    total = jnp.sum(terms_ref[...].astype(F32), axis=0)
    lines = out_ref.shape[1]
    row = lax.broadcasted_iota(jnp.int32, (lines, 1), 0)
    scale = jnp.where(row < lines // 2, factor, 1.0)
    count = out_ref.shape[0] // HALVES
    for n in range(HALVES):
        part = (total[n * lines : (n + 1) * lines] * scale).astype(BF)
        out_ref[n * count : (n + 1) * count] = jnp.broadcast_to(part[None], (count,) + part.shape)


def states_kernel(
    heads, whole_ref, kp_ref, vp_ref, rq_ref, rk_ref, rv_ref, from_ref, to_ref, extra_ref,
    ck_ref, cv_ref, gr_ref, send_ref, wire,
):
    count = whole_ref.shape[0] // HALVES
    rows = whole_ref.shape[1] // 2
    both = (whole_ref[0:count].astype(F32) + whole_ref[count:].astype(F32)).astype(BF)
    ck = both[:, 0:rows, :].reshape(count * rows, -1)
    cv = both[:, rows:, :].reshape(count * rows, -1)
    ck_ref[...] = ck
    cv_ref[...] = cv
    plane = send_ref.shape[0]
    used = 2 * SLICE * heads
    wire[:, used:, :] = jnp.broadcast_to(extra_ref[...][None], (plane,) + extra_ref.shape)
    for i in range(heads):
        at = slice(i * 128, (i + 1) * 128)
        gr = (dot_nt(ck, kp_ref[at, :]) + dot_nt(cv, vp_ref[at, :])).astype(BF)
        gr_ref[:, at] = gr
        query_w = (rq_ref[:, at].astype(F32) * from_ref[:, i : i + 1]).astype(BF)
        key_w = (rk_ref[:, at].astype(F32) * to_ref[:, i : i + 1]).astype(BF)
        grad = dot_tn(query_w, gr)
        state = dot_tn(key_w, rv_ref[:, at])
        for k in range(SLICE):
            part = slice(k * plane, (k + 1) * plane)
            wire[:, SLICE * i + k, :] = grad[part]
            wire[:, SLICE * (heads + i) + k, :] = state[part]
    send_ref[...] = wire[...].astype(BF)


def totals_kernel(heads, part_ref, decay_ref, out_ref):
    count = part_ref.shape[0]
    zero = jnp.zeros(part_ref.shape[1:], F32)

    def step(b, carry):
        fore, back = carry
        fore = decay_ref[b] * fore + part_ref[b].astype(F32)
        r = count - 1 - b
        back = decay_ref[r] * back + part_ref[r].astype(F32)
        return fore, back

    fore, back = lax.fori_loop(0, count, step, (zero, zero), unroll=4)
    row = lax.broadcasted_iota(jnp.int32, zero.shape, 0)
    out_ref[...] = jnp.where(row < SLICE * heads, back, fore)


def scan_kernel(heads, where_ref, part_ref, decay_ref, other_ref, out_ref, ahead, behind):
    count = part_ref.shape[0]
    upper = where_ref[0] >= count
    other = other_ref[...]
    zero = jnp.zeros_like(other)

    def step(b, carry):
        fore, back = carry
        ahead[b] = fore
        fore = decay_ref[b] * fore + part_ref[b].astype(F32)
        r = count - 1 - b
        behind[r] = back
        back = decay_ref[r] * back + part_ref[r].astype(F32)
        return fore, back

    start = (jnp.where(upper, other, zero), jnp.where(upper, zero, other))
    lax.fori_loop(0, count, step, start, unroll=4)
    row = lax.broadcasted_iota(jnp.int32, part_ref.shape, 1)
    out_ref[...] = jnp.where(row < SLICE * heads, behind[...], ahead[...]).astype(BF)


def final_kernel(
    heads, rq_ref, rk_ref, rv_ref, gr_ref, cum_ref, cum_t_ref, from_ref, to_ref, wire_ref,
    q_ref, k_ref, v_ref, wire,
):
    wire[...] = wire_ref[...].astype(F32)

    def matrix(r):
        return jnp.concatenate([wire[:, r + k, :] for k in range(SLICE)], axis=0).astype(BF)

    size = rq_ref.shape[0]
    t = lax.broadcasted_iota(jnp.int32, (size, size), 0)
    u = lax.broadcasted_iota(jnp.int32, (size, size), 1)
    causal = t >= u
    for i in range(heads):
        at = slice(i * 128, (i + 1) * 128)
        qr, kr, vr, gr = rq_ref[:, at], rk_ref[:, at], rv_ref[:, at], gr_ref[:, at]
        grad_b, state_b = matrix(SLICE * i), matrix(SLICE * (heads + i))
        gap = cum_t_ref[:, i : i + 1] - cum_ref[i : i + 1, :]
        decay = jnp.where(causal, jnp.exp(jnp.where(causal, gap, 0.0)), 0.0)
        from_start, to_end = from_ref[:, i : i + 1], to_ref[:, i : i + 1]
        one = (decay * dot_nt(gr, vr)).astype(BF)
        three = (decay * dot_nt(qr, kr)).astype(BF)
        q_ref[:, at] = dot_nn(one, kr) + from_start * dot_nt(gr, state_b)
        k_ref[:, at] = dot_tn(one, qr) + to_end * dot_nt(vr, grad_b)
        v_ref[:, at] = dot_tn(three, gr) + to_end * dot_nn(kr, grad_b)


def query_grad_kernel(heads, factor, own_ref, got_ref, out_ref):
    rows = out_ref.shape[1]
    total = ((own_ref[...] + got_ref[...].astype(F32)) * factor).astype(BF)
    for h in range(heads):
        out_ref[0, :, h * 128 : (h + 1) * 128] = total[h * rows : (h + 1) * rows]


def body(
    offsets,
    queries,
    output_grad,
    attention_out,
    cache_keys,
    cache_values,
    key_projection,
    value_projection,
    retention_query,
    retention_key,
    retention_value,
    retention_decay,
):
    core, chip = lax.axis_index("core"), lax.axis_index("zl")
    place = chip * CORES + core
    secs = CHIPS * CORES
    half = lax.axis_index("zh")
    shard = half * PLANE + lax.axis_index(PLANE_AXES)
    shards = HALVES * PLANE
    block_rows, head = cache_keys.shape
    _, query_rows, query_width = queries.shape
    heads = query_width // head
    flat = query_rows * heads
    width = 2 * flat
    lines = width // 128
    rows = block_rows // secs
    factor = 1.0 / math.sqrt(head)
    blocks = 32
    sizes = (blocks, rows, query_rows, block_rows, factor)
    where = jnp.stack([shard, chip, place, core]).astype(jnp.int32)

    kv_own = jnp.concatenate(
        [lax.dynamic_slice_in_dim(a, place * rows, rows, 0) for a in (cache_keys, cache_values)]
    )
    kv_other = lax.ppermute(kv_own, "zh", [(0, 1), (1, 0)])
    kv = jnp.where(
        half == 0,
        jnp.concatenate([kv_own, kv_other]),
        jnp.concatenate([kv_other, kv_own]),
    )
    kv = jnp.broadcast_to(kv[None], (PLANE,) + kv.shape)
    own = call(
        functools.partial(pack_kernel, heads),
        shape((2 * flat, head), BF), (), (queries, output_grad),
    )
    parts = [own] + [
        lax.ppermute(own, "zl", [(i, (i - k) % CHIPS) for i in range(CHIPS)])
        for k in range(1, CHIPS)
    ]
    delta = call(
        functools.partial(delta_kernel, heads),
        shape((32 - CHIPS * lines, head), F32), (where,), (output_grad, attention_out),
        scratch=[pltpu.VMEM((width, head), F32)],
    )

    local = retention_decay.shape[0]
    used = 2 * SLICE * local
    cum = jnp.cumsum(retention_decay, axis=1)
    cum_t = cum.T
    last = cum[:, -1]
    from_start = jnp.exp(cum_t)
    to_end = jnp.exp(last[None] - cum_t)
    high = last.astype(BF)
    rest = last - high.astype(F32)
    middle = rest.astype(BF)
    low = (rest - middle.astype(F32)).astype(BF)
    extra = jnp.concatenate([high, middle, low]).astype(F32)
    extra = jnp.pad(extra[None], ((0, WIRE - used - 1), (0, head - extra.shape[0])))

    env = (where, offsets, delta, cum, cum_t, from_start, to_end, extra)
    kv, parts[2], env = lax.optimization_barrier((kv, parts[2], env))
    mine = call(gather_kernel, shape((2, CHIPS, flat, head), BF), (where,), tuple(parts))
    kv = lax.all_to_all(kv, PLANE_AXES, 0, 0, tiled=True)
    kv, env = lax.optimization_barrier((kv, env))
    where, offsets, delta = env[:3]
    other = lax.ppermute(mine, "core", [(0, 1), (1, 0)])

    stats = [
        call(
            functools.partial(stats_kernel, *sizes),
            shape((CHIPS // 2 * lines, head), F32), (where, offsets), (part, kv),
            flops=4 << 30,
        )
        for part in (mine, other)
    ]
    own_stats, other_stats = stats
    both = jnp.concatenate([
        jnp.where(core == 0, own_stats, other_stats),
        jnp.where(core == 0, other_stats, own_stats),
        delta,
    ])
    both = jnp.broadcast_to(both[None], (secs,) + both.shape)
    both, (mine, other, kv, env) = pinned_exchange(both, ("zl", "core"), (mine, other, kv, env))
    where, offsets = env[:2]
    tiles = (CORES, CHIPS // 2, 1, width)
    logs = both[:, : CHIPS * lines]
    top = jnp.max(logs, axis=0)
    log_total = (top + jnp.log(jnp.sum(jnp.exp(logs - top), axis=0))).reshape(tiles)
    deltas = both[:, CHIPS * lines : (CHIPS + 1) * lines]
    deltas = deltas.reshape(CHIPS // 2, 2, CORES, lines, head)
    deltas = (deltas[:, 0] + deltas[:, 1]).transpose(1, 0, 2, 3).reshape(tiles)

    dkv, dq_own, dq_other = call(
        functools.partial(grads_kernel, *sizes),
        (shape(kv.shape, BF), shape((CHIPS, flat, head), F32), shape((CHIPS, flat, head), BF)),
        (where, offsets),
        (mine, other, kv, log_total, deltas),
        scratch=[pltpu.VMEM((CORES * CHIPS // 2, head, width), F32)],
        flops=4 << 30,
    )
    terms, env = pinned_exchange(dkv, PLANE_AXES, env)
    total = call(
        functools.partial(total_kernel, factor),
        shape((HALVES * secs, 2 * rows, head), BF), (), (terms,),
    )
    whole, env = pinned_exchange(total, ("zh", "zl", "core"), env)
    where, offsets, delta, cum, cum_t, from_start, to_end, extra = env

    cache_key_grad, cache_value_grad, out_grad, send = call(
        functools.partial(states_kernel, local),
        (
            shape((block_rows, head), BF), shape((block_rows, head), BF),
            shape(retention_query.shape, BF), shape((PLANE, WIRE, head), BF),
        ),
        (),
        (
            whole, key_projection, value_projection,
            retention_query, retention_key, retention_value, from_start, to_end, extra,
        ),
        scratch=[pltpu.VMEM((PLANE, WIRE, head), F32)],
        flops=1 << 27,
    )
    send, dq_own, dq_other = lax.optimization_barrier((send, dq_own, dq_other))
    dq_other = lax.ppermute(dq_other, "core", [(0, 1), (1, 0)])
    keep, away = call(
        chip_pairs_kernel, (shape((2, flat, head), F32), shape((2, flat, head), BF)),
        (where,), (dq_own, dq_other),
    )
    away = lax.ppermute(away, "zl", [(i, i ^ 2) for i in range(CHIPS)])
    part = lax.all_to_all(send, PLANE_AXES, 0, 0, tiled=True)
    part, keep, away, where = lax.optimization_barrier((part, keep, away, where))
    lasts = part[:, used, : 3 * local].astype(F32).reshape(PLANE, 3, local)
    decays = jnp.exp(lasts[:, 0] + lasts[:, 1] + lasts[:, 2])
    decays = jnp.concatenate([decays, decays], axis=1)
    decays = jnp.broadcast_to(decays[:, :, None], (PLANE, 2 * local, SLICE))
    decays = decays.reshape(PLANE, used, 1)
    decays = jnp.pad(decays, ((0, 0), (0, WIRE - used), (0, 0)))
    decays = jnp.broadcast_to(decays, (PLANE, WIRE, head))
    totals = call(
        functools.partial(totals_kernel, local),
        shape((WIRE, head), F32), (), (part, decays),
    )
    totals = lax.ppermute(totals, "zh", [(0, 1), (1, 0)])
    enter = call(
        functools.partial(scan_kernel, local),
        shape(part.shape, BF), (where,), (part, decays, totals),
        scratch=[pltpu.VMEM(part.shape, F32)] * 2,
    )
    enter, keep, away = lax.optimization_barrier((enter, keep, away))
    dq_mine, piece = call(
        chips_kernel, (shape((flat, head), F32), shape((flat, head), BF)), (where,), (keep, away),
    )
    piece = lax.ppermute(piece, "zl", [(i, i ^ 1) for i in range(CHIPS)])
    enter = lax.all_to_all(enter, PLANE_AXES, 0, 0, tiled=True)
    cross_query_grad = call(
        functools.partial(query_grad_kernel, heads, factor),
        shape(queries.shape, BF), (), (dq_mine, piece),
    )
    grads = call(
        functools.partial(final_kernel, local),
        (shape(retention_query.shape, F32),) * 3,
        (),
        (
            retention_query, retention_key, retention_value, out_grad, cum, cum_t,
            from_start, to_end, enter,
        ),
        scratch=[pltpu.VMEM(enter.shape, F32)],
        flops=1 << 28,
    )
    return (cross_query_grad, cache_key_grad, cache_value_grad) + tuple(grads)


def solution(mesh):
    sec, ctx = ("zl", "core"), ("zh", "x", "y")
    split = Mesh(mesh.devices.reshape(CHIPS, CORES, HALVES, 4, 8), sec + ctx)
    in_specs = (
        P(),
        P(sec, ctx, None),
        P(sec, ctx, None),
        P(sec, ctx, None),
        P(ctx, None),
        P(ctx, None),
        P(sec, None),
        P(sec, None),
        P(ctx, sec),
        P(ctx, sec),
        P(ctx, sec),
        P(sec, ctx),
    )
    out_specs = (
        P(sec, ctx, None),
        P(ctx, None),
        P(ctx, None),
        P(ctx, sec),
        P(ctx, sec),
        P(ctx, sec),
    )
    return jax.shard_map(body, mesh=split, in_specs=in_specs, out_specs=out_specs, check_vma=False)
```

```python
import functools
import math

import jax
import jax.numpy as jnp
from jax import lax
from jax.experimental import pallas as pl
from jax.experimental.pallas import tpu as pltpu
from jax.sharding import Mesh
from jax.sharding import PartitionSpec as P

BF = jnp.bfloat16
F32 = jnp.float32
LOW = -1e30
LOG2E = math.log2(math.e)
CHIPS, CORES = 4, 2
HALVES, PLANE = 2, 32
PLANE_AXES = ("x", "y")
SLICE = 4
WIRE = 48
SCOPED = 16 * 1024 * 1024


def dot_nt(a, b):
    return lax.dot_general(a, b, (((1,), (1,)), ((), ())), preferred_element_type=F32)


def dot_nn(a, b):
    return lax.dot_general(a, b, (((1,), (0,)), ((), ())), preferred_element_type=F32)


def dot_tn(a, b):
    return lax.dot_general(a, b, (((0,), (0,)), ((), ())), preferred_element_type=F32)


def call(kernel, outs, in_smem, ins, scratch=(), flops=0):
    vmem = pl.BlockSpec(memory_space=pltpu.VMEM)
    smem = pl.BlockSpec(memory_space=pltpu.SMEM)
    return pl.pallas_call(
        kernel,
        out_shape=outs,
        in_specs=[smem] * len(in_smem) + [vmem] * len(ins),
        out_specs=jax.tree.map(lambda _: vmem, outs),
        scratch_shapes=list(scratch),
        compiler_params=pltpu.CompilerParams(vmem_limit_bytes=SCOPED),
        cost_estimate=pl.CostEstimate(flops=flops, bytes_accessed=1 << 20, transcendentals=0),
    )(*in_smem, *ins)


def shape(dims, dtype):
    return jax.ShapeDtypeStruct(dims, dtype)


def pinned_exchange(array, axes, later):
    array, later = lax.optimization_barrier((array, later))
    array = lax.all_to_all(array, axes, 0, 0, tiled=True)
    return lax.optimization_barrier((array, later))


def pack_kernel(heads, q_ref, g_ref, out_ref):
    rows = q_ref.shape[1]
    for h in range(heads):
        at = slice(h * 128, (h + 1) * 128)
        out_ref[h * rows : (h + 1) * rows, :] = q_ref[0, :, at]
        out_ref[(heads + h) * rows : (heads + h + 1) * rows, :] = g_ref[0, :, at]


def delta_kernel(heads, where_ref, g_ref, o_ref, out_ref, product):
    rows = g_ref.shape[1]
    base = lax.rem(where_ref[1], 2) * (heads * rows)
    product[...] = jnp.zeros_like(product)
    for h in range(heads):
        at = slice(h * 128, (h + 1) * 128)
        to = pl.ds(pl.multiple_of(base + h * rows, rows), rows)
        product[to, :] = g_ref[0, :, at].astype(F32) * o_ref[0, :, at].astype(F32)
    sums = jnp.sum(product[...].T, axis=0, keepdims=True)
    out_ref[...] = jnp.zeros_like(out_ref)
    for n in range(sums.shape[1] // 128):
        out_ref[n : n + 1, :] = sums[:, n * 128 : (n + 1) * 128]


def gather_kernel(where_ref, a_ref, b_ref, c_ref, d_ref, out_ref):
    flat = out_ref.shape[2]
    for k, ref in enumerate((a_ref, b_ref, c_ref, d_ref)):
        chip = lax.rem(where_ref[1] + k, CHIPS)
        out_ref[0, chip] = ref[0:flat]
        out_ref[1, chip] = ref[flat:]


def row_positions(where_ref, offset_ref, width, rows, block_rows):
    lane = lax.broadcasted_iota(jnp.int32, (1, width), 1)
    shard = where_ref[0]
    return lax.rem(lane, rows) + (shard * block_rows + offset_ref[shard])


def key_positions(place, chunk, blocks, rows, block_rows):
    at = lax.broadcasted_iota(jnp.int32, (blocks * rows, 1), 0)
    return (chunk * blocks + at // rows) * block_rows + place * rows + at % rows


def cache_place(kv_ref, chunk, blocks, rows):
    per = kv_ref.shape[0] // blocks
    line = pl.multiple_of((chunk // per) * (2 * rows), 2 * rows)
    return pl.ds(pl.multiple_of(lax.rem(chunk, per) * blocks, blocks), blocks), line


def cache_slice(kv_ref, chunk, blocks, rows, values):
    at, line = cache_place(kv_ref, chunk, blocks, rows)
    line = pl.multiple_of(line + values * rows, rows)
    return kv_ref[at, pl.ds(line, rows), :].reshape(blocks * rows, -1)


def tile(refs, which, n, t):
    return refs[n][which, 2 * t : 2 * t + 2].reshape(2 * refs[n].shape[2], -1)


def stats_kernel(
    blocks, rows, query_rows, block_rows, factor, where_ref, offset_ref, rows_ref, kv_ref, out_ref,
):
    shard, place = where_ref[0], where_ref[2]
    width = 2 * rows_ref.shape[2]
    lines = width // 128
    full = shard // blocks
    pos = row_positions(where_ref, offset_ref, width, query_rows, block_rows)
    scale = factor * LOG2E
    tiles = range(CHIPS // 2)

    def chunk(j, carry, masked=False):
        keys = cache_slice(kv_ref, j, blocks, rows, 0)
        if masked:
            seen = key_positions(place, j, blocks, rows, block_rows) <= pos
        out = []
        for t, (top, total) in zip(tiles, carry):
            s = dot_nt(keys, tile((rows_ref,), 0, 0, t))
            if masked:
                s = jnp.where(seen, s, LOW)
            new = jnp.maximum(top, jnp.max(s, axis=0, keepdims=True))
            p = jnp.exp2((s - new) * scale)
            if masked:
                p = jnp.where(seen, p, 0.0)
            total = total * jnp.exp2((top - new) * scale) + jnp.sum(p, axis=0, keepdims=True)
            out.append((new, total))
        return tuple(out)

    start = ((jnp.full((1, width), LOW, F32), jnp.zeros((1, width), F32)),) * len(tiles)
    done = chunk(full, lax.fori_loop(0, full, chunk, start), masked=True)
    for t, (top, total) in zip(tiles, done):
        lse = jnp.where(total > 0.0, top * factor + jnp.log(total), LOW)
        for m in range(lines):
            out_ref[t * lines + m : t * lines + m + 1, :] = lse[:, m * 128 : (m + 1) * 128]


def grads_kernel(
    blocks, rows, query_rows, block_rows, factor,
    where_ref, offset_ref, mine_ref, other_ref, kv_ref, log_ref, delta_ref,
    dkv_ref, dq_own_ref, dq_other_ref, dq_total,
):
    shard, place, core = where_ref[0], where_ref[2], where_ref[3]
    flat = mine_ref.shape[2]
    width = 2 * flat
    size = blocks * rows
    full = shard // blocks
    pos = row_positions(where_ref, offset_ref, width, query_rows, block_rows)
    scale = factor * LOG2E
    tiles = [(n, t) for n in range(CORES) for t in range(CHIPS // 2)]
    dq_total[...] = jnp.zeros_like(dq_total)

    def chunk(j, masked=False):
        keys = cache_slice(kv_ref, j, blocks, rows, 0)
        values = cache_slice(kv_ref, j, blocks, rows, 1)
        if masked:
            seen = key_positions(place, j, blocks, rows, block_rows) <= pos
        dk = dv = 0.0
        for i, (n, t) in enumerate(tiles):
            q = tile((mine_ref, other_ref), 0, n, t)
            g = tile((mine_ref, other_ref), 1, n, t)
            at_core = lax.rem(core + n, CORES)
            p = jnp.exp2(dot_nt(keys, q) * scale - log_ref[at_core, t] * LOG2E)
            if masked:
                p = jnp.where(seen, p, 0.0)
            ds = (p * (dot_nt(values, g) - delta_ref[at_core, t])).astype(BF)
            dk = dk + dot_nn(ds, q)
            dv = dv + dot_nn(p.astype(BF), g)
            dq_total[i] += dot_tn(keys, ds)
        at, line = cache_place(kv_ref, j, blocks, rows)
        dkv_ref[at, pl.ds(line, rows), :] = dk.astype(BF).reshape(blocks, rows, -1)
        dkv_ref[at, pl.ds(line + rows, rows), :] = dv.astype(BF).reshape(blocks, rows, -1)

    def step(j, _):
        chunk(j)
        return 0

    lax.fori_loop(0, full, step, 0)
    chunk(full, masked=True)

    def clear(j, _):
        at, line = cache_place(kv_ref, j, blocks, rows)
        dkv_ref[at, pl.ds(line, 2 * rows), :] = jnp.zeros((blocks, 2 * rows, kv_ref.shape[-1]), BF)
        return 0

    lax.fori_loop(full + 1, HALVES * kv_ref.shape[0] // blocks, clear, 0)
    for i, (n, t) in enumerate(tiles):
        dq = dq_total[i].T
        dq_ref = (dq_own_ref, dq_other_ref)[n]
        for m in range(2):
            dq_ref[2 * t + m] = dq[m * flat : (m + 1) * flat].astype(dq_ref.dtype)


def chip_pairs_kernel(where_ref, own_ref, other_ref, keep_ref, send_ref):
    pair = where_ref[1] // 2
    for m in range(2):
        to = 2 * pair + m
        keep_ref[m] = own_ref[to] + other_ref[to].astype(F32)
        to = 2 * (1 - pair) + m
        send_ref[m] = (own_ref[to] + other_ref[to].astype(F32)).astype(BF)


def chips_kernel(where_ref, keep_ref, got_ref, own_ref, send_ref):
    own = lax.rem(where_ref[1], 2)
    own_ref[...] = keep_ref[own] + got_ref[own].astype(F32)
    send_ref[...] = (keep_ref[1 - own] + got_ref[1 - own].astype(F32)).astype(BF)


def total_kernel(factor, terms_ref, out_ref):
    total = jnp.sum(terms_ref[...].astype(F32), axis=0)
    lines = out_ref.shape[1]
    row = lax.broadcasted_iota(jnp.int32, (lines, 1), 0)
    scale = jnp.where(row < lines // 2, factor, 1.0)
    count = out_ref.shape[0] // HALVES
    for n in range(HALVES):
        part = (total[n * lines : (n + 1) * lines] * scale).astype(BF)
        out_ref[n * count : (n + 1) * count] = jnp.broadcast_to(part[None], (count,) + part.shape)


def states_kernel(
    heads, whole_ref, kp_ref, vp_ref, rq_ref, rk_ref, rv_ref, from_ref, to_ref, extra_ref,
    ck_ref, cv_ref, gr_ref, send_ref, wire,
):
    count = whole_ref.shape[0] // HALVES
    rows = whole_ref.shape[1] // 2
    both = (whole_ref[0:count].astype(F32) + whole_ref[count:].astype(F32)).astype(BF)
    ck = both[:, 0:rows, :].reshape(count * rows, -1)
    cv = both[:, rows:, :].reshape(count * rows, -1)
    ck_ref[...] = ck
    cv_ref[...] = cv
    plane = send_ref.shape[0]
    used = 2 * SLICE * heads
    wire[:, used:, :] = jnp.broadcast_to(extra_ref[...][None], (plane,) + extra_ref.shape)
    for i in range(heads):
        at = slice(i * 128, (i + 1) * 128)
        gr = (dot_nt(ck, kp_ref[at, :]) + dot_nt(cv, vp_ref[at, :])).astype(BF)
        gr_ref[:, at] = gr
        query_w = (rq_ref[:, at].astype(F32) * from_ref[:, i : i + 1]).astype(BF)
        key_w = (rk_ref[:, at].astype(F32) * to_ref[:, i : i + 1]).astype(BF)
        grad = dot_tn(query_w, gr)
        state = dot_tn(key_w, rv_ref[:, at])
        for k in range(SLICE):
            part = slice(k * plane, (k + 1) * plane)
            wire[:, SLICE * i + k, :] = grad[part]
            wire[:, SLICE * (heads + i) + k, :] = state[part]
    send_ref[...] = wire[...].astype(BF)


def totals_kernel(heads, part_ref, decay_ref, out_ref):
    count = part_ref.shape[0]
    zero = jnp.zeros(part_ref.shape[1:], F32)

    def step(b, carry):
        fore, back = carry
        fore = decay_ref[b] * fore + part_ref[b].astype(F32)
        r = count - 1 - b
        back = decay_ref[r] * back + part_ref[r].astype(F32)
        return fore, back

    fore, back = lax.fori_loop(0, count, step, (zero, zero), unroll=4)
    row = lax.broadcasted_iota(jnp.int32, zero.shape, 0)
    out_ref[...] = jnp.where(row < SLICE * heads, back, fore)


def scan_kernel(heads, where_ref, part_ref, decay_ref, other_ref, out_ref, ahead, behind):
    count = part_ref.shape[0]
    upper = where_ref[0] >= count
    other = other_ref[...]
    zero = jnp.zeros_like(other)

    def step(b, carry):
        fore, back = carry
        ahead[b] = fore
        fore = decay_ref[b] * fore + part_ref[b].astype(F32)
        r = count - 1 - b
        behind[r] = back
        back = decay_ref[r] * back + part_ref[r].astype(F32)
        return fore, back

    start = (jnp.where(upper, other, zero), jnp.where(upper, zero, other))
    lax.fori_loop(0, count, step, start, unroll=4)
    row = lax.broadcasted_iota(jnp.int32, part_ref.shape, 1)
    out_ref[...] = jnp.where(row < SLICE * heads, behind[...], ahead[...]).astype(BF)


def final_kernel(
    heads, rq_ref, rk_ref, rv_ref, gr_ref, cum_ref, cum_t_ref, from_ref, to_ref, wire_ref,
    q_ref, k_ref, v_ref, wire,
):
    wire[...] = wire_ref[...].astype(F32)

    def matrix(r):
        return jnp.concatenate([wire[:, r + k, :] for k in range(SLICE)], axis=0).astype(BF)

    size = rq_ref.shape[0]
    t = lax.broadcasted_iota(jnp.int32, (size, size), 0)
    u = lax.broadcasted_iota(jnp.int32, (size, size), 1)
    causal = t >= u
    for i in range(heads):
        at = slice(i * 128, (i + 1) * 128)
        qr, kr, vr, gr = rq_ref[:, at], rk_ref[:, at], rv_ref[:, at], gr_ref[:, at]
        grad_b, state_b = matrix(SLICE * i), matrix(SLICE * (heads + i))
        gap = cum_t_ref[:, i : i + 1] - cum_ref[i : i + 1, :]
        decay = jnp.where(causal, jnp.exp(jnp.where(causal, gap, 0.0)), 0.0)
        from_start, to_end = from_ref[:, i : i + 1], to_ref[:, i : i + 1]
        one = (decay * dot_nt(gr, vr)).astype(BF)
        three = (decay * dot_nt(qr, kr)).astype(BF)
        q_ref[:, at] = dot_nn(one, kr) + from_start * dot_nt(gr, state_b)
        k_ref[:, at] = dot_tn(one, qr) + to_end * dot_nt(vr, grad_b)
        v_ref[:, at] = dot_tn(three, gr) + to_end * dot_nn(kr, grad_b)


def query_grad_kernel(heads, factor, own_ref, got_ref, out_ref):
    rows = out_ref.shape[1]
    total = ((own_ref[...] + got_ref[...].astype(F32)) * factor).astype(BF)
    for h in range(heads):
        out_ref[0, :, h * 128 : (h + 1) * 128] = total[h * rows : (h + 1) * rows]


def body(
    offsets,
    queries,
    output_grad,
    attention_out,
    cache_keys,
    cache_values,
    key_projection,
    value_projection,
    retention_query,
    retention_key,
    retention_value,
    retention_decay,
):
    core, chip = lax.axis_index("core"), lax.axis_index("zl")
    place = chip * CORES + core
    secs = CHIPS * CORES
    half = lax.axis_index("zh")
    shard = half * PLANE + lax.axis_index(PLANE_AXES)
    shards = HALVES * PLANE
    block_rows, head = cache_keys.shape
    _, query_rows, query_width = queries.shape
    heads = query_width // head
    flat = query_rows * heads
    width = 2 * flat
    lines = width // 128
    rows = block_rows // secs
    factor = 1.0 / math.sqrt(head)
    blocks = 32
    sizes = (blocks, rows, query_rows, block_rows, factor)
    where = jnp.stack([shard, chip, place, core]).astype(jnp.int32)

    kv_own = jnp.concatenate(
        [lax.dynamic_slice_in_dim(a, place * rows, rows, 0) for a in (cache_keys, cache_values)]
    )
    kv_own, queries, output_grad = lax.optimization_barrier((kv_own, queries, output_grad))
    kv_other = lax.ppermute(kv_own, "zh", [(0, 1), (1, 0)])
    kv = jnp.where(
        half == 0,
        jnp.concatenate([kv_own, kv_other]),
        jnp.concatenate([kv_other, kv_own]),
    )
    kv = jnp.broadcast_to(kv[None], (PLANE,) + kv.shape)
    own = call(
        functools.partial(pack_kernel, heads),
        shape((2 * flat, head), BF), (), (queries, output_grad),
    )
    parts = [own] + [
        lax.ppermute(own, "zl", [(i, (i - k) % CHIPS) for i in range(CHIPS)])
        for k in range(1, CHIPS)
    ]
    delta = call(
        functools.partial(delta_kernel, heads),
        shape((32 - CHIPS * lines, head), F32), (where,), (output_grad, attention_out),
        scratch=[pltpu.VMEM((width, head), F32)],
    )

    local = retention_decay.shape[0]
    used = 2 * SLICE * local
    cum = jnp.cumsum(retention_decay, axis=1)
    cum_t = cum.T
    last = cum[:, -1]
    from_start = jnp.exp(cum_t)
    to_end = jnp.exp(last[None] - cum_t)
    high = last.astype(BF)
    rest = last - high.astype(F32)
    middle = rest.astype(BF)
    low = (rest - middle.astype(F32)).astype(BF)
    extra = jnp.concatenate([high, middle, low]).astype(F32)
    extra = jnp.pad(extra[None], ((0, WIRE - used - 1), (0, head - extra.shape[0])))

    env = (where, offsets, delta, cum, cum_t, from_start, to_end, extra)
    mine = call(
        gather_kernel, shape((2, CHIPS, flat, head), BF), (where,), tuple(parts), flops=16 << 30
    )
    kv, env = lax.optimization_barrier((kv, env))
    kv = lax.all_to_all(kv, PLANE_AXES, 0, 0, tiled=True)
    kv, env = lax.optimization_barrier((kv, env))
    where, offsets, delta = env[:3]
    other = lax.ppermute(mine, "core", [(0, 1), (1, 0)])

    stats = [
        call(
            functools.partial(stats_kernel, *sizes),
            shape((CHIPS // 2 * lines, head), F32), (where, offsets), (part, kv),
            flops=4 << 30,
        )
        for part in (mine, other)
    ]
    own_stats, other_stats = stats
    both = jnp.concatenate([
        jnp.where(core == 0, own_stats, other_stats),
        jnp.where(core == 0, other_stats, own_stats),
        delta,
    ])
    both = jnp.broadcast_to(both[None], (secs,) + both.shape)
    both, env = pinned_exchange(both, ("zl", "core"), env)
    where, offsets = env[:2]
    tiles = (CORES, CHIPS // 2, 1, width)
    logs = both[:, : CHIPS * lines]
    top = jnp.max(logs, axis=0)
    log_total = (top + jnp.log(jnp.sum(jnp.exp(logs - top), axis=0))).reshape(tiles)
    deltas = both[:, CHIPS * lines : (CHIPS + 1) * lines]
    deltas = deltas.reshape(CHIPS // 2, 2, CORES, lines, head)
    deltas = (deltas[:, 0] + deltas[:, 1]).transpose(1, 0, 2, 3).reshape(tiles)

    dkv, dq_own, dq_other = call(
        functools.partial(grads_kernel, *sizes),
        (shape(kv.shape, BF), shape((CHIPS, flat, head), F32), shape((CHIPS, flat, head), BF)),
        (where, offsets),
        (mine, other, kv, log_total, deltas),
        scratch=[pltpu.VMEM((CORES * CHIPS // 2, head, width), F32)],
        flops=4 << 30,
    )
    terms, env = pinned_exchange(dkv, PLANE_AXES, env)
    total = call(
        functools.partial(total_kernel, factor),
        shape((HALVES * secs, 2 * rows, head), BF), (), (terms,),
    )
    whole, env = pinned_exchange(total, ("zh", "zl", "core"), env)
    where, offsets, delta, cum, cum_t, from_start, to_end, extra = env

    cache_key_grad, cache_value_grad, out_grad, send = call(
        functools.partial(states_kernel, local),
        (
            shape((block_rows, head), BF), shape((block_rows, head), BF),
            shape(retention_query.shape, BF), shape((PLANE, WIRE, head), BF),
        ),
        (),
        (
            whole, key_projection, value_projection,
            retention_query, retention_key, retention_value, from_start, to_end, extra,
        ),
        scratch=[pltpu.VMEM((PLANE, WIRE, head), F32)],
        flops=1 << 27,
    )
    send, dq_own, dq_other = lax.optimization_barrier((send, dq_own, dq_other))
    dq_other = lax.ppermute(dq_other, "core", [(0, 1), (1, 0)])
    keep, away = call(
        chip_pairs_kernel, (shape((2, flat, head), F32), shape((2, flat, head), BF)),
        (where,), (dq_own, dq_other),
    )
    away = lax.ppermute(away, "zl", [(i, i ^ 2) for i in range(CHIPS)])
    part = lax.all_to_all(send, PLANE_AXES, 0, 0, tiled=True)
    part, where = lax.optimization_barrier((part, where))
    lasts = part[:, used, : 3 * local].astype(F32).reshape(PLANE, 3, local)
    decays = jnp.exp(lasts[:, 0] + lasts[:, 1] + lasts[:, 2])
    decays = jnp.concatenate([decays, decays], axis=1)
    decays = jnp.broadcast_to(decays[:, :, None], (PLANE, 2 * local, SLICE))
    decays = decays.reshape(PLANE, used, 1)
    decays = jnp.pad(decays, ((0, 0), (0, WIRE - used), (0, 0)))
    decays = jnp.broadcast_to(decays, (PLANE, WIRE, head))
    totals = call(
        functools.partial(totals_kernel, local),
        shape((WIRE, head), F32), (), (part, decays),
    )
    totals = lax.ppermute(totals, "zh", [(0, 1), (1, 0)])
    enter = call(
        functools.partial(scan_kernel, local),
        shape(part.shape, BF), (where,), (part, decays, totals),
        scratch=[pltpu.VMEM(part.shape, F32)] * 2,
    )
    enter, keep, away = lax.optimization_barrier((enter, keep, away))
    dq_mine, piece = call(
        chips_kernel, (shape((flat, head), F32), shape((flat, head), BF)), (where,), (keep, away),
    )
    piece = lax.ppermute(piece, "zl", [(i, i ^ 1) for i in range(CHIPS)])
    enter = lax.all_to_all(enter, PLANE_AXES, 0, 0, tiled=True)
    grads = call(
        functools.partial(final_kernel, local),
        (shape(retention_query.shape, F32),) * 3,
        (),
        (
            retention_query, retention_key, retention_value, out_grad, cum, cum_t,
            from_start, to_end, enter,
        ),
        scratch=[pltpu.VMEM(enter.shape, F32)],
        flops=1 << 28,
    )
    grads, dq_mine, piece = lax.optimization_barrier((grads, dq_mine, piece))
    cross_query_grad = call(
        functools.partial(query_grad_kernel, heads, factor),
        shape(queries.shape, BF), (), (dq_mine, piece),
    )
    return (cross_query_grad, cache_key_grad, cache_value_grad) + tuple(grads)


def solution(mesh):
    sec, ctx = ("zl", "core"), ("zh", "x", "y")
    split = Mesh(mesh.devices.reshape(CHIPS, CORES, HALVES, 4, 8), sec + ctx)
    in_specs = (
        P(),
        P(sec, ctx, None),
        P(sec, ctx, None),
        P(sec, ctx, None),
        P(ctx, None),
        P(ctx, None),
        P(sec, None),
        P(sec, None),
        P(ctx, sec),
        P(ctx, sec),
        P(ctx, sec),
        P(sec, ctx),
    )
    out_specs = (
        P(sec, ctx, None),
        P(ctx, None),
        P(ctx, None),
        P(ctx, sec),
        P(ctx, sec),
        P(ctx, sec),
    )
    return jax.shard_map(body, mesh=split, in_specs=in_specs, out_specs=out_specs, check_vma=False)
```

```python
import functools
import math

import jax
import jax.numpy as jnp
from jax import lax
from jax.experimental import pallas as pl
from jax.experimental.pallas import tpu as pltpu
from jax.sharding import Mesh
from jax.sharding import PartitionSpec as P

BF = jnp.bfloat16
F32 = jnp.float32
LOW = -1e30
LOG2E = math.log2(math.e)
CHIPS, CORES = 4, 2
HALVES, PLANE = 2, 32
PLANE_AXES = ("x", "y")
SLICE = 4
WIRE = 48
SCOPED = 16 * 1024 * 1024


def dot_nt(a, b):
    return lax.dot_general(a, b, (((1,), (1,)), ((), ())), preferred_element_type=F32)


def dot_nn(a, b):
    return lax.dot_general(a, b, (((1,), (0,)), ((), ())), preferred_element_type=F32)


def dot_tn(a, b):
    return lax.dot_general(a, b, (((0,), (0,)), ((), ())), preferred_element_type=F32)


def call(kernel, outs, in_smem, ins, scratch=(), flops=0):
    vmem = pl.BlockSpec(memory_space=pltpu.VMEM)
    smem = pl.BlockSpec(memory_space=pltpu.SMEM)
    return pl.pallas_call(
        kernel,
        out_shape=outs,
        in_specs=[smem] * len(in_smem) + [vmem] * len(ins),
        out_specs=jax.tree.map(lambda _: vmem, outs),
        scratch_shapes=list(scratch),
        compiler_params=pltpu.CompilerParams(vmem_limit_bytes=SCOPED),
        cost_estimate=pl.CostEstimate(flops=flops, bytes_accessed=1 << 20, transcendentals=0),
    )(*in_smem, *ins)


def shape(dims, dtype):
    return jax.ShapeDtypeStruct(dims, dtype)


def pinned_exchange(array, axes, later):
    array, later = lax.optimization_barrier((array, later))
    array = lax.all_to_all(array, axes, 0, 0, tiled=True)
    return lax.optimization_barrier((array, later))


def pack_kernel(heads, q_ref, g_ref, out_ref):
    rows = q_ref.shape[1]
    for h in range(heads):
        at = slice(h * 128, (h + 1) * 128)
        out_ref[h * rows : (h + 1) * rows, :] = q_ref[0, :, at]
        out_ref[(heads + h) * rows : (heads + h + 1) * rows, :] = g_ref[0, :, at]


def delta_kernel(heads, where_ref, g_ref, o_ref, out_ref, product):
    rows = g_ref.shape[1]
    base = lax.rem(where_ref[1], 2) * (heads * rows)
    product[...] = jnp.zeros_like(product)
    for h in range(heads):
        at = slice(h * 128, (h + 1) * 128)
        to = pl.ds(pl.multiple_of(base + h * rows, rows), rows)
        product[to, :] = g_ref[0, :, at].astype(F32) * o_ref[0, :, at].astype(F32)
    sums = jnp.sum(product[...].T, axis=0, keepdims=True)
    out_ref[...] = jnp.zeros_like(out_ref)
    for n in range(sums.shape[1] // 128):
        out_ref[n : n + 1, :] = sums[:, n * 128 : (n + 1) * 128]


def gather_kernel(where_ref, a_ref, b_ref, c_ref, d_ref, out_ref):
    flat = out_ref.shape[2]
    for k, ref in enumerate((a_ref, b_ref, c_ref, d_ref)):
        chip = lax.rem(where_ref[1] + k, CHIPS)
        out_ref[0, chip] = ref[0:flat]
        out_ref[1, chip] = ref[flat:]


def row_positions(where_ref, offset_ref, width, rows, block_rows):
    lane = lax.broadcasted_iota(jnp.int32, (1, width), 1)
    shard = where_ref[0]
    return lax.rem(lane, rows) + (shard * block_rows + offset_ref[shard])


def key_positions(place, chunk, blocks, rows, block_rows):
    at = lax.broadcasted_iota(jnp.int32, (blocks * rows, 1), 0)
    return (chunk * blocks + at // rows) * block_rows + place * rows + at % rows


def cache_place(kv_ref, chunk, blocks, rows):
    per = kv_ref.shape[0] // blocks
    line = pl.multiple_of((chunk // per) * (2 * rows), 2 * rows)
    return pl.ds(pl.multiple_of(lax.rem(chunk, per) * blocks, blocks), blocks), line


def cache_slice(kv_ref, chunk, blocks, rows, values):
    at, line = cache_place(kv_ref, chunk, blocks, rows)
    line = pl.multiple_of(line + values * rows, rows)
    return kv_ref[at, pl.ds(line, rows), :].reshape(blocks * rows, -1)


def tile(refs, which, n, t):
    return refs[n][which, 2 * t : 2 * t + 2].reshape(2 * refs[n].shape[2], -1)


def stats_kernel(
    blocks, rows, query_rows, block_rows, factor, where_ref, offset_ref, rows_ref, kv_ref, out_ref,
):
    shard, place = where_ref[0], where_ref[2]
    width = 2 * rows_ref.shape[2]
    lines = width // 128
    full = shard // blocks
    pos = row_positions(where_ref, offset_ref, width, query_rows, block_rows)
    scale = factor * LOG2E
    tiles = range(CHIPS // 2)

    def chunk(j, carry, masked=False):
        keys = cache_slice(kv_ref, j, blocks, rows, 0)
        if masked:
            seen = key_positions(place, j, blocks, rows, block_rows) <= pos
        out = []
        for t, (top, total) in zip(tiles, carry):
            s = dot_nt(keys, tile((rows_ref,), 0, 0, t))
            if masked:
                s = jnp.where(seen, s, LOW)
            new = jnp.maximum(top, jnp.max(s, axis=0, keepdims=True))
            p = jnp.exp2((s - new) * scale)
            if masked:
                p = jnp.where(seen, p, 0.0)
            total = total * jnp.exp2((top - new) * scale) + jnp.sum(p, axis=0, keepdims=True)
            out.append((new, total))
        return tuple(out)

    start = ((jnp.full((1, width), LOW, F32), jnp.zeros((1, width), F32)),) * len(tiles)
    done = chunk(full, lax.fori_loop(0, full, chunk, start), masked=True)
    for t, (top, total) in zip(tiles, done):
        lse = jnp.where(total > 0.0, top * factor + jnp.log(total), LOW)
        for m in range(lines):
            out_ref[t * lines + m : t * lines + m + 1, :] = lse[:, m * 128 : (m + 1) * 128]


def grads_kernel(
    blocks, rows, query_rows, block_rows, factor,
    where_ref, offset_ref, mine_ref, other_ref, kv_ref, log_ref, delta_ref,
    dkv_ref, dq_own_ref, dq_other_ref, dq_total,
):
    shard, place, core = where_ref[0], where_ref[2], where_ref[3]
    flat = mine_ref.shape[2]
    width = 2 * flat
    size = blocks * rows
    full = shard // blocks
    pos = row_positions(where_ref, offset_ref, width, query_rows, block_rows)
    scale = factor * LOG2E
    tiles = [(n, t) for n in range(CORES) for t in range(CHIPS // 2)]
    dq_total[...] = jnp.zeros_like(dq_total)

    def chunk(j, masked=False):
        keys = cache_slice(kv_ref, j, blocks, rows, 0)
        values = cache_slice(kv_ref, j, blocks, rows, 1)
        if masked:
            seen = key_positions(place, j, blocks, rows, block_rows) <= pos
        dk = dv = 0.0
        for i, (n, t) in enumerate(tiles):
            q = tile((mine_ref, other_ref), 0, n, t)
            g = tile((mine_ref, other_ref), 1, n, t)
            at_core = lax.rem(core + n, CORES)
            p = jnp.exp2(dot_nt(keys, q) * scale - log_ref[at_core, t] * LOG2E)
            if masked:
                p = jnp.where(seen, p, 0.0)
            ds = (p * (dot_nt(values, g) - delta_ref[at_core, t])).astype(BF)
            dk = dk + dot_nn(ds, q)
            dv = dv + dot_nn(p.astype(BF), g)
            dq_total[i] += dot_tn(keys, ds)
        at, line = cache_place(kv_ref, j, blocks, rows)
        dkv_ref[at, pl.ds(line, rows), :] = dk.astype(BF).reshape(blocks, rows, -1)
        dkv_ref[at, pl.ds(line + rows, rows), :] = dv.astype(BF).reshape(blocks, rows, -1)

    def step(j, _):
        chunk(j)
        return 0

    lax.fori_loop(0, full, step, 0)
    chunk(full, masked=True)

    def clear(j, _):
        at, line = cache_place(kv_ref, j, blocks, rows)
        dkv_ref[at, pl.ds(line, 2 * rows), :] = jnp.zeros((blocks, 2 * rows, kv_ref.shape[-1]), BF)
        return 0

    lax.fori_loop(full + 1, HALVES * kv_ref.shape[0] // blocks, clear, 0)
    for i, (n, t) in enumerate(tiles):
        dq = dq_total[i].T
        dq_ref = (dq_own_ref, dq_other_ref)[n]
        for m in range(2):
            dq_ref[2 * t + m] = dq[m * flat : (m + 1) * flat].astype(dq_ref.dtype)


def chip_pairs_kernel(where_ref, own_ref, other_ref, keep_ref, send_ref):
    pair = where_ref[1] // 2
    for m in range(2):
        to = 2 * pair + m
        keep_ref[m] = own_ref[to] + other_ref[to].astype(F32)
        to = 2 * (1 - pair) + m
        send_ref[m] = (own_ref[to] + other_ref[to].astype(F32)).astype(BF)


def chips_kernel(where_ref, keep_ref, got_ref, own_ref, send_ref):
    own = lax.rem(where_ref[1], 2)
    own_ref[...] = keep_ref[own] + got_ref[own].astype(F32)
    send_ref[...] = (keep_ref[1 - own] + got_ref[1 - own].astype(F32)).astype(BF)


def total_kernel(factor, terms_ref, out_ref):
    total = jnp.sum(terms_ref[...].astype(F32), axis=0)
    lines = out_ref.shape[1]
    row = lax.broadcasted_iota(jnp.int32, (lines, 1), 0)
    scale = jnp.where(row < lines // 2, factor, 1.0)
    count = out_ref.shape[0] // HALVES
    for n in range(HALVES):
        part = (total[n * lines : (n + 1) * lines] * scale).astype(BF)
        out_ref[n * count : (n + 1) * count] = jnp.broadcast_to(part[None], (count,) + part.shape)


def early_kernel(heads, rk_ref, rv_ref, to_ref, extra_ref, out_ref, wire):
    plane = wire.shape[0]
    used = SLICE * heads
    wire[:, used:, :] = jnp.broadcast_to(extra_ref[...][None], (plane,) + extra_ref.shape)
    for i in range(heads):
        at = slice(i * 128, (i + 1) * 128)
        key_w = (rk_ref[:, at].astype(F32) * to_ref[:, i : i + 1]).astype(BF)
        state = dot_tn(key_w, rv_ref[:, at])
        for k in range(SLICE):
            wire[:, SLICE * i + k, :] = state[k * plane : (k + 1) * plane]
    out_ref[...] = wire[...].astype(BF)


def states_kernel(
    heads, whole_ref, kp_ref, vp_ref, rq_ref, from_ref, early_ref, ck_ref, cv_ref, gr_ref, send_ref, wire,
):
    count = whole_ref.shape[0] // HALVES
    rows = whole_ref.shape[1] // 2
    both = (whole_ref[0:count].astype(F32) + whole_ref[count:].astype(F32)).astype(BF)
    ck = both[:, 0:rows, :].reshape(count * rows, -1)
    cv = both[:, rows:, :].reshape(count * rows, -1)
    ck_ref[...] = ck
    cv_ref[...] = cv
    plane = send_ref.shape[0]
    lines = send_ref.shape[1] - early_ref.shape[1]
    wire[:, SLICE * heads :, :] = jnp.zeros((plane, lines - SLICE * heads, 128), F32)
    for i in range(heads):
        at = slice(i * 128, (i + 1) * 128)
        gr = (dot_nt(ck, kp_ref[at, :]) + dot_nt(cv, vp_ref[at, :])).astype(BF)
        gr_ref[:, at] = gr
        query_w = (rq_ref[:, at].astype(F32) * from_ref[:, i : i + 1]).astype(BF)
        grad = dot_tn(query_w, gr)
        for k in range(SLICE):
            wire[:, SLICE * i + k, :] = grad[k * plane : (k + 1) * plane]
    send_ref[:, 0:lines, :] = wire[...].astype(BF)
    send_ref[:, lines:, :] = early_ref[...]


def totals_kernel(heads, part_ref, decay_ref, out_ref):
    count = part_ref.shape[0]
    zero = jnp.zeros(part_ref.shape[1:], F32)

    def step(b, carry):
        fore, back = carry
        fore = decay_ref[b] * fore + part_ref[b].astype(F32)
        r = count - 1 - b
        back = decay_ref[r] * back + part_ref[r].astype(F32)
        return fore, back

    fore, back = lax.fori_loop(0, count, step, (zero, zero), unroll=4)
    row = lax.broadcasted_iota(jnp.int32, zero.shape, 0)
    out_ref[...] = jnp.where(row < WIRE // 2, back, fore)


def scan_kernel(heads, where_ref, part_ref, decay_ref, other_ref, out_ref, ahead, behind):
    count = part_ref.shape[0]
    upper = where_ref[0] >= count
    other = other_ref[...]
    zero = jnp.zeros_like(other)

    def step(b, carry):
        fore, back = carry
        ahead[b] = fore
        fore = decay_ref[b] * fore + part_ref[b].astype(F32)
        r = count - 1 - b
        behind[r] = back
        back = decay_ref[r] * back + part_ref[r].astype(F32)
        return fore, back

    start = (jnp.where(upper, other, zero), jnp.where(upper, zero, other))
    lax.fori_loop(0, count, step, start, unroll=4)
    row = lax.broadcasted_iota(jnp.int32, part_ref.shape, 1)
    out_ref[...] = jnp.where(row < WIRE // 2, behind[...], ahead[...]).astype(BF)


def within_kernel(
    heads, rq_ref, rk_ref, rv_ref, gr_ref, cum_ref, cum_t_ref, q_ref, k_ref, v_ref,
):
    size = rq_ref.shape[0]
    t = lax.broadcasted_iota(jnp.int32, (size, size), 0)
    u = lax.broadcasted_iota(jnp.int32, (size, size), 1)
    causal = t >= u
    for i in range(heads):
        at = slice(i * 128, (i + 1) * 128)
        qr, kr, vr, gr = rq_ref[:, at], rk_ref[:, at], rv_ref[:, at], gr_ref[:, at]
        gap = cum_t_ref[:, i : i + 1] - cum_ref[i : i + 1, :]
        decay = jnp.where(causal, jnp.exp(jnp.where(causal, gap, 0.0)), 0.0)
        one = (decay * dot_nt(gr, vr)).astype(BF)
        three = (decay * dot_nt(qr, kr)).astype(BF)
        q_ref[:, at] = dot_nn(one, kr)
        k_ref[:, at] = dot_tn(one, qr)
        v_ref[:, at] = dot_tn(three, gr)


def final_kernel(
    heads, rk_ref, rv_ref, gr_ref, from_ref, to_ref, q_in_ref, k_in_ref, v_in_ref, wire_ref,
    q_ref, k_ref, v_ref, wire,
):
    wire[...] = wire_ref[...].astype(F32)

    def matrix(r):
        return jnp.concatenate([wire[:, r + k, :] for k in range(SLICE)], axis=0).astype(BF)

    for i in range(heads):
        at = slice(i * 128, (i + 1) * 128)
        grad_b, state_b = matrix(SLICE * i), matrix(WIRE // 2 + SLICE * i)
        from_start, to_end = from_ref[:, i : i + 1], to_ref[:, i : i + 1]
        q_ref[:, at] = q_in_ref[:, at] + from_start * dot_nt(gr_ref[:, at], state_b)
        k_ref[:, at] = k_in_ref[:, at] + to_end * dot_nt(rv_ref[:, at], grad_b)
        v_ref[:, at] = v_in_ref[:, at] + to_end * dot_nn(rk_ref[:, at], grad_b)


def query_grad_kernel(heads, factor, own_ref, got_ref, out_ref):
    rows = out_ref.shape[1]
    total = ((own_ref[...] + got_ref[...].astype(F32)) * factor).astype(BF)
    for h in range(heads):
        out_ref[0, :, h * 128 : (h + 1) * 128] = total[h * rows : (h + 1) * rows]


def body(
    offsets,
    queries,
    output_grad,
    attention_out,
    cache_keys,
    cache_values,
    key_projection,
    value_projection,
    retention_query,
    retention_key,
    retention_value,
    retention_decay,
):
    core, chip = lax.axis_index("core"), lax.axis_index("zl")
    place = chip * CORES + core
    secs = CHIPS * CORES
    half = lax.axis_index("zh")
    shard = half * PLANE + lax.axis_index(PLANE_AXES)
    shards = HALVES * PLANE
    block_rows, head = cache_keys.shape
    _, query_rows, query_width = queries.shape
    heads = query_width // head
    flat = query_rows * heads
    width = 2 * flat
    lines = width // 128
    rows = block_rows // secs
    factor = 1.0 / math.sqrt(head)
    blocks = 32
    sizes = (blocks, rows, query_rows, block_rows, factor)
    where = jnp.stack([shard, chip, place, core]).astype(jnp.int32)

    kv_own = jnp.concatenate(
        [lax.dynamic_slice_in_dim(a, place * rows, rows, 0) for a in (cache_keys, cache_values)]
    )
    kv_other = lax.ppermute(kv_own, "zh", [(0, 1), (1, 0)])
    kv = jnp.where(
        half == 0,
        jnp.concatenate([kv_own, kv_other]),
        jnp.concatenate([kv_other, kv_own]),
    )
    kv = jnp.broadcast_to(kv[None], (PLANE,) + kv.shape)
    own = call(
        functools.partial(pack_kernel, heads),
        shape((2 * flat, head), BF), (), (queries, output_grad),
    )
    parts = [own] + [
        lax.ppermute(own, "zl", [(i, (i - k) % CHIPS) for i in range(CHIPS)])
        for k in range(1, CHIPS)
    ]
    delta = call(
        functools.partial(delta_kernel, heads),
        shape((32 - CHIPS * lines, head), F32), (where,), (output_grad, attention_out),
        scratch=[pltpu.VMEM((width, head), F32)],
    )

    local = retention_decay.shape[0]
    used = SLICE * local
    lines_half = WIRE // 2
    cum = jnp.cumsum(retention_decay, axis=1)
    cum_t = cum.T
    last = cum[:, -1]
    from_start = jnp.exp(cum_t)
    to_end = jnp.exp(last[None] - cum_t)
    high = last.astype(BF)
    rest = last - high.astype(F32)
    middle = rest.astype(BF)
    low = (rest - middle.astype(F32)).astype(BF)
    extra = jnp.concatenate([high, middle, low]).astype(F32)
    extra = jnp.pad(extra[None], ((0, lines_half - used - 1), (0, head - extra.shape[0])))

    wide = retention_query.shape
    early = call(
        functools.partial(early_kernel, local),
        shape((PLANE, WIRE // 2, head), BF), (),
        (retention_key, retention_value, to_end, extra),
        scratch=[pltpu.VMEM((PLANE, WIRE // 2, head), F32)], flops=1 << 26,
    )

    env = (where, offsets, delta, cum, cum_t, from_start, to_end, early)
    mine = call(
        gather_kernel, shape((2, CHIPS, flat, head), BF), (where,), tuple(parts)
    )
    kv, env = lax.optimization_barrier((kv, env))
    kv = lax.all_to_all(kv, PLANE_AXES, 0, 0, tiled=True)
    kv, env = lax.optimization_barrier((kv, env))
    where, offsets, delta = env[:3]
    other = lax.ppermute(mine, "core", [(0, 1), (1, 0)])

    stats = [
        call(
            functools.partial(stats_kernel, *sizes),
            shape((CHIPS // 2 * lines, head), F32), (where, offsets), (part, kv),
            flops=4 << 30,
        )
        for part in (mine, other)
    ]
    own_stats, other_stats = stats
    both = jnp.concatenate([
        jnp.where(core == 0, own_stats, other_stats),
        jnp.where(core == 0, other_stats, own_stats),
        delta,
    ])
    both = jnp.broadcast_to(both[None], (secs,) + both.shape)
    both, env = pinned_exchange(both, ("zl", "core"), env)
    where, offsets = env[:2]
    tiles = (CORES, CHIPS // 2, 1, width)
    logs = both[:, : CHIPS * lines]
    top = jnp.max(logs, axis=0)
    log_total = (top + jnp.log(jnp.sum(jnp.exp(logs - top), axis=0))).reshape(tiles)
    deltas = both[:, CHIPS * lines : (CHIPS + 1) * lines]
    deltas = deltas.reshape(CHIPS // 2, 2, CORES, lines, head)
    deltas = (deltas[:, 0] + deltas[:, 1]).transpose(1, 0, 2, 3).reshape(tiles)

    dkv, dq_own, dq_other = call(
        functools.partial(grads_kernel, *sizes),
        (shape(kv.shape, BF), shape((CHIPS, flat, head), F32), shape((CHIPS, flat, head), BF)),
        (where, offsets),
        (mine, other, kv, log_total, deltas),
        scratch=[pltpu.VMEM((CORES * CHIPS // 2, head, width), F32)],
        flops=4 << 30,
    )
    terms, env = pinned_exchange(dkv, PLANE_AXES, env)
    total = call(
        functools.partial(total_kernel, factor),
        shape((HALVES * secs, 2 * rows, head), BF), (), (terms,),
    )
    whole, env = pinned_exchange(total, ("zh", "zl", "core"), env)
    where, offsets, delta, cum, cum_t, from_start, to_end, early = env

    cache_key_grad, cache_value_grad, out_grad, send = call(
        functools.partial(states_kernel, local),
        (
            shape((block_rows, head), BF), shape((block_rows, head), BF),
            shape(wide, BF), shape((PLANE, WIRE, head), BF),
        ),
        (),
        (whole, key_projection, value_projection, retention_query, from_start, early),
        scratch=[pltpu.VMEM((PLANE, WIRE // 2, head), F32)],
        flops=1 << 27,
    )
    send, dq_own, dq_other = lax.optimization_barrier((send, dq_own, dq_other))
    dq_other = lax.ppermute(dq_other, "core", [(0, 1), (1, 0)])
    keep, away = call(
        chip_pairs_kernel, (shape((2, flat, head), F32), shape((2, flat, head), BF)),
        (where,), (dq_own, dq_other),
    )
    away = lax.ppermute(away, "zl", [(i, i ^ 2) for i in range(CHIPS)])
    part = lax.all_to_all(send, PLANE_AXES, 0, 0, tiled=True)
    part, where = lax.optimization_barrier((part, where))
    lasts = part[:, lines_half + used, : 3 * local].astype(F32).reshape(PLANE, 3, local)
    decays = jnp.exp(lasts[:, 0] + lasts[:, 1] + lasts[:, 2])
    decays = jnp.broadcast_to(decays[:, :, None], (PLANE, local, SLICE))
    decays = jnp.pad(decays.reshape(PLANE, used), ((0, 0), (0, lines_half - used)))
    decays = jnp.concatenate([decays, decays], axis=1)[:, :, None]
    decays = jnp.broadcast_to(decays, (PLANE, WIRE, head))
    totals = call(
        functools.partial(totals_kernel, local),
        shape((WIRE, head), F32), (), (part, decays),
    )
    totals = lax.ppermute(totals, "zh", [(0, 1), (1, 0)])
    enter = call(
        functools.partial(scan_kernel, local),
        shape(part.shape, BF), (where,), (part, decays, totals),
        scratch=[pltpu.VMEM(part.shape, F32)] * 2,
    )
    enter, keep, away = lax.optimization_barrier((enter, keep, away))
    dq_mine, piece = call(
        chips_kernel, (shape((flat, head), F32), shape((flat, head), BF)), (where,), (keep, away),
    )
    piece = lax.ppermute(piece, "zl", [(i, i ^ 1) for i in range(CHIPS)])
    enter = lax.all_to_all(enter, PLANE_AXES, 0, 0, tiled=True)
    within = call(
        functools.partial(within_kernel, local), (shape(wide, F32),) * 3, (),
        (retention_query, retention_key, retention_value, out_grad, cum, cum_t),
        flops=1 << 28,
    )
    grads = call(
        functools.partial(final_kernel, local), (shape(wide, F32),) * 3, (),
        (retention_key, retention_value, out_grad, from_start, to_end, *within, enter),
        scratch=[pltpu.VMEM(enter.shape, F32)],
        flops=1 << 27,
    )
    grads, dq_mine, piece = lax.optimization_barrier((grads, dq_mine, piece))
    cross_query_grad = call(
        functools.partial(query_grad_kernel, heads, factor),
        shape(queries.shape, BF), (), (dq_mine, piece),
    )
    return (cross_query_grad, cache_key_grad, cache_value_grad) + tuple(grads)


def solution(mesh):
    sec, ctx = ("zl", "core"), ("zh", "x", "y")
    split = Mesh(mesh.devices.reshape(CHIPS, CORES, HALVES, 4, 8), sec + ctx)
    in_specs = (
        P(),
        P(sec, ctx, None),
        P(sec, ctx, None),
        P(sec, ctx, None),
        P(ctx, None),
        P(ctx, None),
        P(sec, None),
        P(sec, None),
        P(ctx, sec),
        P(ctx, sec),
        P(ctx, sec),
        P(sec, ctx),
    )
    out_specs = (
        P(sec, ctx, None),
        P(ctx, None),
        P(ctx, None),
        P(ctx, sec),
        P(ctx, sec),
        P(ctx, sec),
    )
    return jax.shard_map(body, mesh=split, in_specs=in_specs, out_specs=out_specs, check_vma=False)
```

```python
import functools
import math

import jax
import jax.numpy as jnp
from jax import lax
from jax.experimental import pallas as pl
from jax.experimental.pallas import tpu as pltpu
from jax.sharding import Mesh
from jax.sharding import PartitionSpec as P

BF = jnp.bfloat16
F32 = jnp.float32
LOW = -1e30
LOG2E = math.log2(math.e)
CHIPS, CORES = 4, 2
HALVES, PLANE = 2, 32
PLANE_AXES = ("x", "y")
SLICE = 4
WIRE = 48
SCOPED = 16 * 1024 * 1024


def dot_nt(a, b):
    return lax.dot_general(a, b, (((1,), (1,)), ((), ())), preferred_element_type=F32)


def dot_nn(a, b):
    return lax.dot_general(a, b, (((1,), (0,)), ((), ())), preferred_element_type=F32)


def dot_tn(a, b):
    return lax.dot_general(a, b, (((0,), (0,)), ((), ())), preferred_element_type=F32)


def call(kernel, outs, in_smem, ins, scratch=(), flops=0, smem_outs=0):
    vmem = pl.BlockSpec(memory_space=pltpu.VMEM)
    smem = pl.BlockSpec(memory_space=pltpu.SMEM)
    out_specs = jax.tree.map(lambda _: vmem, outs)
    if smem_outs:
        out_specs = (vmem,) * (len(outs) - smem_outs) + (smem,) * smem_outs
    return pl.pallas_call(
        kernel,
        out_shape=outs,
        in_specs=[smem] * len(in_smem) + [vmem] * len(ins),
        out_specs=out_specs,
        scratch_shapes=list(scratch),
        compiler_params=pltpu.CompilerParams(vmem_limit_bytes=SCOPED),
        cost_estimate=pl.CostEstimate(flops=flops, bytes_accessed=1 << 20, transcendentals=0),
    )(*in_smem, *ins)


def shape(dims, dtype):
    return jax.ShapeDtypeStruct(dims, dtype)


def pinned_exchange(array, axes, later):
    array, later = lax.optimization_barrier((array, later))
    array = lax.all_to_all(array, axes, 0, 0, tiled=True)
    return lax.optimization_barrier((array, later))


def pack_kernel(heads, q_ref, g_ref, out_ref):
    rows = q_ref.shape[1]
    for h in range(heads):
        at = slice(h * 128, (h + 1) * 128)
        out_ref[h * rows : (h + 1) * rows, :] = q_ref[0, :, at]
        out_ref[(heads + h) * rows : (heads + h + 1) * rows, :] = g_ref[0, :, at]


def spread_kernel(where_ref, own_ref, other_ref, out_ref):
    plane = out_ref.shape[0]
    half = where_ref[0] // plane
    out_ref[:, half] = jnp.broadcast_to(own_ref[...][None], (plane,) + own_ref.shape)
    out_ref[:, 1 - half] = jnp.broadcast_to(other_ref[...][None], (plane,) + other_ref.shape)


def delta_kernel(heads, where_ref, offset_ref, g_ref, o_ref, out_ref, place_ref, product):
    for n in range(4):
        place_ref[n] = where_ref[n]
    place_ref[4] = offset_ref[where_ref[0]]
    rows = g_ref.shape[1]
    base = lax.rem(where_ref[1], 2) * (heads * rows)
    product[...] = jnp.zeros_like(product)
    for h in range(heads):
        at = slice(h * 128, (h + 1) * 128)
        to = pl.ds(pl.multiple_of(base + h * rows, rows), rows)
        product[to, :] = g_ref[0, :, at].astype(F32) * o_ref[0, :, at].astype(F32)
    sums = jnp.sum(product[...].T, axis=0, keepdims=True)
    out_ref[...] = jnp.zeros_like(out_ref)
    for n in range(sums.shape[1] // 128):
        out_ref[n : n + 1, :] = sums[:, n * 128 : (n + 1) * 128]


def gather_kernel(where_ref, a_ref, b_ref, c_ref, d_ref, out_ref):
    flat = out_ref.shape[2]
    for k, ref in enumerate((a_ref, b_ref, c_ref, d_ref)):
        chip = lax.rem(where_ref[1] + k, CHIPS)
        out_ref[0, chip] = ref[0:flat]
        out_ref[1, chip] = ref[flat:]


def row_positions(where_ref, width, rows, block_rows):
    lane = lax.broadcasted_iota(jnp.int32, (1, width), 1)
    shard = where_ref[0]
    return lax.rem(lane, rows) + (shard * block_rows + where_ref[4])


def key_positions(place, chunk, blocks, rows, block_rows):
    at = lax.broadcasted_iota(jnp.int32, (blocks * rows, 1), 0)
    return (chunk * blocks + at // rows) * block_rows + place * rows + at % rows


def cache_place(kv_ref, chunk, blocks, rows):
    per = kv_ref.shape[0] // blocks
    line = pl.multiple_of((chunk // per) * (2 * rows), 2 * rows)
    return pl.ds(pl.multiple_of(lax.rem(chunk, per) * blocks, blocks), blocks), line


def keys_slice(kv_ref, chunk, blocks, rows, values):
    at = pl.ds(pl.multiple_of(chunk * blocks, blocks), blocks)
    return kv_ref[at, values * rows : (values + 1) * rows, :].reshape(blocks * rows, -1)


def tile(refs, which, n, t):
    return refs[n][which, 2 * t : 2 * t + 2].reshape(2 * refs[n].shape[2], -1)


def stats_kernel(
    blocks, rows, query_rows, block_rows, factor, where_ref, rows_ref, kv_ref, out_ref,
):
    shard, place = where_ref[0], where_ref[2]
    width = 2 * rows_ref.shape[2]
    lines = width // 128
    full = shard // blocks
    pos = row_positions(where_ref, width, query_rows, block_rows)
    scale = factor * LOG2E
    tiles = range(CHIPS // 2)

    def chunk(j, carry, masked=False):
        keys = keys_slice(kv_ref, j, blocks, rows, 0)
        if masked:
            seen = key_positions(place, j, blocks, rows, block_rows) <= pos
        out = []
        for t, (top, total) in zip(tiles, carry):
            s = dot_nt(keys, tile((rows_ref,), 0, 0, t))
            if masked:
                s = jnp.where(seen, s, LOW)
            new = jnp.maximum(top, jnp.max(s, axis=0, keepdims=True))
            p = jnp.exp2((s - new) * scale)
            if masked:
                p = jnp.where(seen, p, 0.0)
            total = total * jnp.exp2((top - new) * scale) + jnp.sum(p, axis=0, keepdims=True)
            out.append((new, total))
        return tuple(out)

    start = ((jnp.full((1, width), LOW, F32), jnp.zeros((1, width), F32)),) * len(tiles)
    done = chunk(full, lax.fori_loop(0, full, chunk, start), masked=True)
    for t, (top, total) in zip(tiles, done):
        lse = jnp.where(total > 0.0, top * factor + jnp.log(total), LOW)
        for m in range(lines):
            out_ref[t * lines + m : t * lines + m + 1, :] = lse[:, m * 128 : (m + 1) * 128]


def grads_kernel(
    blocks, rows, query_rows, block_rows, factor,
    where_ref, mine_ref, other_ref, kv_ref, log_ref, delta_ref,
    dkv_ref, dq_own_ref, dq_other_ref, dq_total,
):
    shard, place, core = where_ref[0], where_ref[2], where_ref[3]
    flat = mine_ref.shape[2]
    width = 2 * flat
    size = blocks * rows
    full = shard // blocks
    pos = row_positions(where_ref, width, query_rows, block_rows)
    scale = factor * LOG2E
    tiles = [(n, t) for n in range(CORES) for t in range(CHIPS // 2)]
    dq_total[...] = jnp.zeros_like(dq_total)

    def chunk(j, masked=False):
        keys = keys_slice(kv_ref, j, blocks, rows, 0)
        values = keys_slice(kv_ref, j, blocks, rows, 1)
        if masked:
            seen = key_positions(place, j, blocks, rows, block_rows) <= pos
        dk = dv = 0.0
        for i, (n, t) in enumerate(tiles):
            q = tile((mine_ref, other_ref), 0, n, t)
            g = tile((mine_ref, other_ref), 1, n, t)
            at_core = lax.rem(core + n, CORES)
            p = jnp.exp2(dot_nt(keys, q) * scale - log_ref[at_core, t] * LOG2E)
            if masked:
                p = jnp.where(seen, p, 0.0)
            ds = (p * (dot_nt(values, g) - delta_ref[at_core, t])).astype(BF)
            dk = dk + dot_nn(ds, q)
            dv = dv + dot_nn(p.astype(BF), g)
            dq_total[i] += dot_tn(keys, ds)
        at, line = cache_place(dkv_ref, j, blocks, rows)
        dkv_ref[at, pl.ds(line, rows), :] = dk.astype(BF).reshape(blocks, rows, -1)
        dkv_ref[at, pl.ds(line + rows, rows), :] = dv.astype(BF).reshape(blocks, rows, -1)

    def step(j, _):
        chunk(j)
        return 0

    lax.fori_loop(0, full, step, 0)
    chunk(full, masked=True)

    def clear(j, _):
        at, line = cache_place(dkv_ref, j, blocks, rows)
        dkv_ref[at, pl.ds(line, 2 * rows), :] = jnp.zeros((blocks, 2 * rows, kv_ref.shape[-1]), BF)
        return 0

    lax.fori_loop(full + 1, HALVES * dkv_ref.shape[0] // blocks, clear, 0)
    for i, (n, t) in enumerate(tiles):
        dq = dq_total[i].T
        dq_ref = (dq_own_ref, dq_other_ref)[n]
        for m in range(2):
            dq_ref[2 * t + m] = dq[m * flat : (m + 1) * flat].astype(dq_ref.dtype)


def chip_pairs_kernel(where_ref, own_ref, other_ref, keep_ref, send_ref):
    pair = where_ref[1] // 2
    for m in range(2):
        to = 2 * pair + m
        keep_ref[m] = own_ref[to] + other_ref[to].astype(F32)
        to = 2 * (1 - pair) + m
        send_ref[m] = (own_ref[to] + other_ref[to].astype(F32)).astype(BF)


def chips_kernel(where_ref, keep_ref, got_ref, own_ref, send_ref):
    own = lax.rem(where_ref[1], 2)
    own_ref[...] = keep_ref[own] + got_ref[own].astype(F32)
    send_ref[...] = (keep_ref[1 - own] + got_ref[1 - own].astype(F32)).astype(BF)


def total_kernel(factor, terms_ref, out_ref):
    total = jnp.sum(terms_ref[...].astype(F32), axis=0)
    lines = out_ref.shape[1]
    row = lax.broadcasted_iota(jnp.int32, (lines, 1), 0)
    scale = jnp.where(row < lines // 2, factor, 1.0)
    count = out_ref.shape[0] // HALVES
    for n in range(HALVES):
        part = (total[n * lines : (n + 1) * lines] * scale).astype(BF)
        out_ref[n * count : (n + 1) * count] = jnp.broadcast_to(part[None], (count,) + part.shape)


def early_kernel(heads, rk_ref, rv_ref, to_ref, extra_ref, out_ref, wire):
    plane = wire.shape[0]
    used = SLICE * heads
    wire[:, used:, :] = jnp.broadcast_to(extra_ref[...][None], (plane,) + extra_ref.shape)
    for i in range(heads):
        at = slice(i * 128, (i + 1) * 128)
        key_w = (rk_ref[:, at].astype(F32) * to_ref[:, i : i + 1]).astype(BF)
        state = dot_tn(key_w, rv_ref[:, at])
        for k in range(SLICE):
            wire[:, SLICE * i + k, :] = state[k * plane : (k + 1) * plane]
    out_ref[...] = wire[...].astype(BF)


def states_kernel(
    heads, whole_ref, kp_ref, vp_ref, rq_ref, from_ref, early_ref, ck_ref, cv_ref, gr_ref, send_ref, wire,
):
    count = whole_ref.shape[0] // HALVES
    rows = whole_ref.shape[1] // 2
    both = (whole_ref[0:count].astype(F32) + whole_ref[count:].astype(F32)).astype(BF)
    ck = both[:, 0:rows, :].reshape(count * rows, -1)
    cv = both[:, rows:, :].reshape(count * rows, -1)
    ck_ref[...] = ck
    cv_ref[...] = cv
    plane = send_ref.shape[0]
    lines = send_ref.shape[1] - early_ref.shape[1]
    wire[:, SLICE * heads :, :] = jnp.zeros((plane, lines - SLICE * heads, 128), F32)
    for i in range(heads):
        at = slice(i * 128, (i + 1) * 128)
        gr = (dot_nt(ck, kp_ref[at, :]) + dot_nt(cv, vp_ref[at, :])).astype(BF)
        gr_ref[:, at] = gr
        query_w = (rq_ref[:, at].astype(F32) * from_ref[:, i : i + 1]).astype(BF)
        grad = dot_tn(query_w, gr)
        for k in range(SLICE):
            wire[:, SLICE * i + k, :] = grad[k * plane : (k + 1) * plane]
    send_ref[:, 0:lines, :] = wire[...].astype(BF)
    send_ref[:, lines:, :] = early_ref[...]


def totals_kernel(heads, part_ref, decay_ref, out_ref):
    count = part_ref.shape[0]
    zero = jnp.zeros(part_ref.shape[1:], F32)

    def step(b, carry):
        fore, back = carry
        fore = decay_ref[b] * fore + part_ref[b].astype(F32)
        r = count - 1 - b
        back = decay_ref[r] * back + part_ref[r].astype(F32)
        return fore, back

    fore, back = lax.fori_loop(0, count, step, (zero, zero), unroll=4)
    row = lax.broadcasted_iota(jnp.int32, zero.shape, 0)
    out_ref[...] = jnp.where(row < WIRE // 2, back, fore)


def scan_kernel(heads, where_ref, part_ref, decay_ref, other_ref, out_ref, ahead, behind):
    count = part_ref.shape[0]
    upper = where_ref[0] >= count
    other = other_ref[...]
    zero = jnp.zeros_like(other)

    def step(b, carry):
        fore, back = carry
        ahead[b] = fore
        fore = decay_ref[b] * fore + part_ref[b].astype(F32)
        r = count - 1 - b
        behind[r] = back
        back = decay_ref[r] * back + part_ref[r].astype(F32)
        return fore, back

    start = (jnp.where(upper, other, zero), jnp.where(upper, zero, other))
    lax.fori_loop(0, count, step, start, unroll=4)
    used = SLICE * heads
    at = WIRE // 2
    both = jnp.concatenate([behind[:, 0:used, :], ahead[:, at : at + used, :]], axis=1)
    out_ref[...] = both.astype(BF)


def within_kernel(
    heads, rq_ref, rk_ref, rv_ref, gr_ref, cum_ref, cum_t_ref, q_ref, k_ref, v_ref,
):
    size = rq_ref.shape[0]
    t = lax.broadcasted_iota(jnp.int32, (size, size), 0)
    u = lax.broadcasted_iota(jnp.int32, (size, size), 1)
    causal = t >= u
    for i in range(heads):
        at = slice(i * 128, (i + 1) * 128)
        qr, kr, vr, gr = rq_ref[:, at], rk_ref[:, at], rv_ref[:, at], gr_ref[:, at]
        gap = cum_t_ref[:, i : i + 1] - cum_ref[i : i + 1, :]
        decay = jnp.where(causal, jnp.exp(jnp.where(causal, gap, 0.0)), 0.0)
        one = (decay * dot_nt(gr, vr)).astype(BF)
        three = (decay * dot_nt(qr, kr)).astype(BF)
        q_ref[:, at] = dot_nn(one, kr)
        k_ref[:, at] = dot_tn(one, qr)
        v_ref[:, at] = dot_tn(three, gr)


def final_kernel(
    heads, rk_ref, rv_ref, gr_ref, from_ref, to_ref, q_in_ref, k_in_ref, v_in_ref, wire_ref,
    q_ref, k_ref, v_ref, wire,
):
    wire[...] = wire_ref[...].astype(F32)

    def matrix(r):
        return jnp.concatenate([wire[:, r + k, :] for k in range(SLICE)], axis=0).astype(BF)

    for i in range(heads):
        at = slice(i * 128, (i + 1) * 128)
        grad_b, state_b = matrix(SLICE * i), matrix(SLICE * (heads + i))
        from_start, to_end = from_ref[:, i : i + 1], to_ref[:, i : i + 1]
        q_ref[:, at] = q_in_ref[:, at] + from_start * dot_nt(gr_ref[:, at], state_b)
        k_ref[:, at] = k_in_ref[:, at] + to_end * dot_nt(rv_ref[:, at], grad_b)
        v_ref[:, at] = v_in_ref[:, at] + to_end * dot_nn(rk_ref[:, at], grad_b)


def query_grad_kernel(heads, factor, own_ref, got_ref, out_ref):
    rows = out_ref.shape[1]
    total = ((own_ref[...] + got_ref[...].astype(F32)) * factor).astype(BF)
    for h in range(heads):
        out_ref[0, :, h * 128 : (h + 1) * 128] = total[h * rows : (h + 1) * rows]


def body(
    offsets,
    queries,
    output_grad,
    attention_out,
    cache_keys,
    cache_values,
    key_projection,
    value_projection,
    retention_query,
    retention_key,
    retention_value,
    retention_decay,
):
    core, chip = lax.axis_index("core"), lax.axis_index("zl")
    place = chip * CORES + core
    secs = CHIPS * CORES
    half = lax.axis_index("zh")
    shard = half * PLANE + lax.axis_index(PLANE_AXES)
    shards = HALVES * PLANE
    block_rows, head = cache_keys.shape
    _, query_rows, query_width = queries.shape
    heads = query_width // head
    flat = query_rows * heads
    width = 2 * flat
    lines = width // 128
    rows = block_rows // secs
    factor = 1.0 / math.sqrt(head)
    blocks = 32
    sizes = (blocks, rows, query_rows, block_rows, factor)
    where = jnp.stack([shard, chip, place, core]).astype(jnp.int32)

    kv_own = jnp.concatenate(
        [lax.dynamic_slice_in_dim(a, place * rows, rows, 0) for a in (cache_keys, cache_values)]
    )
    kv = jnp.broadcast_to(kv_own[None], (shards,) + kv_own.shape)
    own = call(
        functools.partial(pack_kernel, heads),
        shape((2 * flat, head), BF), (), (queries, output_grad), flops=1 << 20,
    )
    parts = [own] + [
        lax.ppermute(own, "zl", [(i, (i - k) % CHIPS) for i in range(CHIPS)])
        for k in range(1, CHIPS)
    ]
    delta, where = call(
        functools.partial(delta_kernel, heads),
        (shape((32 - CHIPS * lines, head), F32), shape((5,), jnp.int32)),
        (where, offsets), (output_grad, attention_out), smem_outs=1,
        scratch=[pltpu.VMEM((width, head), F32)],
    )

    local = retention_decay.shape[0]
    used = SLICE * local
    lines_half = WIRE // 2
    cum = jnp.cumsum(retention_decay, axis=1)
    cum_t = cum.T
    last = cum[:, -1]
    from_start = jnp.exp(cum_t)
    to_end = jnp.exp(last[None] - cum_t)
    high = last.astype(BF)
    rest = last - high.astype(F32)
    middle = rest.astype(BF)
    low = (rest - middle.astype(F32)).astype(BF)
    extra = jnp.concatenate([high, middle, low]).astype(F32)
    extra = jnp.pad(extra[None], ((0, lines_half - used - 1), (0, head - extra.shape[0])))

    wide = retention_query.shape
    early = call(
        functools.partial(early_kernel, local),
        shape((PLANE, WIRE // 2, head), BF), (),
        (retention_key, retention_value, to_end, extra),
        scratch=[pltpu.VMEM((PLANE, WIRE // 2, head), F32)], flops=1 << 26,
    )

    env = (where, delta, cum, cum_t, from_start, to_end, early)
    mine = call(
        gather_kernel, shape((2, CHIPS, flat, head), BF), (where,), tuple(parts), flops=4 << 30
    )
    kv = lax.all_to_all(kv, ("zh",) + PLANE_AXES, 0, 0, tiled=True)
    kv, env = lax.optimization_barrier((kv, env))
    where, delta = env[:2]
    other = lax.ppermute(mine, "core", [(0, 1), (1, 0)])

    stats = [
        call(
            functools.partial(stats_kernel, *sizes),
            shape((CHIPS // 2 * lines, head), F32), (where,), (part, kv),
            flops=1 << 28,
        )
        for part in (mine, other)
    ]
    own_stats, other_stats = stats
    both = jnp.concatenate([
        jnp.where(core == 0, own_stats, other_stats),
        jnp.where(core == 0, other_stats, own_stats),
        delta,
    ])
    both = jnp.broadcast_to(both[None], (secs,) + both.shape)
    both, env = pinned_exchange(both, ("zl", "core"), env)
    where = env[0]
    tiles = (CORES, CHIPS // 2, 1, width)
    logs = both[:, : CHIPS * lines]
    top = jnp.max(logs, axis=0)
    log_total = (top + jnp.log(jnp.sum(jnp.exp(logs - top), axis=0))).reshape(tiles)
    deltas = both[:, CHIPS * lines : (CHIPS + 1) * lines]
    deltas = deltas.reshape(CHIPS // 2, 2, CORES, lines, head)
    deltas = (deltas[:, 0] + deltas[:, 1]).transpose(1, 0, 2, 3).reshape(tiles)

    dkv, dq_own, dq_other = call(
        functools.partial(grads_kernel, *sizes),
        (shape((PLANE, HALVES * 2 * rows, head), BF), shape((CHIPS, flat, head), F32), shape((CHIPS, flat, head), BF)),
        (where,),
        (mine, other, kv, log_total, deltas),
        scratch=[pltpu.VMEM((CORES * CHIPS // 2, head, width), F32)],
        flops=4 << 30,
    )
    terms, env = pinned_exchange(dkv, PLANE_AXES, env)
    total = call(
        functools.partial(total_kernel, factor),
        shape((HALVES * secs, 2 * rows, head), BF), (), (terms,),
    )
    whole, env = pinned_exchange(total, ("zh", "zl", "core"), env)
    where, delta, cum, cum_t, from_start, to_end, early = env

    cache_key_grad, cache_value_grad, out_grad, send = call(
        functools.partial(states_kernel, local),
        (
            shape((block_rows, head), BF), shape((block_rows, head), BF),
            shape(wide, BF), shape((PLANE, WIRE, head), BF),
        ),
        (),
        (whole, key_projection, value_projection, retention_query, from_start, early),
        scratch=[pltpu.VMEM((PLANE, WIRE // 2, head), F32)],
        flops=1 << 27,
    )
    send, dq_own, dq_other = lax.optimization_barrier((send, dq_own, dq_other))
    dq_other = lax.ppermute(dq_other, "core", [(0, 1), (1, 0)])
    keep, away = call(
        chip_pairs_kernel, (shape((2, flat, head), F32), shape((2, flat, head), BF)),
        (where,), (dq_own, dq_other),
    )
    away = lax.ppermute(away, "zl", [(i, i ^ 2) for i in range(CHIPS)])
    part = lax.all_to_all(send, PLANE_AXES, 0, 0, tiled=True)
    part, where = lax.optimization_barrier((part, where))
    lasts = part[:, lines_half + used, : 3 * local].astype(F32).reshape(PLANE, 3, local)
    decays = jnp.exp(lasts[:, 0] + lasts[:, 1] + lasts[:, 2])
    decays = jnp.broadcast_to(decays[:, :, None], (PLANE, local, SLICE))
    decays = jnp.pad(decays.reshape(PLANE, used), ((0, 0), (0, lines_half - used)))
    decays = jnp.concatenate([decays, decays], axis=1)[:, :, None]
    decays = jnp.broadcast_to(decays, (PLANE, WIRE, head))
    totals = call(
        functools.partial(totals_kernel, local),
        shape((WIRE, head), F32), (), (part, decays),
    )
    totals = lax.ppermute(totals, "zh", [(0, 1), (1, 0)])
    enter = call(
        functools.partial(scan_kernel, local),
        shape((PLANE, 2 * used, head), BF), (where,), (part, decays, totals),
        scratch=[pltpu.VMEM(part.shape, F32)] * 2,
    )
    enter, keep, away = lax.optimization_barrier((enter, keep, away))
    dq_mine, piece = call(
        chips_kernel, (shape((flat, head), F32), shape((flat, head), BF)), (where,), (keep, away),
    )
    piece = lax.ppermute(piece, "zl", [(i, i ^ 1) for i in range(CHIPS)])
    enter = lax.all_to_all(enter, PLANE_AXES, 0, 0, tiled=True)
    within = call(
        functools.partial(within_kernel, local), (shape(wide, F32),) * 3, (),
        (retention_query, retention_key, retention_value, out_grad, cum, cum_t),
        flops=1 << 28,
    )
    grads = call(
        functools.partial(final_kernel, local), (shape(wide, F32),) * 3, (),
        (retention_key, retention_value, out_grad, from_start, to_end, *within, enter),
        scratch=[pltpu.VMEM(enter.shape, F32)],
        flops=1 << 27,
    )
    grads, dq_mine, piece = lax.optimization_barrier((grads, dq_mine, piece))
    cross_query_grad = call(
        functools.partial(query_grad_kernel, heads, factor),
        shape(queries.shape, BF), (), (dq_mine, piece),
    )
    return (cross_query_grad, cache_key_grad, cache_value_grad) + tuple(grads)


def solution(mesh):
    sec, ctx = ("zl", "core"), ("zh", "x", "y")
    split = Mesh(mesh.devices.reshape(CHIPS, CORES, HALVES, 4, 8), sec + ctx)
    in_specs = (
        P(),
        P(sec, ctx, None),
        P(sec, ctx, None),
        P(sec, ctx, None),
        P(ctx, None),
        P(ctx, None),
        P(sec, None),
        P(sec, None),
        P(ctx, sec),
        P(ctx, sec),
        P(ctx, sec),
        P(sec, ctx),
    )
    out_specs = (
        P(sec, ctx, None),
        P(ctx, None),
        P(ctx, None),
        P(ctx, sec),
        P(ctx, sec),
        P(ctx, sec),
    )
    return jax.shard_map(body, mesh=split, in_specs=in_specs, out_specs=out_specs, check_vma=False)
```

```python
import functools
import math

import jax
import jax.numpy as jnp
from jax import lax
from jax.experimental import pallas as pl
from jax.experimental.pallas import tpu as pltpu
from jax.sharding import Mesh
from jax.sharding import PartitionSpec as P

BF = jnp.bfloat16
F32 = jnp.float32
LOW = -1e30
LOG2E = math.log2(math.e)
CHIPS, CORES = 4, 2
HALVES, PLANE = 2, 32
PLANE_AXES = ("x", "y")
SLICE = 4
WIRE = 48
SCOPED = 16 * 1024 * 1024


def dot_nt(a, b):
    return lax.dot_general(a, b, (((1,), (1,)), ((), ())), preferred_element_type=F32)


def dot_nn(a, b):
    return lax.dot_general(a, b, (((1,), (0,)), ((), ())), preferred_element_type=F32)


def dot_tn(a, b):
    return lax.dot_general(a, b, (((0,), (0,)), ((), ())), preferred_element_type=F32)


def call(kernel, outs, in_smem, ins, scratch=(), flops=0, smem_outs=0, space=pltpu.VMEM, scoped=SCOPED):
    vmem = pl.BlockSpec(memory_space=pltpu.VMEM)
    smem = pl.BlockSpec(memory_space=pltpu.SMEM)
    out_specs = jax.tree.map(lambda _: vmem, outs)
    if smem_outs:
        out_specs = (vmem,) * (len(outs) - smem_outs) + (smem,) * smem_outs
    return pl.pallas_call(
        kernel,
        out_shape=outs,
        in_specs=[smem] * len(in_smem) + [pl.BlockSpec(memory_space=space)] * len(ins),
        out_specs=out_specs,
        scratch_shapes=list(scratch),
        compiler_params=pltpu.CompilerParams(vmem_limit_bytes=scoped),
        cost_estimate=pl.CostEstimate(flops=flops, bytes_accessed=1 << 20, transcendentals=0),
    )(*in_smem, *ins)


def shape(dims, dtype):
    return jax.ShapeDtypeStruct(dims, dtype)


def pinned_exchange(array, axes, later):
    array, later = lax.optimization_barrier((array, later))
    array = lax.all_to_all(array, axes, 0, 0, tiled=True)
    return lax.optimization_barrier((array, later))


def pack_kernel(heads, q_hbm, g_hbm, out_ref, q_ref, g_ref, sems):
    rows = q_ref.shape[1]
    copies = [
        pltpu.make_async_copy(q_hbm, q_ref, sems.at[0]),
        pltpu.make_async_copy(g_hbm, g_ref, sems.at[1]),
    ]
    for copy in copies:
        copy.start()
    for copy in copies:
        copy.wait()
    for h in range(heads):
        at = slice(h * 128, (h + 1) * 128)
        out_ref[h * rows : (h + 1) * rows, :] = q_ref[0, :, at]
        out_ref[(heads + h) * rows : (heads + h + 1) * rows, :] = g_ref[0, :, at]


def delta_kernel(heads, where_ref, offset_ref, g_ref, o_ref, out_ref, place_ref, product):
    for n in range(4):
        place_ref[n] = where_ref[n]
    place_ref[4] = offset_ref[where_ref[0]]
    rows = g_ref.shape[1]
    base = lax.rem(where_ref[1], 2) * (heads * rows)
    product[...] = jnp.zeros_like(product)
    for h in range(heads):
        at = slice(h * 128, (h + 1) * 128)
        to = pl.ds(pl.multiple_of(base + h * rows, rows), rows)
        product[to, :] = g_ref[0, :, at].astype(F32) * o_ref[0, :, at].astype(F32)
    sums = jnp.sum(product[...].T, axis=0, keepdims=True)
    out_ref[...] = jnp.zeros_like(out_ref)
    for n in range(sums.shape[1] // 128):
        out_ref[n : n + 1, :] = sums[:, n * 128 : (n + 1) * 128]


def gather_kernel(where_ref, a_ref, b_ref, c_ref, d_ref, out_ref):
    flat = out_ref.shape[2]
    for k, ref in enumerate((a_ref, b_ref, c_ref, d_ref)):
        chip = lax.rem(where_ref[1] + k, CHIPS)
        out_ref[0, chip] = ref[0:flat]
        out_ref[1, chip] = ref[flat:]


def row_positions(where_ref, width, rows, block_rows):
    lane = lax.broadcasted_iota(jnp.int32, (1, width), 1)
    shard = where_ref[0]
    return lax.rem(lane, rows) + (shard * block_rows + where_ref[4])


def key_positions(place, chunk, blocks, rows, block_rows):
    at = lax.broadcasted_iota(jnp.int32, (blocks * rows, 1), 0)
    return (chunk * blocks + at // rows) * block_rows + place * rows + at % rows


def cache_place(kv_ref, chunk, blocks, rows):
    per = kv_ref.shape[0] // blocks
    line = pl.multiple_of((chunk // per) * (2 * rows), 2 * rows)
    return pl.ds(pl.multiple_of(lax.rem(chunk, per) * blocks, blocks), blocks), line


def keys_slice(kv_ref, chunk, blocks, rows, values):
    at = pl.ds(pl.multiple_of(chunk * blocks, blocks), blocks)
    return kv_ref[at, values * rows : (values + 1) * rows, :].reshape(blocks * rows, -1)


def tile(refs, which, n, t):
    return refs[n][which, 2 * t : 2 * t + 2].reshape(2 * refs[n].shape[2], -1)


def stats_kernel(
    blocks, rows, query_rows, block_rows, factor, where_ref, rows_ref, kv_ref, out_ref,
):
    shard, place = where_ref[0], where_ref[2]
    width = 2 * rows_ref.shape[2]
    lines = width // 128
    full = shard // blocks
    pos = row_positions(where_ref, width, query_rows, block_rows)
    scale = factor * LOG2E
    tiles = range(CHIPS // 2)

    def chunk(j, carry, masked=False):
        keys = keys_slice(kv_ref, j, blocks, rows, 0)
        if masked:
            seen = key_positions(place, j, blocks, rows, block_rows) <= pos
        out = []
        for t, (top, total) in zip(tiles, carry):
            s = dot_nt(keys, tile((rows_ref,), 0, 0, t))
            if masked:
                s = jnp.where(seen, s, LOW)
            new = jnp.maximum(top, jnp.max(s, axis=0, keepdims=True))
            p = jnp.exp2((s - new) * scale)
            if masked:
                p = jnp.where(seen, p, 0.0)
            total = total * jnp.exp2((top - new) * scale) + jnp.sum(p, axis=0, keepdims=True)
            out.append((new, total))
        return tuple(out)

    start = ((jnp.full((1, width), LOW, F32), jnp.zeros((1, width), F32)),) * len(tiles)
    done = chunk(full, lax.fori_loop(0, full, chunk, start), masked=True)
    for t, (top, total) in zip(tiles, done):
        lse = jnp.where(total > 0.0, top * factor + jnp.log(total), LOW)
        for m in range(lines):
            out_ref[t * lines + m : t * lines + m + 1, :] = lse[:, m * 128 : (m + 1) * 128]


def grads_kernel(
    blocks, rows, query_rows, block_rows, factor,
    where_ref, mine_ref, other_ref, kv_ref, log_ref, delta_ref,
    dkv_ref, dq_own_ref, dq_other_ref, dq_total,
):
    shard, place, core = where_ref[0], where_ref[2], where_ref[3]
    flat = mine_ref.shape[2]
    width = 2 * flat
    size = blocks * rows
    full = shard // blocks
    pos = row_positions(where_ref, width, query_rows, block_rows)
    scale = factor * LOG2E
    tiles = [(n, t) for n in range(CORES) for t in range(CHIPS // 2)]
    dq_total[...] = jnp.zeros_like(dq_total)

    def chunk(j, masked=False):
        keys = keys_slice(kv_ref, j, blocks, rows, 0)
        values = keys_slice(kv_ref, j, blocks, rows, 1)
        if masked:
            seen = key_positions(place, j, blocks, rows, block_rows) <= pos
        dk = dv = 0.0
        for i, (n, t) in enumerate(tiles):
            q = tile((mine_ref, other_ref), 0, n, t)
            g = tile((mine_ref, other_ref), 1, n, t)
            at_core = lax.rem(core + n, CORES)
            p = jnp.exp2(dot_nt(keys, q) * scale - log_ref[at_core, t] * LOG2E)
            if masked:
                p = jnp.where(seen, p, 0.0)
            ds = (p * (dot_nt(values, g) - delta_ref[at_core, t])).astype(BF)
            dk = dk + dot_nn(ds, q)
            dv = dv + dot_nn(p.astype(BF), g)
            dq_total[i] += dot_tn(keys, ds)
        at, line = cache_place(dkv_ref, j, blocks, rows)
        dkv_ref[at, pl.ds(line, rows), :] = dk.astype(BF).reshape(blocks, rows, -1)
        dkv_ref[at, pl.ds(line + rows, rows), :] = dv.astype(BF).reshape(blocks, rows, -1)

    def step(j, _):
        chunk(j)
        return 0

    lax.fori_loop(0, full, step, 0)
    chunk(full, masked=True)

    def clear(j, _):
        at, line = cache_place(dkv_ref, j, blocks, rows)
        dkv_ref[at, pl.ds(line, 2 * rows), :] = jnp.zeros((blocks, 2 * rows, kv_ref.shape[-1]), BF)
        return 0

    lax.fori_loop(full + 1, HALVES * dkv_ref.shape[0] // blocks, clear, 0)
    for i, (n, t) in enumerate(tiles):
        dq = dq_total[i].T
        dq_ref = (dq_own_ref, dq_other_ref)[n]
        for m in range(2):
            dq_ref[2 * t + m] = dq[m * flat : (m + 1) * flat].astype(dq_ref.dtype)


def chip_pairs_kernel(where_ref, own_ref, other_ref, keep_ref, send_ref):
    pair = where_ref[1] // 2
    for m in range(2):
        to = 2 * pair + m
        keep_ref[m] = own_ref[to] + other_ref[to].astype(F32)
        to = 2 * (1 - pair) + m
        send_ref[m] = (own_ref[to] + other_ref[to].astype(F32)).astype(BF)


def chips_kernel(where_ref, keep_ref, got_ref, own_ref, send_ref):
    own = lax.rem(where_ref[1], 2)
    own_ref[...] = keep_ref[own] + got_ref[own].astype(F32)
    send_ref[...] = (keep_ref[1 - own] + got_ref[1 - own].astype(F32)).astype(BF)


def total_kernel(factor, terms_ref, out_ref):
    total = jnp.sum(terms_ref[...].astype(F32), axis=0)
    lines = out_ref.shape[1]
    row = lax.broadcasted_iota(jnp.int32, (lines, 1), 0)
    scale = jnp.where(row < lines // 2, factor, 1.0)
    count = out_ref.shape[0] // HALVES
    for n in range(HALVES):
        part = (total[n * lines : (n + 1) * lines] * scale).astype(BF)
        out_ref[n * count : (n + 1) * count] = jnp.broadcast_to(part[None], (count,) + part.shape)


def early_kernel(heads, rk_ref, rv_ref, to_ref, extra_ref, out_ref, wire):
    plane = wire.shape[0]
    used = SLICE * heads
    wire[:, used:, :] = jnp.broadcast_to(extra_ref[...][None], (plane,) + extra_ref.shape)
    for i in range(heads):
        at = slice(i * 128, (i + 1) * 128)
        key_w = (rk_ref[:, at].astype(F32) * to_ref[:, i : i + 1]).astype(BF)
        state = dot_tn(key_w, rv_ref[:, at])
        for k in range(SLICE):
            wire[:, SLICE * i + k, :] = state[k * plane : (k + 1) * plane]
    out_ref[...] = wire[...].astype(BF)


def states_kernel(
    heads, whole_ref, kp_ref, vp_ref, rq_ref, from_ref, early_ref, ck_ref, cv_ref, gr_ref, send_ref, wire,
):
    count = whole_ref.shape[0] // HALVES
    rows = whole_ref.shape[1] // 2
    both = (whole_ref[0:count].astype(F32) + whole_ref[count:].astype(F32)).astype(BF)
    ck = both[:, 0:rows, :].reshape(count * rows, -1)
    cv = both[:, rows:, :].reshape(count * rows, -1)
    ck_ref[...] = ck
    cv_ref[...] = cv
    plane = send_ref.shape[0]
    lines = send_ref.shape[1] - early_ref.shape[1]
    wire[:, SLICE * heads :, :] = jnp.zeros((plane, lines - SLICE * heads, 128), F32)
    both = jnp.concatenate([ck, cv], axis=1)
    projection = jnp.concatenate([kp_ref[...], vp_ref[...]], axis=1)
    out_grad = dot_nt(both, projection).astype(BF)
    gr_ref[...] = out_grad
    for i in range(heads):
        at = slice(i * 128, (i + 1) * 128)
        gr = out_grad[:, at]
        query_w = (rq_ref[:, at].astype(F32) * from_ref[:, i : i + 1]).astype(BF)
        grad = dot_tn(query_w, gr)
        for k in range(SLICE):
            wire[:, SLICE * i + k, :] = grad[k * plane : (k + 1) * plane]
    send_ref[:, 0:lines, :] = wire[...].astype(BF)
    send_ref[:, lines:, :] = early_ref[...]


def totals_kernel(heads, part_ref, decay_ref, out_ref):
    count = part_ref.shape[0]
    zero = jnp.zeros(part_ref.shape[1:], F32)

    def step(b, carry):
        fore, back = carry
        fore = decay_ref[b] * fore + part_ref[b].astype(F32)
        r = count - 1 - b
        back = decay_ref[r] * back + part_ref[r].astype(F32)
        return fore, back

    fore, back = lax.fori_loop(0, count, step, (zero, zero), unroll=4)
    row = lax.broadcasted_iota(jnp.int32, zero.shape, 0)
    out_ref[...] = jnp.where(row < WIRE // 2, back, fore)


def scan_kernel(heads, where_ref, part_ref, decay_ref, other_ref, out_ref, ahead, behind):
    count = part_ref.shape[0]
    upper = where_ref[0] >= count
    other = other_ref[...]
    zero = jnp.zeros_like(other)

    def step(b, carry):
        fore, back = carry
        ahead[b] = fore
        fore = decay_ref[b] * fore + part_ref[b].astype(F32)
        r = count - 1 - b
        behind[r] = back
        back = decay_ref[r] * back + part_ref[r].astype(F32)
        return fore, back

    start = (jnp.where(upper, other, zero), jnp.where(upper, zero, other))
    lax.fori_loop(0, count, step, start, unroll=4)
    used = SLICE * heads
    at = WIRE // 2
    both = jnp.concatenate([behind[:, 0:used, :], ahead[:, at : at + used, :]], axis=1)
    out_ref[...] = both.astype(BF)


def within_kernel(
    heads, rq_ref, rk_ref, rv_ref, gr_ref, cum_ref, cum_t_ref, q_ref, k_ref, v_ref,
):
    size = rq_ref.shape[0]
    t = lax.broadcasted_iota(jnp.int32, (size, size), 0)
    u = lax.broadcasted_iota(jnp.int32, (size, size), 1)
    causal = t >= u
    for i in range(heads):
        at = slice(i * 128, (i + 1) * 128)
        qr, kr, vr, gr = rq_ref[:, at], rk_ref[:, at], rv_ref[:, at], gr_ref[:, at]
        gap = cum_t_ref[:, i : i + 1] - cum_ref[i : i + 1, :]
        decay = jnp.where(causal, jnp.exp(jnp.where(causal, gap, 0.0)), 0.0)
        one = (decay * dot_nt(gr, vr)).astype(BF)
        three = (decay * dot_nt(qr, kr)).astype(BF)
        q_ref[:, at] = dot_nn(one, kr)
        k_ref[:, at] = dot_tn(one, qr)
        v_ref[:, at] = dot_tn(three, gr)


def final_kernel(
    heads, query_heads, factor, rk_ref, rv_ref, gr_ref, from_ref, to_ref, q_in_ref, k_in_ref, v_in_ref,
    wire_ref, own_ref, got_ref, q_ref, k_ref, v_ref, cross_ref, wire,
):
    rows = cross_ref.shape[1]
    total = ((own_ref[...] + got_ref[...].astype(F32)) * factor).astype(BF)
    for h in range(query_heads):
        cross_ref[0, :, h * 128 : (h + 1) * 128] = total[h * rows : (h + 1) * rows]
    wire[...] = wire_ref[...].astype(F32)

    def matrix(r):
        return jnp.concatenate([wire[:, r + k, :] for k in range(SLICE)], axis=0).astype(BF)

    for i in range(heads):
        at = slice(i * 128, (i + 1) * 128)
        grad_b, state_b = matrix(SLICE * i), matrix(SLICE * (heads + i))
        from_start, to_end = from_ref[:, i : i + 1], to_ref[:, i : i + 1]
        q_ref[:, at] = q_in_ref[:, at] + from_start * dot_nt(gr_ref[:, at], state_b)
        k_ref[:, at] = k_in_ref[:, at] + to_end * dot_nt(rv_ref[:, at], grad_b)
        v_ref[:, at] = v_in_ref[:, at] + to_end * dot_nn(rk_ref[:, at], grad_b)


def body(
    offsets,
    queries,
    output_grad,
    attention_out,
    cache_keys,
    cache_values,
    key_projection,
    value_projection,
    retention_query,
    retention_key,
    retention_value,
    retention_decay,
):
    core, chip = lax.axis_index("core"), lax.axis_index("zl")
    place = chip * CORES + core
    secs = CHIPS * CORES
    half = lax.axis_index("zh")
    shard = half * PLANE + lax.axis_index(PLANE_AXES)
    shards = HALVES * PLANE
    block_rows, head = cache_keys.shape
    _, query_rows, query_width = queries.shape
    heads = query_width // head
    flat = query_rows * heads
    width = 2 * flat
    lines = width // 128
    rows = block_rows // secs
    factor = 1.0 / math.sqrt(head)
    blocks = 32
    sizes = (blocks, rows, query_rows, block_rows, factor)
    where = jnp.stack([shard, chip, place, core]).astype(jnp.int32)

    kv_own = jnp.concatenate(
        [lax.dynamic_slice_in_dim(a, place * rows, rows, 0) for a in (cache_keys, cache_values)]
    )
    kv = jnp.broadcast_to(kv_own[None], (shards,) + kv_own.shape)
    own = call(
        functools.partial(pack_kernel, heads),
        shape((2 * flat, head), BF), (), (queries, output_grad),
        scratch=[pltpu.VMEM(queries.shape, BF)] * 2 + [pltpu.SemaphoreType.DMA((2,))],
        space=pltpu.HBM, scoped=56 * 1024 * 1024,
    )
    parts = [own] + [
        lax.ppermute(own, "zl", [(i, (i - k) % CHIPS) for i in range(CHIPS)])
        for k in range(1, CHIPS)
    ]
    delta, where = call(
        functools.partial(delta_kernel, heads),
        (shape((32 - CHIPS * lines, head), F32), shape((5,), jnp.int32)),
        (where, offsets), (output_grad, attention_out), smem_outs=1,
        scratch=[pltpu.VMEM((width, head), F32)],
    )

    local = retention_decay.shape[0]
    used = SLICE * local
    lines_half = WIRE // 2
    cum = jnp.cumsum(retention_decay, axis=1)
    cum_t = cum.T
    last = cum[:, -1]
    from_start = jnp.exp(cum_t)
    to_end = jnp.exp(last[None] - cum_t)
    high = last.astype(BF)
    rest = last - high.astype(F32)
    middle = rest.astype(BF)
    low = (rest - middle.astype(F32)).astype(BF)
    extra = jnp.concatenate([high, middle, low]).astype(F32)
    extra = jnp.pad(extra[None], ((0, lines_half - used - 1), (0, head - extra.shape[0])))

    wide = retention_query.shape
    early = call(
        functools.partial(early_kernel, local),
        shape((PLANE, WIRE // 2, head), BF), (),
        (retention_key, retention_value, to_end, extra),
        scratch=[pltpu.VMEM((PLANE, WIRE // 2, head), F32)], flops=1 << 26,
    )

    env = (where, delta, cum, cum_t, from_start, to_end, early)
    mine = call(
        gather_kernel, shape((2, CHIPS, flat, head), BF), (where,), tuple(parts), flops=4 << 30
    )
    kv = lax.all_to_all(kv, ("zh",) + PLANE_AXES, 0, 0, tiled=True)
    kv, env = lax.optimization_barrier((kv, env))
    where, delta = env[:2]
    other = lax.ppermute(mine, "core", [(0, 1), (1, 0)])

    stats = [
        call(
            functools.partial(stats_kernel, *sizes),
            shape((CHIPS // 2 * lines, head), F32), (where,), (part, kv),
            flops=1 << 28,
        )
        for part in (mine, other)
    ]
    own_stats, other_stats = stats
    both = jnp.concatenate([
        jnp.where(core == 0, own_stats, other_stats),
        jnp.where(core == 0, other_stats, own_stats),
        delta,
    ])
    both = jnp.broadcast_to(both[None], (secs,) + both.shape)
    both, env = pinned_exchange(both, ("zl", "core"), env)
    where = env[0]
    tiles = (CORES, CHIPS // 2, 1, width)
    logs = both[:, : CHIPS * lines]
    top = jnp.max(logs, axis=0)
    log_total = (top + jnp.log(jnp.sum(jnp.exp(logs - top), axis=0))).reshape(tiles)
    deltas = both[:, CHIPS * lines : (CHIPS + 1) * lines]
    deltas = deltas.reshape(CHIPS // 2, 2, CORES, lines, head)
    deltas = (deltas[:, 0] + deltas[:, 1]).transpose(1, 0, 2, 3).reshape(tiles)

    dkv, dq_own, dq_other = call(
        functools.partial(grads_kernel, *sizes),
        (shape((PLANE, HALVES * 2 * rows, head), BF), shape((CHIPS, flat, head), F32), shape((CHIPS, flat, head), BF)),
        (where,),
        (mine, other, kv, log_total, deltas),
        scratch=[pltpu.VMEM((CORES * CHIPS // 2, head, width), F32)],
        flops=4 << 30,
    )
    terms, env = pinned_exchange(dkv, PLANE_AXES, env)
    total = call(
        functools.partial(total_kernel, factor),
        shape((HALVES * secs, 2 * rows, head), BF), (), (terms,),
    )
    whole, env = pinned_exchange(total, ("zh", "zl", "core"), env)
    where, delta, cum, cum_t, from_start, to_end, early = env

    cache_key_grad, cache_value_grad, out_grad, send = call(
        functools.partial(states_kernel, local),
        (
            shape((block_rows, head), BF), shape((block_rows, head), BF),
            shape(wide, BF), shape((PLANE, WIRE, head), BF),
        ),
        (),
        (whole, key_projection, value_projection, retention_query, from_start, early),
        scratch=[pltpu.VMEM((PLANE, WIRE // 2, head), F32)],
        flops=1 << 27,
    )
    send, dq_own, dq_other = lax.optimization_barrier((send, dq_own, dq_other))
    dq_other = lax.ppermute(dq_other, "core", [(0, 1), (1, 0)])
    keep, away = call(
        chip_pairs_kernel, (shape((2, flat, head), F32), shape((2, flat, head), BF)),
        (where,), (dq_own, dq_other),
    )
    away = lax.ppermute(away, "zl", [(i, i ^ 2) for i in range(CHIPS)])
    part = lax.all_to_all(send, PLANE_AXES, 0, 0, tiled=True)
    part, where = lax.optimization_barrier((part, where))
    lasts = part[:, lines_half + used, : 3 * local].astype(F32).reshape(PLANE, 3, local)
    decays = jnp.exp(lasts[:, 0] + lasts[:, 1] + lasts[:, 2])
    decays = jnp.broadcast_to(decays[:, :, None], (PLANE, local, SLICE))
    decays = jnp.pad(decays.reshape(PLANE, used), ((0, 0), (0, lines_half - used)))
    decays = jnp.concatenate([decays, decays], axis=1)[:, :, None]
    decays = jnp.broadcast_to(decays, (PLANE, WIRE, head))
    totals = call(
        functools.partial(totals_kernel, local),
        shape((WIRE, head), F32), (), (part, decays),
    )
    totals = lax.ppermute(totals, "zh", [(0, 1), (1, 0)])
    enter = call(
        functools.partial(scan_kernel, local),
        shape((PLANE, 2 * used, head), BF), (where,), (part, decays, totals),
        scratch=[pltpu.VMEM(part.shape, F32)] * 2,
    )
    enter, keep, away = lax.optimization_barrier((enter, keep, away))
    dq_mine, piece = call(
        chips_kernel, (shape((flat, head), F32), shape((flat, head), BF)), (where,), (keep, away),
    )
    piece = lax.ppermute(piece, "zl", [(i, i ^ 1) for i in range(CHIPS)])
    enter = lax.all_to_all(enter, PLANE_AXES, 0, 0, tiled=True)
    within = call(
        functools.partial(within_kernel, local), (shape(wide, F32),) * 3, (),
        (retention_query, retention_key, retention_value, out_grad, cum, cum_t),
        flops=1 << 28,
    )
    *grads, cross_query_grad = call(
        functools.partial(final_kernel, local, heads, factor),
        (shape(wide, F32),) * 3 + (shape(queries.shape, BF),),
        (),
        (
            retention_key, retention_value, out_grad, from_start, to_end, *within, enter,
            dq_mine, piece,
        ),
        scratch=[pltpu.VMEM(enter.shape, F32)],
        flops=1 << 27,
    )
    return (cross_query_grad, cache_key_grad, cache_value_grad) + tuple(grads)


def solution(mesh):
    sec, ctx = ("zl", "core"), ("zh", "x", "y")
    split = Mesh(mesh.devices.reshape(CHIPS, CORES, HALVES, 4, 8), sec + ctx)
    in_specs = (
        P(),
        P(sec, ctx, None),
        P(sec, ctx, None),
        P(sec, ctx, None),
        P(ctx, None),
        P(ctx, None),
        P(sec, None),
        P(sec, None),
        P(ctx, sec),
        P(ctx, sec),
        P(ctx, sec),
        P(sec, ctx),
    )
    out_specs = (
        P(sec, ctx, None),
        P(ctx, None),
        P(ctx, None),
        P(ctx, sec),
        P(ctx, sec),
        P(ctx, sec),
    )
    return jax.shard_map(body, mesh=split, in_specs=in_specs, out_specs=out_specs, check_vma=False)
```

```python
import functools
import math

import jax
import jax.numpy as jnp
from jax import lax
from jax.experimental import pallas as pl
from jax.experimental.pallas import tpu as pltpu
from jax.sharding import Mesh
from jax.sharding import PartitionSpec as P

BF = jnp.bfloat16
F32 = jnp.float32
LOW = -1e30
LOG2E = math.log2(math.e)
CHIPS, CORES = 4, 2
HALVES, PLANE = 2, 32
PLANE_AXES = ("x", "y")
SLICE = 4
WIRE = 48
SCOPED = 16 * 1024 * 1024


def dot_nt(a, b):
    return lax.dot_general(a, b, (((1,), (1,)), ((), ())), preferred_element_type=F32)


def dot_nn(a, b):
    return lax.dot_general(a, b, (((1,), (0,)), ((), ())), preferred_element_type=F32)


def dot_tn(a, b):
    return lax.dot_general(a, b, (((0,), (0,)), ((), ())), preferred_element_type=F32)


def call(kernel, outs, in_smem, ins, scratch=(), flops=0, smem_outs=0, space=pltpu.VMEM, scoped=SCOPED):
    vmem = pl.BlockSpec(memory_space=pltpu.VMEM)
    smem = pl.BlockSpec(memory_space=pltpu.SMEM)
    out_specs = jax.tree.map(lambda _: vmem, outs)
    if smem_outs:
        out_specs = (vmem,) * (len(outs) - smem_outs) + (smem,) * smem_outs
    return pl.pallas_call(
        kernel,
        out_shape=outs,
        in_specs=[smem] * len(in_smem) + [pl.BlockSpec(memory_space=space)] * len(ins),
        out_specs=out_specs,
        scratch_shapes=list(scratch),
        compiler_params=pltpu.CompilerParams(vmem_limit_bytes=scoped),
        cost_estimate=pl.CostEstimate(flops=flops, bytes_accessed=1 << 20, transcendentals=0),
    )(*in_smem, *ins)


def shape(dims, dtype):
    return jax.ShapeDtypeStruct(dims, dtype)


def pinned_exchange(array, axes, later):
    array, later = lax.optimization_barrier((array, later))
    array = lax.all_to_all(array, axes, 0, 0, tiled=True)
    return lax.optimization_barrier((array, later))


def pack_kernel(heads, q_hbm, g_hbm, out_ref, q_ref, g_ref, sems):
    rows = q_ref.shape[1]
    copies = [
        pltpu.make_async_copy(q_hbm, q_ref, sems.at[0]),
        pltpu.make_async_copy(g_hbm, g_ref, sems.at[1]),
    ]
    for copy in copies:
        copy.start()
    for copy in copies:
        copy.wait()
    for h in range(heads):
        at = slice(h * 128, (h + 1) * 128)
        out_ref[h * rows : (h + 1) * rows, :] = q_ref[0, :, at]
        out_ref[(heads + h) * rows : (heads + h + 1) * rows, :] = g_ref[0, :, at]


def delta_kernel(heads, where_ref, offset_ref, g_ref, o_ref, out_ref, place_ref, product):
    for n in range(4):
        place_ref[n] = where_ref[n]
    place_ref[4] = offset_ref[where_ref[0]]
    rows = g_ref.shape[1]
    base = lax.rem(where_ref[1], 2) * (heads * rows)
    product[...] = jnp.zeros_like(product)
    for h in range(heads):
        at = slice(h * 128, (h + 1) * 128)
        to = pl.ds(pl.multiple_of(base + h * rows, rows), rows)
        product[to, :] = g_ref[0, :, at].astype(F32) * o_ref[0, :, at].astype(F32)
    sums = jnp.sum(product[...].T, axis=0, keepdims=True)
    out_ref[...] = jnp.zeros_like(out_ref)
    for n in range(sums.shape[1] // 128):
        out_ref[n : n + 1, :] = sums[:, n * 128 : (n + 1) * 128]


def gather_kernel(where_ref, a_ref, b_ref, c_ref, d_ref, out_ref):
    flat = out_ref.shape[2]
    for k, ref in enumerate((a_ref, b_ref, c_ref, d_ref)):
        chip = lax.rem(where_ref[1] + k, CHIPS)
        out_ref[0, chip] = ref[0:flat]
        out_ref[1, chip] = ref[flat:]


def row_positions(where_ref, width, rows, block_rows):
    lane = lax.broadcasted_iota(jnp.int32, (1, width), 1)
    shard = where_ref[0]
    return lax.rem(lane, rows) + (shard * block_rows + where_ref[4])


def key_positions(place, chunk, blocks, rows, block_rows):
    at = lax.broadcasted_iota(jnp.int32, (blocks * rows, 1), 0)
    return (chunk * blocks + at // rows) * block_rows + place * rows + at % rows


def cache_place(kv_ref, chunk, blocks, rows):
    per = kv_ref.shape[0] // blocks
    line = pl.multiple_of((chunk // per) * (2 * rows), 2 * rows)
    return pl.ds(pl.multiple_of(lax.rem(chunk, per) * blocks, blocks), blocks), line


def keys_slice(kv_ref, chunk, blocks, rows, values):
    at = pl.ds(pl.multiple_of(chunk * blocks, blocks), blocks)
    return kv_ref[at, values * rows : (values + 1) * rows, :].reshape(blocks * rows, -1)


def tile(refs, which, n, t):
    return refs[n][which, 2 * t : 2 * t + 2].reshape(2 * refs[n].shape[2], -1)


def stats_kernel(
    blocks, rows, query_rows, block_rows, factor, where_ref, rows_ref, kv_ref, out_ref,
):
    shard, place = where_ref[0], where_ref[2]
    width = 2 * rows_ref.shape[2]
    lines = width // 128
    full = shard // blocks
    pos = row_positions(where_ref, width, query_rows, block_rows)
    scale = factor * LOG2E
    tiles = range(CHIPS // 2)

    def chunk(j, carry, masked=False):
        keys = keys_slice(kv_ref, j, blocks, rows, 0)
        if masked:
            seen = key_positions(place, j, blocks, rows, block_rows) <= pos
        out = []
        for t, (top, total) in zip(tiles, carry):
            s = dot_nt(keys, tile((rows_ref,), 0, 0, t))
            if masked:
                s = jnp.where(seen, s, LOW)
            new = jnp.maximum(top, jnp.max(s, axis=0, keepdims=True))
            p = jnp.exp2((s - new) * scale)
            total = total * jnp.exp2((top - new) * scale) + jnp.sum(p, axis=0, keepdims=True)
            out.append((new, total))
        return tuple(out)

    start = ((jnp.full((1, width), LOW, F32), jnp.zeros((1, width), F32)),) * len(tiles)
    done = chunk(full, lax.fori_loop(0, full, chunk, start), masked=True)
    for t, (top, total) in zip(tiles, done):
        lse = jnp.where(top > LOW, top * factor + jnp.log(total), LOW)
        for m in range(lines):
            out_ref[t * lines + m : t * lines + m + 1, :] = lse[:, m * 128 : (m + 1) * 128]


def grads_kernel(
    blocks, rows, query_rows, block_rows, factor,
    where_ref, mine_ref, other_ref, kv_ref, log_ref, delta_ref,
    dkv_ref, dq_own_ref, dq_other_ref, dq_total,
):
    shard, place, core = where_ref[0], where_ref[2], where_ref[3]
    flat = mine_ref.shape[2]
    width = 2 * flat
    size = blocks * rows
    full = shard // blocks
    pos = row_positions(where_ref, width, query_rows, block_rows)
    scale = factor * LOG2E
    tiles = [(n, t) for n in range(CORES) for t in range(CHIPS // 2)]
    dq_total[...] = jnp.zeros_like(dq_total)

    def chunk(j, masked=False):
        keys = keys_slice(kv_ref, j, blocks, rows, 0)
        values = keys_slice(kv_ref, j, blocks, rows, 1)
        if masked:
            seen = key_positions(place, j, blocks, rows, block_rows) <= pos
        dk = dv = 0.0
        for i, (n, t) in enumerate(tiles):
            q = tile((mine_ref, other_ref), 0, n, t)
            g = tile((mine_ref, other_ref), 1, n, t)
            at_core = lax.rem(core + n, CORES)
            p = jnp.exp2(dot_nt(keys, q) * scale - log_ref[at_core, t] * LOG2E)
            if masked:
                p = jnp.where(seen, p, 0.0)
            ds = (p * (dot_nt(values, g) - delta_ref[at_core, t])).astype(BF)
            dk = dk + dot_nn(ds, q)
            dv = dv + dot_nn(p.astype(BF), g)
            dq_total[i] += dot_tn(keys, ds)
        at, line = cache_place(dkv_ref, j, blocks, rows)
        dkv_ref[at, pl.ds(line, rows), :] = dk.astype(BF).reshape(blocks, rows, -1)
        dkv_ref[at, pl.ds(line + rows, rows), :] = dv.astype(BF).reshape(blocks, rows, -1)

    def step(j, _):
        chunk(j)
        return 0

    lax.fori_loop(0, full, step, 0)
    chunk(full, masked=True)

    def clear(j, _):
        at, line = cache_place(dkv_ref, j, blocks, rows)
        dkv_ref[at, pl.ds(line, 2 * rows), :] = jnp.zeros((blocks, 2 * rows, kv_ref.shape[-1]), BF)
        return 0

    lax.fori_loop(full + 1, HALVES * dkv_ref.shape[0] // blocks, clear, 0)
    for i, (n, t) in enumerate(tiles):
        dq = dq_total[i].T
        dq_ref = (dq_own_ref, dq_other_ref)[n]
        for m in range(2):
            dq_ref[2 * t + m] = dq[m * flat : (m + 1) * flat].astype(dq_ref.dtype)


def chip_pairs_kernel(where_ref, own_ref, other_ref, keep_ref, send_ref):
    pair = where_ref[1] // 2
    for m in range(2):
        to = 2 * pair + m
        keep_ref[m] = own_ref[to] + other_ref[to].astype(F32)
        to = 2 * (1 - pair) + m
        send_ref[m] = (own_ref[to] + other_ref[to].astype(F32)).astype(BF)


def chips_kernel(where_ref, keep_ref, got_ref, own_ref, send_ref):
    own = lax.rem(where_ref[1], 2)
    own_ref[...] = keep_ref[own] + got_ref[own].astype(F32)
    send_ref[...] = (keep_ref[1 - own] + got_ref[1 - own].astype(F32)).astype(BF)


def total_kernel(factor, terms_ref, out_ref):
    total = jnp.sum(terms_ref[...].astype(F32), axis=0)
    lines = out_ref.shape[1]
    row = lax.broadcasted_iota(jnp.int32, (lines, 1), 0)
    scale = jnp.where(row < lines // 2, factor, 1.0)
    count = out_ref.shape[0] // HALVES
    for n in range(HALVES):
        part = (total[n * lines : (n + 1) * lines] * scale).astype(BF)
        out_ref[n * count : (n + 1) * count] = jnp.broadcast_to(part[None], (count,) + part.shape)


def early_kernel(heads, rk_ref, rv_ref, to_ref, extra_ref, out_ref, wire):
    plane = wire.shape[0]
    used = SLICE * heads
    wire[:, used:, :] = jnp.broadcast_to(extra_ref[...][None], (plane,) + extra_ref.shape)
    for i in range(heads):
        at = slice(i * 128, (i + 1) * 128)
        key_w = (rk_ref[:, at].astype(F32) * to_ref[:, i : i + 1]).astype(BF)
        state = dot_tn(key_w, rv_ref[:, at])
        for k in range(SLICE):
            wire[:, SLICE * i + k, :] = state[k * plane : (k + 1) * plane]
    out_ref[...] = wire[...].astype(BF)


def states_kernel(
    heads, whole_ref, kp_ref, vp_ref, rq_ref, from_ref, early_ref, ck_ref, cv_ref, gr_ref, send_ref, wire,
):
    count = whole_ref.shape[0] // HALVES
    rows = whole_ref.shape[1] // 2
    both = (whole_ref[0:count].astype(F32) + whole_ref[count:].astype(F32)).astype(BF)
    ck = both[:, 0:rows, :].reshape(count * rows, -1)
    cv = both[:, rows:, :].reshape(count * rows, -1)
    ck_ref[...] = ck
    cv_ref[...] = cv
    plane = send_ref.shape[0]
    lines = send_ref.shape[1] - early_ref.shape[1]
    wire[:, SLICE * heads :, :] = jnp.zeros((plane, lines - SLICE * heads, 128), F32)
    both = jnp.concatenate([ck, cv], axis=1)
    projection = jnp.concatenate([kp_ref[...], vp_ref[...]], axis=1)
    out_grad = dot_nt(both, projection).astype(BF)
    gr_ref[...] = out_grad
    for i in range(heads):
        at = slice(i * 128, (i + 1) * 128)
        gr = out_grad[:, at]
        query_w = (rq_ref[:, at].astype(F32) * from_ref[:, i : i + 1]).astype(BF)
        grad = dot_tn(query_w, gr)
        for k in range(SLICE):
            wire[:, SLICE * i + k, :] = grad[k * plane : (k + 1) * plane]
    send_ref[...] = jnp.concatenate([wire[...], early_ref[...].astype(F32)], axis=1).astype(BF)


def totals_kernel(heads, part_ref, decay_ref, out_ref):
    count = part_ref.shape[0]
    zero = jnp.zeros(part_ref.shape[1:], F32)

    def step(b, carry):
        fore, back = carry
        fore = decay_ref[b] * fore + part_ref[b].astype(F32)
        r = count - 1 - b
        back = decay_ref[r] * back + part_ref[r].astype(F32)
        return fore, back

    fore, back = lax.fori_loop(0, count, step, (zero, zero), unroll=8)
    row = lax.broadcasted_iota(jnp.int32, zero.shape, 0)
    out_ref[...] = jnp.where(row < WIRE // 2, back, fore)


def scan_kernel(heads, where_ref, part_ref, decay_ref, other_ref, out_ref, ahead, behind):
    count = part_ref.shape[0]
    upper = where_ref[0] >= count
    other = other_ref[...]
    zero = jnp.zeros_like(other)

    def step(b, carry):
        fore, back = carry
        ahead[b] = fore
        fore = decay_ref[b] * fore + part_ref[b].astype(F32)
        r = count - 1 - b
        behind[r] = back
        back = decay_ref[r] * back + part_ref[r].astype(F32)
        return fore, back

    start = (jnp.where(upper, other, zero), jnp.where(upper, zero, other))
    lax.fori_loop(0, count, step, start, unroll=8)
    used = SLICE * heads
    at = WIRE // 2
    both = jnp.concatenate([behind[:, 0:used, :], ahead[:, at : at + used, :]], axis=1)
    out_ref[...] = both.astype(BF)


def within_kernel(
    heads, rq_ref, rk_ref, rv_ref, gr_ref, cum_ref, cum_t_ref, q_ref, k_ref, v_ref,
):
    size = rq_ref.shape[0]
    t = lax.broadcasted_iota(jnp.int32, (size, size), 0)
    u = lax.broadcasted_iota(jnp.int32, (size, size), 1)
    causal = t >= u
    for i in range(heads):
        at = slice(i * 128, (i + 1) * 128)
        qr, kr, vr, gr = rq_ref[:, at], rk_ref[:, at], rv_ref[:, at], gr_ref[:, at]
        gap = cum_t_ref[:, i : i + 1] - cum_ref[i : i + 1, :]
        decay = jnp.where(causal, jnp.exp(jnp.where(causal, gap, 0.0)), 0.0)
        one = (decay * dot_nt(gr, vr)).astype(BF)
        three = (decay * dot_nt(qr, kr)).astype(BF)
        q_ref[:, at] = dot_nn(one, kr)
        k_ref[:, at] = dot_tn(one, qr)
        v_ref[:, at] = dot_tn(three, gr)


def final_kernel(
    heads, query_heads, factor, rk_ref, rv_ref, gr_ref, from_ref, to_ref, q_in_ref, k_in_ref, v_in_ref,
    wire_ref, own_ref, got_ref, q_ref, k_ref, v_ref, cross_ref, wire,
):
    rows = cross_ref.shape[1]
    total = ((own_ref[...] + got_ref[...].astype(F32)) * factor).astype(BF)
    for h in range(query_heads):
        cross_ref[0, :, h * 128 : (h + 1) * 128] = total[h * rows : (h + 1) * rows]
    wire[...] = wire_ref[...].astype(F32)

    def matrix(r):
        return jnp.concatenate([wire[:, r + k, :] for k in range(SLICE)], axis=0).astype(BF)

    for i in range(heads):
        at = slice(i * 128, (i + 1) * 128)
        grad_b, state_b = matrix(SLICE * i), matrix(SLICE * (heads + i))
        from_start, to_end = from_ref[:, i : i + 1], to_ref[:, i : i + 1]
        q_ref[:, at] = q_in_ref[:, at] + from_start * dot_nt(gr_ref[:, at], state_b)
        k_ref[:, at] = k_in_ref[:, at] + to_end * dot_nt(rv_ref[:, at], grad_b)
        v_ref[:, at] = v_in_ref[:, at] + to_end * dot_nn(rk_ref[:, at], grad_b)


def body(
    offsets,
    queries,
    output_grad,
    attention_out,
    cache_keys,
    cache_values,
    key_projection,
    value_projection,
    retention_query,
    retention_key,
    retention_value,
    retention_decay,
):
    core, chip = lax.axis_index("core"), lax.axis_index("zl")
    place = chip * CORES + core
    secs = CHIPS * CORES
    half = lax.axis_index("zh")
    shard = half * PLANE + lax.axis_index(PLANE_AXES)
    shards = HALVES * PLANE
    block_rows, head = cache_keys.shape
    _, query_rows, query_width = queries.shape
    heads = query_width // head
    flat = query_rows * heads
    width = 2 * flat
    lines = width // 128
    rows = block_rows // secs
    factor = 1.0 / math.sqrt(head)
    blocks = 32
    sizes = (blocks, rows, query_rows, block_rows, factor)
    where = jnp.stack([shard, chip, place, core]).astype(jnp.int32)

    kv_own = jnp.concatenate(
        [lax.dynamic_slice_in_dim(a, place * rows, rows, 0) for a in (cache_keys, cache_values)]
    )
    kv = jnp.broadcast_to(kv_own[None], (shards,) + kv_own.shape)
    own = call(
        functools.partial(pack_kernel, heads),
        shape((2 * flat, head), BF), (), (queries, output_grad),
        scratch=[pltpu.VMEM(queries.shape, BF)] * 2 + [pltpu.SemaphoreType.DMA((2,))],
        space=pltpu.HBM, scoped=56 * 1024 * 1024,
    )
    parts = [own] + [
        lax.ppermute(own, "zl", [(i, (i - k) % CHIPS) for i in range(CHIPS)])
        for k in range(1, CHIPS)
    ]
    delta, where = call(
        functools.partial(delta_kernel, heads),
        (shape((32 - CHIPS * lines, head), F32), shape((5,), jnp.int32)),
        (where, offsets), (output_grad, attention_out), smem_outs=1,
        scratch=[pltpu.VMEM((width, head), F32)],
    )

    local = retention_decay.shape[0]
    used = SLICE * local
    lines_half = WIRE // 2
    cum = jnp.cumsum(retention_decay, axis=1)
    cum_t = cum.T
    last = cum[:, -1]
    from_start = jnp.exp(cum_t)
    to_end = jnp.exp(last[None] - cum_t)
    high = last.astype(BF)
    rest = last - high.astype(F32)
    middle = rest.astype(BF)
    low = (rest - middle.astype(F32)).astype(BF)
    extra = jnp.concatenate([high, middle, low]).astype(F32)
    extra = jnp.pad(extra[None], ((0, lines_half - used - 1), (0, head - extra.shape[0])))

    wide = retention_query.shape
    early = call(
        functools.partial(early_kernel, local),
        shape((PLANE, WIRE // 2, head), BF), (),
        (retention_key, retention_value, to_end, extra),
        scratch=[pltpu.VMEM((PLANE, WIRE // 2, head), F32)], flops=1 << 26,
    )

    env = (where, delta, cum, cum_t, from_start, to_end, early)
    mine = call(
        gather_kernel, shape((2, CHIPS, flat, head), BF), (where,), tuple(parts), flops=4 << 30
    )
    kv = lax.all_to_all(kv, ("zh",) + PLANE_AXES, 0, 0, tiled=True)
    kv, env = lax.optimization_barrier((kv, env))
    where, delta = env[:2]
    other = lax.ppermute(mine, "core", [(0, 1), (1, 0)])

    stats = [
        call(
            functools.partial(stats_kernel, *sizes),
            shape((CHIPS // 2 * lines, head), F32), (where,), (part, kv),
            flops=1 << 28,
        )
        for part in (mine, other)
    ]
    own_stats, other_stats = stats
    both = jnp.concatenate([
        jnp.where(core == 0, own_stats, other_stats),
        jnp.where(core == 0, other_stats, own_stats),
        delta,
    ])
    both = jnp.broadcast_to(both[None], (secs,) + both.shape)
    both, env = pinned_exchange(both, ("zl", "core"), env)
    where = env[0]
    tiles = (CORES, CHIPS // 2, 1, width)
    logs = both[:, : CHIPS * lines]
    top = jnp.max(logs, axis=0)
    log_total = (top + jnp.log(jnp.sum(jnp.exp(logs - top), axis=0))).reshape(tiles)
    deltas = both[:, CHIPS * lines : (CHIPS + 1) * lines]
    deltas = deltas.reshape(CHIPS // 2, 2, CORES, lines, head)
    deltas = (deltas[:, 0] + deltas[:, 1]).transpose(1, 0, 2, 3).reshape(tiles)

    dkv, dq_own, dq_other = call(
        functools.partial(grads_kernel, *sizes),
        (shape((PLANE, HALVES * 2 * rows, head), BF), shape((CHIPS, flat, head), F32), shape((CHIPS, flat, head), BF)),
        (where,),
        (mine, other, kv, log_total, deltas),
        scratch=[pltpu.VMEM((CORES * CHIPS // 2, head, width), F32)],
        flops=4 << 30,
    )
    terms, env = pinned_exchange(dkv, PLANE_AXES, env)
    total = call(
        functools.partial(total_kernel, factor),
        shape((HALVES * secs, 2 * rows, head), BF), (), (terms,),
    )
    whole, env = pinned_exchange(total, ("zh", "zl", "core"), env)
    where, delta, cum, cum_t, from_start, to_end, early = env

    cache_key_grad, cache_value_grad, out_grad, send = call(
        functools.partial(states_kernel, local),
        (
            shape((block_rows, head), BF), shape((block_rows, head), BF),
            shape(wide, BF), shape((PLANE, WIRE, head), BF),
        ),
        (),
        (whole, key_projection, value_projection, retention_query, from_start, early),
        scratch=[pltpu.VMEM((PLANE, WIRE // 2, head), F32)],
        flops=1 << 27,
    )
    send, dq_own, dq_other = lax.optimization_barrier((send, dq_own, dq_other))
    dq_other = lax.ppermute(dq_other, "core", [(0, 1), (1, 0)])
    keep, away = call(
        chip_pairs_kernel, (shape((2, flat, head), F32), shape((2, flat, head), BF)),
        (where,), (dq_own, dq_other),
    )
    away = lax.ppermute(away, "zl", [(i, i ^ 2) for i in range(CHIPS)])
    part = lax.all_to_all(send, PLANE_AXES, 0, 0, tiled=True)
    part, where = lax.optimization_barrier((part, where))
    lasts = part[:, lines_half + used, : 3 * local].astype(F32).reshape(PLANE, 3, local)
    decays = jnp.exp(lasts[:, 0] + lasts[:, 1] + lasts[:, 2])
    decays = jnp.broadcast_to(decays[:, :, None], (PLANE, local, SLICE))
    decays = jnp.pad(decays.reshape(PLANE, used), ((0, 0), (0, lines_half - used)))
    decays = jnp.concatenate([decays, decays], axis=1)[:, :, None]
    decays = jnp.broadcast_to(decays, (PLANE, WIRE, head))
    totals = call(
        functools.partial(totals_kernel, local),
        shape((WIRE, head), F32), (), (part, decays),
    )
    totals = lax.ppermute(totals, "zh", [(0, 1), (1, 0)])
    enter = call(
        functools.partial(scan_kernel, local),
        shape((PLANE, 2 * used, head), BF), (where,), (part, decays, totals),
        scratch=[pltpu.VMEM(part.shape, F32)] * 2,
    )
    enter, keep, away = lax.optimization_barrier((enter, keep, away))
    dq_mine, piece = call(
        chips_kernel, (shape((flat, head), F32), shape((flat, head), BF)), (where,), (keep, away),
    )
    piece = lax.ppermute(piece, "zl", [(i, i ^ 1) for i in range(CHIPS)])
    enter = lax.all_to_all(enter, PLANE_AXES, 0, 0, tiled=True)
    within = call(
        functools.partial(within_kernel, local), (shape(wide, F32),) * 3, (),
        (retention_query, retention_key, retention_value, out_grad, cum, cum_t),
        flops=1 << 28,
    )
    *grads, cross_query_grad = call(
        functools.partial(final_kernel, local, heads, factor),
        (shape(wide, F32),) * 3 + (shape(queries.shape, BF),),
        (),
        (
            retention_key, retention_value, out_grad, from_start, to_end, *within, enter,
            dq_mine, piece,
        ),
        scratch=[pltpu.VMEM(enter.shape, F32)],
        flops=1 << 27,
    )
    return (cross_query_grad, cache_key_grad, cache_value_grad) + tuple(grads)


def solution(mesh):
    sec, ctx = ("zl", "core"), ("zh", "x", "y")
    split = Mesh(mesh.devices.reshape(CHIPS, CORES, HALVES, 4, 8), sec + ctx)
    in_specs = (
        P(),
        P(sec, ctx, None),
        P(sec, ctx, None),
        P(sec, ctx, None),
        P(ctx, None),
        P(ctx, None),
        P(sec, None),
        P(sec, None),
        P(ctx, sec),
        P(ctx, sec),
        P(ctx, sec),
        P(sec, ctx),
    )
    out_specs = (
        P(sec, ctx, None),
        P(ctx, None),
        P(ctx, None),
        P(ctx, sec),
        P(ctx, sec),
        P(ctx, sec),
    )
    return jax.shard_map(body, mesh=split, in_specs=in_specs, out_specs=out_specs, check_vma=False)
```
